32 devices in a mesh: row: 8 (over z, y), col: 4 (over x, core).
Axes of the slice: x: 2, y: 2, z: 4, core: 2. Of those that a mesh axis runs over, the one named last changes fastest.
Arguments:
- state: float32 [5, 8, 64, 512], P(None, None, 'row', 'col'), may hold values from -1.6 to 7, as said below
- gamma: float32 [8, 64, 512], P(None, 'row', 'col'), may hold values from 1.2 to 1.67
Outputs:
- advanced: float32 [5, 8, 64, 512], P(None, None, 'row', 'col')
The draws below stay inside these ranges and needn't reach their ends.
Inputs may be any that keep to these rules, and one draw needn't show every extreme that they name: `state`: density lies in 0.5 to 2, every velocity (momentum / density) in -0.8 to 0.8, and energy minus kinetic energy is 1.25 to 5, so that pressure is positive for every gamma in its range.
All inputs are finite; a program needn't handle non-finite values.
Results may differ from the reference program's by a relative error of at most 0.00002.
Values sent between devices are 32-bit elements; how exact they have to be, the bound alone decides.
No kernel may reach another device: no remote copies, remote signals or barrier semaphores. Data moves between devices by JAX's collectives and lax.ppermute only.
A program may use at most 64 MiB of HBM per device.

```python
import jax
import jax.numpy as jnp
from jax import lax

CZ = 128
NX = 8
NY = 64
NZ = 512


def draw_state(key, part):
    key = jax.random.fold_in(key, 11)
    keys = jax.random.split(key, 3)
    shape = (NX, NY, NZ)
    density = jax.random.uniform(keys[0], shape, jnp.float32, 0.5, 2.0)
    velocity = jax.random.uniform(keys[1], (3,) + shape, jnp.float32, -0.8, 0.8)
    pressure = jax.random.uniform(keys[2], shape, jnp.float32, 0.5, 2.0)
    momenta = density[None] * velocity
    energy = pressure / 0.4 + 0.5 * density * jnp.sum(velocity * velocity, axis=0)
    return jnp.concatenate([density[None], momenta, energy[None]], axis=0).astype(jnp.float32)


def block_scale(own_key, dims, cuts, smallest, top_value):
    gain = 1.0
    for dim, parts in cuts:
        draws = jax.random.uniform(jax.random.fold_in(jax.random.fold_in(own_key, 6), dim), (parts,), jnp.float32, smallest / len(cuts), top_value / len(cuts))
        gain = gain * jnp.repeat(jnp.exp(draws), dims[dim] // parts).reshape((-1,) + (1,) * (len(dims) - 1 - dim))
    return gain


def setup_inputs(seed: int = 0) -> dict:
    seeds = jax.random.split(jax.random.key(seed), 3)
    return {
        "state": draw_state(jax.random.fold_in(seeds[2], 71), 0),
        "gamma": jnp.clip(1.2 + 0.4699999 * jax.random.uniform(seeds[1], (NX, NY, NZ), jnp.float32) ** block_scale(seeds[1], (NX, NY, NZ), ((1, 8), (2, 4)), -0.2, 0.2), 1.2, 1.67),
    }


step_ratio = 0.08

def minmod(first, second):
    return jnp.maximum(jnp.minimum(first, second), 0.0) + jnp.minimum(jnp.maximum(first, second), 0.0)

def window(array, start, stop, sweep_axis):
    return lax.slice_in_dim(array, start, stop, axis=sweep_axis)

def fluxes(density, normal_vel, trans_one, trans_two, pressure, gamma_side):
    energy = pressure / (gamma_side - 1.0) + 0.5 * density * (normal_vel * normal_vel + trans_one * trans_one + trans_two * trans_two)
    conserved = [density, density * normal_vel, density * trans_one, density * trans_two, energy]
    flux = [density * normal_vel, density * normal_vel * normal_vel + pressure, density * normal_vel * trans_one, density * normal_vel * trans_two, normal_vel * (energy + pressure)]
    speed = jnp.abs(normal_vel) + jnp.sqrt(gamma_side * pressure / density)
    return (conserved, flux, speed)

def sweep_update(padded, gamma_pad, sweep_axis, normal):
    length = gamma_pad.shape[sweep_axis]
    density = padded[0]
    velocity = [padded[1] / density, padded[2] / density, padded[3] / density]
    kinetic = 0.5 * (padded[1] * velocity[0] + padded[2] * velocity[1] + padded[3] * velocity[2])
    pressure = (gamma_pad - 1.0) * (padded[4] - kinetic)
    others = [component for component in range(3) if component != normal]
    primitives = [density, velocity[normal], velocity[others[0]], velocity[others[1]], pressure]
    left_states = []
    right_states = []
    for quantity in primitives:
        lower_zone = window(quantity, 1, length - 2, sweep_axis)
        upper_zone = window(quantity, 2, length - 1, sweep_axis)
        face_value = (7.0 * (lower_zone + upper_zone) - (window(quantity, 0, length - 3, sweep_axis) + window(quantity, 3, length, sweep_axis))) / 12.0
        face_value = jnp.minimum(jnp.maximum(face_value, jnp.minimum(lower_zone, upper_zone)), jnp.maximum(lower_zone, upper_zone))
        centre = window(quantity, 2, length - 2, sweep_axis)
        rise_right = window(face_value, 1, length - 3, sweep_axis) - centre
        rise_left = centre - window(face_value, 0, length - 4, sweep_axis)
        upper_edge = centre + minmod(rise_right, 2.0 * rise_left)
        lower_edge = centre - minmod(rise_left, 2.0 * rise_right)
        left_states.append(window(upper_edge, 0, length - 5, sweep_axis))
        right_states.append(window(lower_edge, 1, length - 4, sweep_axis))
    cons_left, flux_left, speed_left = fluxes(*left_states, window(gamma_pad, 2, length - 3, sweep_axis))
    cons_right, flux_right, speed_right = fluxes(*right_states, window(gamma_pad, 3, length - 2, sweep_axis))
    speed = jnp.maximum(speed_left, speed_right)
    interface = [0.5 * (flux_left[item] + flux_right[item]) - 0.5 * speed * (cons_right[item] - cons_left[item]) for item in range(5)]
    field_flux = [interface[0], None, None, None, interface[4]]
    field_flux[1 + normal] = interface[1]
    field_flux[1 + others[0]] = interface[2]
    field_flux[1 + others[1]] = interface[3]
    updated = []
    for field in range(5):
        change = window(field_flux[field], 1, length - 5, sweep_axis) - window(field_flux[field], 0, length - 6, sweep_axis)
        updated.append(window(padded[field], 3, length - 3, sweep_axis) - step_ratio * change)
    return jnp.stack(updated)

def edge_sweep(conserved, gamma_field, sweep_axis, normal):
    widths = [(0, 0)] * gamma_field.ndim
    widths[sweep_axis] = (3, 3)
    gamma_pad = jnp.pad(gamma_field, widths, mode='edge')
    padded = jnp.pad(conserved, [(0, 0)] + widths, mode='edge')
    return sweep_update(padded, gamma_pad, sweep_axis, normal)

def reference(state, gamma):
    blocks = NZ // CZ
    slabs = state.reshape(5, NX, NY, blocks, CZ).transpose(3, 0, 1, 2, 4)
    gamma_slabs = gamma.reshape(NX, NY, blocks, CZ).transpose(2, 0, 1, 3)

    def first_two(pair):
        swept = edge_sweep(pair[0], pair[1], 0, 0)
        return edge_sweep(swept, pair[1], 1, 1)
    slabs = lax.map(first_two, (slabs, gamma_slabs))
    middle = slabs.transpose(1, 2, 3, 0, 4).reshape(5, NX, NY, NZ)

    def third(pair):
        return edge_sweep(pair[0], pair[1], 1, 2)
    planes = lax.map(third, (jnp.moveaxis(middle, 1, 0), gamma))
    return jnp.moveaxis(planes, 0, 1)
```

```python
import functools

import jax
import jax.numpy as jnp
from jax import lax
from jax.experimental import pallas as pl
from jax.experimental.pallas import tpu as pltpu
from jax.sharding import PartitionSpec as P

STEP = 0.08
HALO = 3
SUB, LANES = 8, 128
GROUP = LANES // SUB


def recip(x):
    r = pl.reciprocal(x, approx=True)
    return r * (2.0 - x * r)


def clamp_zero(u, v):
    return jnp.maximum(jnp.minimum(u, jnp.maximum(v, 0.0)), jnp.minimum(v, 0.0))


def primitives(cons, gam1, normal):
    rho, m0, m1, m2, energy = cons
    inv = recip(rho)
    vel = [m0 * inv, m1 * inv, m2 * inv]
    kinetic = 0.5 * (m0 * vel[0] + m1 * vel[1] + m2 * vel[2])
    pressure = gam1 * (energy - kinetic)
    others = [c for c in range(3) if c != normal]
    return [rho, vel[normal], vel[others[0]], vel[others[1]], pressure]


def face_rise(before, here, after):
    if here is None:
        return None
    rise = 0.5 * here
    if before is not None and after is not None:
        rise = rise + (before - after) * (1.0 / 12.0)
    elif before is not None:
        rise = rise + before * (1.0 / 12.0)
    elif after is not None:
        rise = rise - after * (1.0 / 12.0)
    return clamp_zero(rise, here)


def edges(q, right, left):
    if right is None or left is None:
        return q, q
    return q + clamp_zero(right, 2.0 * left), q - clamp_zero(left, 2.0 * right)


def state_flux(prim, gamma, inv_gam1):
    rho, un, u1, u2, p = prim
    mn, m1, m2 = rho * un, rho * u1, rho * u2
    nn = mn * un
    energy = p * inv_gam1 + 0.5 * (nn + m1 * u1 + m2 * u2)
    flux = [mn, nn + p, mn * u1, mn * u2, un * (energy + p)]
    gp = gamma * p
    speed = jnp.abs(un) + gp * lax.rsqrt(jnp.maximum(gp * rho, 1e-30))
    return [rho, mn, m1, m2, energy], flux, speed


def double_flux(left, right):
    if left is right:
        return [f + f for f in left[1]]
    speed = jnp.maximum(left[2], right[2])
    return [
        (left[1][k] + right[1][k]) - speed * (right[0][k] - left[0][k]) for k in range(5)
    ]


def place(normal):
    others = [c for c in range(3) if c != normal]
    return [0, 1 + normal, 1 + others[0], 1 + others[1], 4]


def updated(cons, flux_right, flux_left, normal):
    out = list(cons)
    for k, field in enumerate(place(normal)):
        out[field] = cons[field] - (0.5 * STEP) * (flux_right[k] - flux_left[k])
    return out


def sweep_rows(load, load_gamma, store, n, normal, outflow):
    cons, gam, prim, diff, rise, edge = {}, {}, {}, {}, {}, {}

    def zone(i):
        return min(max(i, 0), n - 1) if outflow else i

    def get(i):
        i = zone(i)
        if i not in cons:
            cons[i] = load(i)
            g = load_gamma(i)
            gam1 = g - 1.0
            gam[i] = (g, recip(gam1))
            prim[i] = primitives(cons[i], gam1, normal)
        return prim[i]

    def get_diff(i):
        if i not in diff:
            a, b = get(i), get(i + 1)
            diff[i] = [None] * 5 if a is b else [y - x for x, y in zip(a, b)]
        return diff[i]

    def get_rise(i):
        if i not in rise:
            before, here, after = get_diff(i - 1), get_diff(i), get_diff(i + 1)
            right = [face_rise(*t) for t in zip(before, here, after)]
            left = [None if r is None else h - r for h, r in zip(here, right)]
            rise[i] = (right, left)
        return rise[i]

    def get_edge(i):
        if i not in edge:
            q, right, left = get(i), get_rise(i)[0], get_rise(i - 1)[1]
            pairs = [edges(*t) for t in zip(q, right, left)]
            upper = [p[0] for p in pairs]
            lower = [p[1] for p in pairs]
            if all(u is w for u, w in zip(upper, lower)):
                one = state_flux(upper, *gam[zone(i)])
                edge[i] = (one, one, zone(i))
            else:
                edge[i] = [upper, lower, zone(i)]
        return edge[i]

    def side(i, which):
        e = get_edge(i)
        if isinstance(e, tuple):
            return e[which]
        return state_flux(e[which], *gam[e[2]])

    def face(i):
        if outflow and i < 0:
            whole = get_edge(0)
            return double_flux(whole[0], whole[0])
        if outflow and i == n - 1:
            whole = get_edge(n - 1)
            return double_flux(whole[1], whole[1])
        return double_flux(side(i, 0), side(i + 1, 1))

    previous = face(-1)
    for i in range(n):
        current = face(i)
        store(i, updated(cons[i], current, previous, normal))
        previous = current


def first_kernel(row_axis, state_ref, gamma_ref, swept_ref, one_ref, two_ref):
    nx, ny = gamma_ref.shape[0], gamma_ref.shape[1]

    def store(x, cons):
        for f in range(5):
            swept_ref[f, pl.ds(x, ny, stride=nx), :] = cons[f]

    sweep_rows(
        lambda x: [state_ref[f, x] for f in range(5)],
        lambda x: gamma_ref[x],
        store,
        nx,
        0,
        True,
    )
    for x in range(nx):
        swept_ref[5, pl.ds(x, ny, stride=nx), :] = gamma_ref[x]
    odd = lax.rem(lax.axis_index(row_axis), 2)
    low, high = 0, (ny - HALO) * nx
    start_one = pl.multiple_of(jnp.where(odd == 1, low, high), SUB)
    start_two = pl.multiple_of(jnp.where(odd == 1, high, low), SUB)
    for f in range(6):
        one_ref[f] = swept_ref[f, pl.ds(start_one, HALO * nx), :]
        two_ref[f] = swept_ref[f, pl.ds(start_two, HALO * nx), :]


def second_kernel(row_axis, rows, swept_ref, one_ref, two_ref, next_ref, window_ref):
    nx = swept_ref.shape[1] // SUB
    ny = SUB
    row = lax.axis_index(row_axis)
    odd = lax.rem(row, 2) == 1
    first, last = row == 0, row == rows - 1
    lane = lax.broadcasted_iota(jnp.int32, (SUB, LANES), 1)
    group = lane // GROUP
    for tile in range(nx // SUB):
        base = tile * SUB

        def load_field(f, y):
            if 0 <= y < ny:
                return swept_ref[f, pl.ds(y * nx + base, SUB), :]
            at = pl.ds((y + HALO if y < 0 else y - ny) * nx + base, SUB)
            one, two = one_ref[f, at, :], two_ref[f, at, :]
            if y < 0:
                got = jnp.where(odd, one, two)
                return jnp.where(first, swept_ref[f, pl.ds(base, SUB), :], got)
            got = jnp.where(odd, two, one)
            return jnp.where(last, swept_ref[f, pl.ds((ny - 1) * nx + base, SUB), :], got)

        windows = [None] * 6

        def into_window(f, y, value):
            turn = (GROUP * y + 6) % LANES
            rolled = pltpu.roll(value, turn, 1) if turn else value
            windows[f] = rolled if windows[f] is None else jnp.where(group == y, rolled, windows[f])

        def store(y, cons):
            for f in range(5):
                next_ref[f, pl.ds(y * nx + base, SUB), :] = cons[f]
                into_window(f, y, cons[f])

        sweep_rows(
            lambda y: [load_field(f, y) for f in range(5)],
            lambda y: load_field(5, y),
            store,
            ny,
            1,
            False,
        )
        for y in range(ny):
            into_window(5, y, swept_ref[5, pl.ds(y * nx + base, SUB), :])
        for f in range(6):
            window_ref[f, pl.ds(base, SUB), :] = windows[f]


def sweep_lanes(cons, gamma, normal):
    def ahead(x):
        return pltpu.roll(x, LANES - 1, 1)

    def behind(x):
        return pltpu.roll(x, 1, 1)

    gam1 = gamma - 1.0
    inv_gam1 = recip(gam1)
    prim = primitives(cons, gam1, normal)
    upper, lower_next = [], []
    for q in prim:
        here = ahead(q) - q
        right = face_rise(behind(here), here, ahead(here))
        left = behind(here - right)
        up, low = edges(q, right, left)
        upper.append(up)
        lower_next.append(ahead(low))
    flux = double_flux(
        state_flux(upper, gamma, inv_gam1),
        state_flux(lower_next, ahead(gamma), ahead(inv_gam1)),
    )
    return updated(cons, flux, [behind(x) for x in flux], normal)


def third_kernel(col_axis, cols, swept_ref, gamma_ref, window_ref, one_ref, two_ref, out_ref):
    nx = window_ref.shape[1]
    ny = SUB
    col = lax.axis_index(col_axis)
    odd = lax.rem(col, 2) == 1
    first, last = col == 0, col == cols - 1
    lane = lax.broadcasted_iota(jnp.int32, (SUB, LANES), 1)
    slot = lane % GROUP
    for tile in range(nx // SUB):
        base = tile * SUB
        rows = pl.ds(base, SUB)
        left_window, right_window = [], []
        for f in range(6):
            own, one, two = window_ref[f, rows, :], one_ref[f, rows, :], two_ref[f, rows, :]
            before = jnp.where(odd, one, two)
            after = jnp.where(odd, two, one)
            low = jnp.where(
                slot == 3,
                pltpu.roll(own, LANES - 3, 1),
                jnp.where(slot == 4, pltpu.roll(own, LANES - 2, 1), pltpu.roll(own, LANES - 1, 1)),
            )
            high = jnp.where(
                slot == 6,
                pltpu.roll(own, 1, 1),
                jnp.where(slot == 7, pltpu.roll(own, 2, 1), pltpu.roll(own, 3, 1)),
            )
            before = jnp.where(first, low, before)
            after = jnp.where(last, high, after)
            left_window.append(jnp.where((slot >= 3) & (slot <= 5), before, own))
            right_window.append(jnp.where((slot >= 6) & (slot <= 8), after, own))
        left_new = sweep_lanes(left_window[:5], left_window[5], 2)
        right_new = sweep_lanes(right_window[:5], right_window[5], 2)
        edge_new = [jnp.where(slot >= 6, a, b) for a, b in zip(left_new, right_new)]
        at_edge = (lane < HALO) | (lane >= LANES - HALO)
        for y in range(ny):
            at = pl.ds(y * nx + base, SUB)
            cons = [swept_ref[f, at, :] for f in range(5)]
            inner = sweep_lanes(cons, gamma_ref[5, at, :], 2)
            turn = (LANES - 6 - GROUP * y) % LANES
            for f in range(5):
                edge = pltpu.roll(edge_new[f], turn, 1)
                out_ref[f, pl.ds(base * ny + y, SUB, stride=ny), :] = jnp.where(
                    at_edge, edge, inner[f]
                )


def swap_pairs(mesh, axis, inner):
    rows, cols = mesh.shape["row"], mesh.shape["col"]
    pairs = []
    for r in range(rows):
        for c in range(cols):
            k, n = (r, rows) if axis == "row" else (c, cols)
            if not inner:
                k ^= 1
            elif 0 < k < n - 1:
                k = ((k - 1) ^ 1) + 1
            else:
                k = None
            if axis == "row":
                to = (r, c ^ 1) if k is None else (k, c)
            else:
                to = (r ^ 1, c) if k is None else (r, k)
            pairs.append((r * cols + c, to[0] * cols + to[1]))
    return pairs


def body(mesh, state, gamma):
    rows, cols = mesh.shape["row"], mesh.shape["col"]
    _, nx, ny, nz = state.shape
    assert ny == SUB and nz == LANES and nx % SUB == 0 and rows % 2 == 0 and cols % 2 == 0
    shape = lambda *dims: jax.ShapeDtypeStruct(dims, jnp.float32)
    swap = lambda x, axis, inner: lax.ppermute(x, ("row", "col"), swap_pairs(mesh, axis, inner))

    swept, one, two = pl.pallas_call(
        functools.partial(first_kernel, "row"),
        out_shape=(
            shape(6, ny * nx, nz),
            shape(6, HALO * nx, nz),
            shape(6, HALO * nx, nz),
        ),
        name="sweep_first",
    )(state, gamma)
    one, two = swap(one, "row", False), swap(two, "row", True)
    after, window = pl.pallas_call(
        functools.partial(second_kernel, "row", rows),
        out_shape=(shape(5, ny * nx, nz), shape(6, nx, nz)),
        name="sweep_second",
    )(swept, one, two)
    one, two = swap(window, "col", False), swap(window, "col", True)
    out = pl.pallas_call(
        functools.partial(third_kernel, "col", cols),
        out_shape=shape(5, nx * ny, nz),
        name="sweep_third",
    )(after, swept, window, one, two)
    return out.reshape(5, nx, ny, nz)


def solution(mesh):
    in_specs = (P(None, None, "row", "col"), P(None, "row", "col"))
    out_specs = P(None, None, "row", "col")
    return jax.shard_map(
        functools.partial(body, mesh),
        mesh=mesh,
        in_specs=in_specs,
        out_specs=out_specs,
        check_vma=False,
    )
```

```python
import functools

import jax
import jax.numpy as jnp
from jax import lax
from jax.experimental import pallas as pl
from jax.experimental.pallas import tpu as pltpu
from jax.sharding import PartitionSpec as P

STEP = 0.08
HALO = 3
SUB, LANES = 8, 128
GROUP = LANES // SUB


def recip(x):
    r = pl.reciprocal(x, approx=True)
    return r * (2.0 - x * r)


def clamp_zero(u, v):
    return jnp.maximum(jnp.minimum(u, jnp.maximum(v, 0.0)), jnp.minimum(v, 0.0))


def primitives(cons, gam1, normal):
    rho, m0, m1, m2, energy = cons
    inv = recip(rho)
    vel = [m0 * inv, m1 * inv, m2 * inv]
    kinetic = 0.5 * (m0 * vel[0] + m1 * vel[1] + m2 * vel[2])
    pressure = gam1 * (energy - kinetic)
    others = [c for c in range(3) if c != normal]
    return [rho, vel[normal], vel[others[0]], vel[others[1]], pressure]


def face_rise(before, here, after):
    if here is None:
        return None
    rise = 0.5 * here
    if before is not None and after is not None:
        rise = rise + (before - after) * (1.0 / 12.0)
    elif before is not None:
        rise = rise + before * (1.0 / 12.0)
    elif after is not None:
        rise = rise - after * (1.0 / 12.0)
    return clamp_zero(rise, here)


def edges(q, right, left):
    if right is None or left is None:
        return q, q
    return q + clamp_zero(right, 2.0 * left), q - clamp_zero(left, 2.0 * right)


def state_flux(prim, gamma, inv_gam1):
    rho, un, u1, u2, p = prim
    mn, m1, m2 = rho * un, rho * u1, rho * u2
    nn = mn * un
    energy = p * inv_gam1 + 0.5 * (nn + m1 * u1 + m2 * u2)
    flux = [mn, nn + p, mn * u1, mn * u2, un * (energy + p)]
    gp = gamma * p
    speed = jnp.abs(un) + gp * lax.rsqrt(jnp.maximum(gp * rho, 1e-30))
    return [rho, mn, m1, m2, energy], flux, speed


def double_flux(left, right):
    if left is right:
        return [f + f for f in left[1]]
    speed = jnp.maximum(left[2], right[2])
    return [
        (left[1][k] + right[1][k]) - speed * (right[0][k] - left[0][k]) for k in range(5)
    ]


def place(normal):
    others = [c for c in range(3) if c != normal]
    return [0, 1 + normal, 1 + others[0], 1 + others[1], 4]


def updated(cons, flux_right, flux_left, normal):
    out = list(cons)
    for k, field in enumerate(place(normal)):
        out[field] = cons[field] - (0.5 * STEP) * (flux_right[k] - flux_left[k])
    return out


def sweep_rows(load, load_gamma, store, n, normal, outflow):
    cons, gam, prim, diff, rise, edge = {}, {}, {}, {}, {}, {}

    def zone(i):
        return min(max(i, 0), n - 1) if outflow else i

    def get(i):
        i = zone(i)
        if i not in cons:
            cons[i] = load(i)
            g = load_gamma(i)
            gam1 = g - 1.0
            gam[i] = (g, recip(gam1))
            prim[i] = primitives(cons[i], gam1, normal)
        return prim[i]

    def get_diff(i):
        if i not in diff:
            a, b = get(i), get(i + 1)
            diff[i] = [None] * 5 if a is b else [y - x for x, y in zip(a, b)]
        return diff[i]

    def get_rise(i):
        if i not in rise:
            before, here, after = get_diff(i - 1), get_diff(i), get_diff(i + 1)
            right = [face_rise(*t) for t in zip(before, here, after)]
            left = [None if r is None else h - r for h, r in zip(here, right)]
            rise[i] = (right, left)
        return rise[i]

    def get_edge(i):
        if i not in edge:
            q, right, left = get(i), get_rise(i)[0], get_rise(i - 1)[1]
            pairs = [edges(*t) for t in zip(q, right, left)]
            upper = [p[0] for p in pairs]
            lower = [p[1] for p in pairs]
            if all(u is w for u, w in zip(upper, lower)):
                one = state_flux(upper, *gam[zone(i)])
                edge[i] = (one, one, zone(i))
            else:
                edge[i] = [upper, lower, zone(i)]
        return edge[i]

    def side(i, which):
        e = get_edge(i)
        if isinstance(e, tuple):
            return e[which]
        return state_flux(e[which], *gam[e[2]])

    def face(i):
        if outflow and i < 0:
            whole = get_edge(0)
            return double_flux(whole[0], whole[0])
        if outflow and i == n - 1:
            whole = get_edge(n - 1)
            return double_flux(whole[1], whole[1])
        return double_flux(side(i, 0), side(i + 1, 1))

    previous = face(-1)
    for i in range(n):
        current = face(i)
        store(i, updated(cons[i], current, previous, normal))
        previous = current


def first_kernel(row_axis, state_ref, gamma_ref, swept_ref, one_ref, two_ref):
    nx, ny = gamma_ref.shape[0], gamma_ref.shape[1]

    def store(x, cons):
        for f in range(5):
            swept_ref[f, pl.ds(x, ny, stride=nx), :] = cons[f]

    sweep_rows(
        lambda x: [state_ref[f, x] for f in range(5)],
        lambda x: gamma_ref[x],
        store,
        nx,
        0,
        True,
    )
    for x in range(nx):
        swept_ref[5, pl.ds(x, ny, stride=nx), :] = gamma_ref[x]
    odd = lax.rem(lax.axis_index(row_axis), 2)
    low, high = 0, (ny - HALO) * nx
    start_one = pl.multiple_of(jnp.where(odd == 1, low, high), SUB)
    start_two = pl.multiple_of(jnp.where(odd == 1, high, low), SUB)
    for f in range(6):
        one_ref[f] = swept_ref[f, pl.ds(start_one, HALO * nx), :]
        two_ref[f] = swept_ref[f, pl.ds(start_two, HALO * nx), :]


def second_kernel(row_axis, rows, swept_ref, one_ref, two_ref, next_ref, window_ref):
    nx = swept_ref.shape[1] // SUB
    ny = SUB
    row = lax.axis_index(row_axis)
    odd = lax.rem(row, 2) == 1
    first, last = row == 0, row == rows - 1
    lane = lax.broadcasted_iota(jnp.int32, (SUB, LANES), 1)
    group = lane // GROUP
    for tile in range(nx // SUB):
        base = tile * SUB

        def load_field(f, y):
            if 0 <= y < ny:
                return swept_ref[f, pl.ds(y * nx + base, SUB), :]
            at = pl.ds((y + HALO if y < 0 else y - ny) * nx + base, SUB)
            one, two = one_ref[f, at, :], two_ref[f, at, :]
            if y < 0:
                got = jnp.where(odd, one, two)
                return jnp.where(first, swept_ref[f, pl.ds(base, SUB), :], got)
            got = jnp.where(odd, two, one)
            return jnp.where(last, swept_ref[f, pl.ds((ny - 1) * nx + base, SUB), :], got)

        windows = [None] * 6

        def into_window(f, y, value):
            turn = (GROUP * y + 6) % LANES
            rolled = pltpu.roll(value, turn, 1) if turn else value
            windows[f] = rolled if windows[f] is None else jnp.where(group == y, rolled, windows[f])

        def store(y, cons):
            for f in range(5):
                next_ref[f, pl.ds(y * nx + base, SUB), :] = cons[f]
                into_window(f, y, cons[f])

        sweep_rows(
            lambda y: [load_field(f, y) for f in range(5)],
            lambda y: load_field(5, y),
            store,
            ny,
            1,
            False,
        )
        for y in range(ny):
            into_window(5, y, swept_ref[5, pl.ds(y * nx + base, SUB), :])
        for f in range(6):
            window_ref[f, pl.ds(base, SUB), :] = windows[f]


def sweep_lanes(cons, gamma, normal):
    def ahead(x):
        return pltpu.roll(x, LANES - 1, 1)

    def behind(x):
        return pltpu.roll(x, 1, 1)

    gam1 = gamma - 1.0
    inv_gam1 = recip(gam1)
    prim = primitives(cons, gam1, normal)
    upper, lower_next = [], []
    for q in prim:
        here = ahead(q) - q
        right = face_rise(behind(here), here, ahead(here))
        left = behind(here - right)
        up, low = edges(q, right, left)
        upper.append(up)
        lower_next.append(ahead(low))
    flux = double_flux(
        state_flux(upper, gamma, inv_gam1),
        state_flux(lower_next, ahead(gamma), ahead(inv_gam1)),
    )
    return updated(cons, flux, [behind(x) for x in flux], normal)


def third_kernel(col_axis, cols, swept_ref, gamma_ref, window_ref, one_ref, two_ref, out_ref):
    nx = window_ref.shape[1]
    ny = SUB
    col = lax.axis_index(col_axis)
    odd = lax.rem(col, 2) == 1
    first, last = col == 0, col == cols - 1
    lane = lax.broadcasted_iota(jnp.int32, (SUB, LANES), 1)
    slot = lane % GROUP
    for tile in range(nx // SUB):
        base = tile * SUB
        rows = pl.ds(base, SUB)
        left_window, right_window = [], []
        for f in range(6):
            own, one, two = window_ref[f, rows, :], one_ref[f, rows, :], two_ref[f, rows, :]
            before = jnp.where(odd, one, two)
            after = jnp.where(odd, two, one)
            low = jnp.where(
                slot == 3,
                pltpu.roll(own, LANES - 3, 1),
                jnp.where(slot == 4, pltpu.roll(own, LANES - 2, 1), pltpu.roll(own, LANES - 1, 1)),
            )
            high = jnp.where(
                slot == 6,
                pltpu.roll(own, 1, 1),
                jnp.where(slot == 7, pltpu.roll(own, 2, 1), pltpu.roll(own, 3, 1)),
            )
            before = jnp.where(first, low, before)
            after = jnp.where(last, high, after)
            left_window.append(jnp.where((slot >= 3) & (slot <= 5), before, own))
            right_window.append(jnp.where((slot >= 6) & (slot <= 8), after, own))
        left_new = sweep_lanes(left_window[:5], left_window[5], 2)
        right_new = sweep_lanes(right_window[:5], right_window[5], 2)
        edge_new = [jnp.where(slot >= 6, a, b) for a, b in zip(left_new, right_new)]
        at_edge = (lane < HALO) | (lane >= LANES - HALO)
        for y in range(ny):
            at = pl.ds(y * nx + base, SUB)
            cons = [swept_ref[f, at, :] for f in range(5)]
            inner = sweep_lanes(cons, gamma_ref[5, at, :], 2)
            turn = (LANES - 6 - GROUP * y) % LANES
            for f in range(5):
                edge = pltpu.roll(edge_new[f], turn, 1)
                out_ref[f, pl.ds(base * ny + y, SUB, stride=ny), :] = jnp.where(
                    at_edge, edge, inner[f]
                )


def swap_pairs(mesh, axis, inner):
    rows, cols = mesh.shape["row"], mesh.shape["col"]
    pairs = []
    for r in range(rows):
        for c in range(cols):
            k, n = (r, rows) if axis == "row" else (c, cols)
            if not inner:
                k ^= 1
            elif 0 < k < n - 1:
                k = ((k - 1) ^ 1) + 1
            else:
                k = None
            if axis == "row":
                to = (r, c ^ 1) if k is None else (k, c)
            else:
                to = (r ^ 1, c) if k is None else (r, k)
            pairs.append((r * cols + c, to[0] * cols + to[1]))
    return pairs


def body(mesh, state, gamma):
    rows, cols = mesh.shape["row"], mesh.shape["col"]
    _, nx, ny, nz = state.shape
    assert ny == SUB and nz == LANES and nx % SUB == 0 and rows % 2 == 0 and cols % 2 == 0
    here = lambda *dims: pltpu.VMEM(dims, jnp.float32)
    keep = lambda x: pltpu.with_memory_space_constraint(x, pltpu.VMEM)
    near = pl.BlockSpec(memory_space=pltpu.VMEM)
    swap = lambda x, axis, inner: lax.ppermute(x, ("row", "col"), swap_pairs(mesh, axis, inner))

    swept, one, two = pl.pallas_call(
        functools.partial(first_kernel, "row"),
        out_shape=(
            here(6, ny * nx, nz),
            here(6, HALO * nx, nz),
            here(6, HALO * nx, nz),
        ),
        out_specs=(near,) * 3,
        name="sweep_first",
    )(state, gamma)
    one, two = swap(one, "row", False), swap(two, "row", True)
    after, window = pl.pallas_call(
        functools.partial(second_kernel, "row", rows),
        out_shape=(here(5, ny * nx, nz), here(6, nx, nz)),
        in_specs=[near] * 3,
        out_specs=(near,) * 2,
        name="sweep_second",
    )(keep(swept), keep(one), keep(two))
    one, two = swap(window, "col", False), swap(window, "col", True)
    out = pl.pallas_call(
        functools.partial(third_kernel, "col", cols),
        out_shape=jax.ShapeDtypeStruct((5, nx * ny, nz), jnp.float32),
        in_specs=[near] * 5,
        name="sweep_third",
    )(keep(after), keep(swept), keep(window), keep(one), keep(two))
    return out.reshape(5, nx, ny, nz)


def solution(mesh):
    in_specs = (P(None, None, "row", "col"), P(None, "row", "col"))
    out_specs = P(None, None, "row", "col")
    return jax.shard_map(
        functools.partial(body, mesh),
        mesh=mesh,
        in_specs=in_specs,
        out_specs=out_specs,
        check_vma=False,
    )
```

```python
import functools

import jax
import jax.numpy as jnp
from jax import lax
from jax.experimental import pallas as pl
from jax.experimental.pallas import tpu as pltpu
from jax.sharding import PartitionSpec as P

STEP = 0.08
HALO = 3
SUB, LANES = 8, 128
GROUP = LANES // SUB


def recip(x):
    r = pl.reciprocal(x, approx=True)
    return r * (2.0 - x * r)


def clamp_zero(u, v):
    return jnp.maximum(jnp.minimum(u, jnp.maximum(v, 0.0)), jnp.minimum(v, 0.0))


def primitives(cons, gam1, normal):
    rho, m0, m1, m2, energy = cons
    inv = recip(rho)
    vel = [m0 * inv, m1 * inv, m2 * inv]
    kinetic = 0.5 * (m0 * vel[0] + m1 * vel[1] + m2 * vel[2])
    pressure = gam1 * (energy - kinetic)
    others = [c for c in range(3) if c != normal]
    return [rho, vel[normal], vel[others[0]], vel[others[1]], pressure]


def face_rise(before, here, after):
    if here is None:
        return None
    rise = 0.5 * here
    if before is not None and after is not None:
        rise = rise + (before - after) * (1.0 / 12.0)
    elif before is not None:
        rise = rise + before * (1.0 / 12.0)
    elif after is not None:
        rise = rise - after * (1.0 / 12.0)
    return clamp_zero(rise, here)


def edges(q, right, left):
    if right is None or left is None:
        return q, q
    return q + clamp_zero(right, 2.0 * left), q - clamp_zero(left, 2.0 * right)


def state_flux(prim, gamma, inv_gam1):
    rho, un, u1, u2, p = prim
    mn, m1, m2 = rho * un, rho * u1, rho * u2
    nn = mn * un
    energy = p * inv_gam1 + 0.5 * (nn + m1 * u1 + m2 * u2)
    flux = [mn, nn + p, mn * u1, mn * u2, un * (energy + p)]
    gp = gamma * p
    speed = jnp.abs(un) + gp * lax.rsqrt(jnp.maximum(gp * rho, 1e-30))
    return [rho, mn, m1, m2, energy], flux, speed


def double_flux(left, right):
    if left is right:
        return [f + f for f in left[1]]
    speed = jnp.maximum(left[2], right[2])
    return [
        (left[1][k] + right[1][k]) - speed * (right[0][k] - left[0][k]) for k in range(5)
    ]


def place(normal):
    others = [c for c in range(3) if c != normal]
    return [0, 1 + normal, 1 + others[0], 1 + others[1], 4]


def updated(cons, flux_right, flux_left, normal):
    out = list(cons)
    for k, field in enumerate(place(normal)):
        out[field] = cons[field] - (0.5 * STEP) * (flux_right[k] - flux_left[k])
    return out


def sweep_rows(load, load_gamma, store, n, normal, outflow):
    cons, gam, prim, diff, rise, edge = {}, {}, {}, {}, {}, {}

    def zone(i):
        return min(max(i, 0), n - 1) if outflow else i

    def get(i):
        i = zone(i)
        if i not in cons:
            cons[i] = load(i)
            g = load_gamma(i)
            gam1 = g - 1.0
            gam[i] = (g, recip(gam1))
            prim[i] = primitives(cons[i], gam1, normal)
        return prim[i]

    def get_diff(i):
        if i not in diff:
            a, b = get(i), get(i + 1)
            diff[i] = [None] * 5 if a is b else [y - x for x, y in zip(a, b)]
        return diff[i]

    def get_rise(i):
        if i not in rise:
            before, here, after = get_diff(i - 1), get_diff(i), get_diff(i + 1)
            right = [face_rise(*t) for t in zip(before, here, after)]
            left = [None if r is None else h - r for h, r in zip(here, right)]
            rise[i] = (right, left)
        return rise[i]

    def get_edge(i):
        if i not in edge:
            q, right, left = get(i), get_rise(i)[0], get_rise(i - 1)[1]
            pairs = [edges(*t) for t in zip(q, right, left)]
            upper = [p[0] for p in pairs]
            lower = [p[1] for p in pairs]
            if all(u is w for u, w in zip(upper, lower)):
                one = state_flux(upper, *gam[zone(i)])
                edge[i] = (one, one, zone(i))
            else:
                edge[i] = [upper, lower, zone(i)]
        return edge[i]

    def side(i, which):
        e = get_edge(i)
        if isinstance(e, tuple):
            return e[which]
        return state_flux(e[which], *gam[e[2]])

    def face(i):
        if outflow and i < 0:
            whole = get_edge(0)
            return double_flux(whole[0], whole[0])
        if outflow and i == n - 1:
            whole = get_edge(n - 1)
            return double_flux(whole[1], whole[1])
        return double_flux(side(i, 0), side(i + 1, 1))

    previous = face(-1)
    for i in range(n):
        current = face(i)
        store(i, updated(cons[i], current, previous, normal))
        previous = current


def first_kernel(row_axis, state_ref, gamma_ref, swept_ref, one_ref, two_ref):
    nx, ny = gamma_ref.shape[0], gamma_ref.shape[1]

    def store(x, cons):
        for f in range(5):
            swept_ref[f, pl.ds(x, ny, stride=nx), :] = cons[f]

    sweep_rows(
        lambda x: [state_ref[f, x] for f in range(5)],
        lambda x: gamma_ref[x],
        store,
        nx,
        0,
        True,
    )
    for x in range(nx):
        swept_ref[5, pl.ds(x, ny, stride=nx), :] = gamma_ref[x]
    odd = lax.rem(lax.axis_index(row_axis), 2)
    low, high = 0, (ny - HALO) * nx
    start_one = pl.multiple_of(jnp.where(odd == 1, low, high), SUB)
    start_two = pl.multiple_of(jnp.where(odd == 1, high, low), SUB)
    for f in range(6):
        one_ref[f] = swept_ref[f, pl.ds(start_one, HALO * nx), :]
        two_ref[f] = swept_ref[f, pl.ds(start_two, HALO * nx), :]


def second_kernel(row_axis, rows, swept_ref, one_ref, two_ref, next_ref, window_ref):
    nx = swept_ref.shape[1] // SUB
    ny = SUB
    row = lax.axis_index(row_axis)
    odd = lax.rem(row, 2) == 1
    first, last = row == 0, row == rows - 1
    lane = lax.broadcasted_iota(jnp.int32, (SUB, LANES), 1)
    group = lane // GROUP
    for tile in range(nx // SUB):
        base = tile * SUB

        def load_field(f, y):
            if 0 <= y < ny:
                return swept_ref[f, pl.ds(y * nx + base, SUB), :]
            at = pl.ds((y + HALO if y < 0 else y - ny) * nx + base, SUB)
            one, two = one_ref[f, at, :], two_ref[f, at, :]
            if y < 0:
                got = jnp.where(odd, one, two)
                return jnp.where(first, swept_ref[f, pl.ds(base, SUB), :], got)
            got = jnp.where(odd, two, one)
            return jnp.where(last, swept_ref[f, pl.ds((ny - 1) * nx + base, SUB), :], got)

        windows = [None] * 6

        def into_window(f, y, value):
            turn = (GROUP * y + 6) % LANES
            rolled = pltpu.roll(value, turn, 1) if turn else value
            windows[f] = rolled if windows[f] is None else jnp.where(group == y, rolled, windows[f])

        def store(y, cons):
            for f in range(5):
                next_ref[f, pl.ds(y * nx + base, SUB), :] = cons[f]
                into_window(f, y, cons[f])

        sweep_rows(
            lambda y: [load_field(f, y) for f in range(5)],
            lambda y: load_field(5, y),
            store,
            ny,
            1,
            False,
        )
        for y in range(ny):
            into_window(5, y, swept_ref[5, pl.ds(y * nx + base, SUB), :])
        for f in range(6):
            window_ref[f, pl.ds(base, SUB), :] = windows[f]


def sweep_lanes(cons, gamma, normal):
    def ahead(x):
        return pltpu.roll(x, LANES - 1, 1)

    def behind(x):
        return pltpu.roll(x, 1, 1)

    gam1 = gamma - 1.0
    inv_gam1 = recip(gam1)
    prim = primitives(cons, gam1, normal)
    upper, lower_next = [], []
    for q in prim:
        here = ahead(q) - q
        right = face_rise(behind(here), here, ahead(here))
        left = behind(here - right)
        up, low = edges(q, right, left)
        upper.append(up)
        lower_next.append(ahead(low))
    flux = double_flux(
        state_flux(upper, gamma, inv_gam1),
        state_flux(lower_next, ahead(gamma), ahead(inv_gam1)),
    )
    return updated(cons, flux, [behind(x) for x in flux], normal)


def third_kernel(swept_ref, gamma_ref, out_ref):
    ny = SUB
    nx = swept_ref.shape[1] // ny
    for tile in range(nx // SUB):
        base = tile * SUB
        for y in range(ny):
            at = pl.ds(y * nx + base, SUB)
            cons = [swept_ref[f, at, :] for f in range(5)]
            inner = sweep_lanes(cons, gamma_ref[5, at, :], 2)
            for f in range(5):
                out_ref[f, pl.ds(base * ny + y, SUB, stride=ny), :] = inner[f]


def edge_kernel(col_axis, cols, inner_ref, window_ref, one_ref, two_ref, out_ref, held, sems):
    nx = window_ref.shape[1]
    ny = SUB
    col = lax.axis_index(col_axis)
    odd = lax.rem(col, 2) == 1
    first, last = col == 0, col == cols - 1
    lane = lax.broadcasted_iota(jnp.int32, (SUB, LANES), 1)
    slot = lane % GROUP
    at_edge = (lane < HALO) | (lane >= LANES - HALO)
    edge_new = []
    for tile in range(nx // SUB):
        rows = pl.ds(tile * SUB, SUB)
        left_window, right_window = [], []
        for f in range(6):
            own, one, two = window_ref[f, rows, :], one_ref[f, rows, :], two_ref[f, rows, :]
            before = jnp.where(odd, one, two)
            after = jnp.where(odd, two, one)
            low = jnp.where(
                slot == 3,
                pltpu.roll(own, LANES - 3, 1),
                jnp.where(slot == 4, pltpu.roll(own, LANES - 2, 1), pltpu.roll(own, LANES - 1, 1)),
            )
            high = jnp.where(
                slot == 6,
                pltpu.roll(own, 1, 1),
                jnp.where(slot == 7, pltpu.roll(own, 2, 1), pltpu.roll(own, 3, 1)),
            )
            before = jnp.where(first, low, before)
            after = jnp.where(last, high, after)
            left_window.append(jnp.where((slot >= 3) & (slot <= 5), before, own))
            right_window.append(jnp.where((slot >= 6) & (slot <= 8), after, own))
        left_new = sweep_lanes(left_window[:5], left_window[5], 2)
        right_new = sweep_lanes(right_window[:5], right_window[5], 2)
        edge_new.append([jnp.where(slot >= 6, a, b) for a, b in zip(left_new, right_new)])
    copies = []
    for f in range(5):
        for tile in range(nx // SUB):
            for y in range(ny):
                turn = (LANES - 6 - GROUP * y) % LANES
                edge = pltpu.roll(edge_new[tile][f], turn, 1)
                at = pl.ds(tile * SUB * ny + y, SUB, stride=ny)
                held[f, at, :] = jnp.where(at_edge, edge, inner_ref[f, at, :])
        copy = pltpu.make_async_copy(held.at[f], out_ref.at[f], sems.at[f])
        copy.start()
        copies.append(copy)
    for copy in copies:
        copy.wait()


def swap_pairs(mesh, axis, inner):
    rows, cols = mesh.shape["row"], mesh.shape["col"]
    pairs = []
    for r in range(rows):
        for c in range(cols):
            k, n = (r, rows) if axis == "row" else (c, cols)
            if not inner:
                k ^= 1
            elif 0 < k < n - 1:
                k = ((k - 1) ^ 1) + 1
            else:
                k = None
            if axis == "row":
                to = (r, c ^ 1) if k is None else (k, c)
            else:
                to = (r, cols - 1 - c) if k is None else (r, k)
            pairs.append((r * cols + c, to[0] * cols + to[1]))
    return pairs


def body(mesh, state, gamma):
    rows, cols = mesh.shape["row"], mesh.shape["col"]
    _, nx, ny, nz = state.shape
    assert ny == SUB and nz == LANES and nx % SUB == 0 and rows % 2 == 0 and cols % 2 == 0
    here = lambda *dims: pltpu.VMEM(dims, jnp.float32)
    keep = lambda x: pltpu.with_memory_space_constraint(x, pltpu.VMEM)
    near = pl.BlockSpec(memory_space=pltpu.VMEM)
    swap = lambda x, axis, inner: lax.ppermute(x, ("row", "col"), swap_pairs(mesh, axis, inner))

    swept, one, two = pl.pallas_call(
        functools.partial(first_kernel, "row"),
        out_shape=(
            here(6, ny * nx, nz),
            here(6, HALO * nx, nz),
            here(6, HALO * nx, nz),
        ),
        out_specs=(near,) * 3,
        name="sweep_first",
    )(state, gamma)
    one, two = swap(one, "row", False), swap(two, "row", True)
    after, window = pl.pallas_call(
        functools.partial(second_kernel, "row", rows),
        out_shape=(here(5, ny * nx, nz), here(6, nx, nz)),
        in_specs=[near] * 3,
        out_specs=(near,) * 2,
        name="sweep_second",
    )(keep(swept), keep(one), keep(two))
    one, two = swap(window, "col", False), swap(window, "col", True)
    inner = pl.pallas_call(
        third_kernel,
        out_shape=here(5, nx * ny, nz),
        in_specs=[near] * 2,
        out_specs=near,
        name="sweep_third",
    )(keep(after), keep(swept))
    out = pl.pallas_call(
        functools.partial(edge_kernel, "col", cols),
        out_shape=jax.ShapeDtypeStruct((5, nx * ny, nz), jnp.float32),
        in_specs=[near] * 4,
        out_specs=pl.BlockSpec(memory_space=pltpu.HBM),
        scratch_shapes=[
            pltpu.VMEM((5, nx * ny, nz), jnp.float32),
            pltpu.SemaphoreType.DMA((5,)),
        ],
        name="third_edges",
    )(keep(inner), keep(window), keep(one), keep(two))
    return out.reshape(5, nx, ny, nz)


def solution(mesh):
    in_specs = (P(None, None, "row", "col"), P(None, "row", "col"))
    out_specs = P(None, None, "row", "col")
    return jax.shard_map(
        functools.partial(body, mesh),
        mesh=mesh,
        in_specs=in_specs,
        out_specs=out_specs,
        check_vma=False,
    )
```

```python
import functools

import jax
import jax.numpy as jnp
from jax import lax
from jax.experimental import pallas as pl
from jax.experimental.pallas import tpu as pltpu
from jax.sharding import PartitionSpec as P

STEP = 0.08
HALO = 3
SUB, LANES = 8, 128
GROUP = LANES // SUB


def recip(x):
    r = pl.reciprocal(x, approx=True)
    return r * (2.0 - x * r)


def clamp_zero(u, v):
    return jnp.maximum(jnp.minimum(u, jnp.maximum(v, 0.0)), jnp.minimum(v, 0.0))


def primitives(cons, gam1, normal):
    rho, m0, m1, m2, energy = cons
    inv = recip(rho)
    vel = [m0 * inv, m1 * inv, m2 * inv]
    kinetic = 0.5 * (m0 * vel[0] + m1 * vel[1] + m2 * vel[2])
    pressure = gam1 * (energy - kinetic)
    others = [c for c in range(3) if c != normal]
    return [rho, vel[normal], vel[others[0]], vel[others[1]], pressure]


def face_rise(before, here, after):
    if here is None:
        return None
    rise = 0.5 * here
    if before is not None and after is not None:
        rise = rise + (before - after) * (1.0 / 12.0)
    elif before is not None:
        rise = rise + before * (1.0 / 12.0)
    elif after is not None:
        rise = rise - after * (1.0 / 12.0)
    return clamp_zero(rise, here)


def edges(q, right, left):
    if right is None or left is None:
        return q, q
    return q + clamp_zero(right, 2.0 * left), q - clamp_zero(left, 2.0 * right)


def state_flux(prim, gamma, inv_gam1):
    rho, un, u1, u2, p = prim
    mn, m1, m2 = rho * un, rho * u1, rho * u2
    nn = mn * un
    energy = p * inv_gam1 + 0.5 * (nn + m1 * u1 + m2 * u2)
    flux = [mn, nn + p, mn * u1, mn * u2, un * (energy + p)]
    gp = gamma * p
    speed = jnp.abs(un) + gp * lax.rsqrt(jnp.maximum(gp * rho, 1e-30))
    return [rho, mn, m1, m2, energy], flux, speed


def double_flux(left, right):
    if left is right:
        return [f + f for f in left[1]]
    speed = jnp.maximum(left[2], right[2])
    return [
        (left[1][k] + right[1][k]) - speed * (right[0][k] - left[0][k]) for k in range(5)
    ]


def place(normal):
    others = [c for c in range(3) if c != normal]
    return [0, 1 + normal, 1 + others[0], 1 + others[1], 4]


def updated(cons, flux_right, flux_left, normal):
    out = list(cons)
    for k, field in enumerate(place(normal)):
        out[field] = cons[field] - (0.5 * STEP) * (flux_right[k] - flux_left[k])
    return out


def sweep_rows(load, load_gamma, store, n, normal, halo=None):
    outflow = halo is None
    cons, gam, prim, diff, rise, edge = {}, {}, {}, {}, {}, {}

    def zone(i):
        return min(max(i, 0), n - 1) if outflow else i

    def get(i):
        i = zone(i)
        if i not in cons:
            inside = 0 <= i < n
            if inside or i in (-1, n):
                g = load_gamma(i)
                gam1 = g - 1.0
                gam[i] = (g, recip(gam1))
            if inside:
                cons[i] = load(i)
                prim[i] = primitives(cons[i], gam1, normal)
            else:
                prim[i] = halo(i, get(0 if i < 0 else n - 1))
        return prim[i]

    def get_diff(i):
        if i not in diff:
            a, b = get(i), get(i + 1)
            diff[i] = [None] * 5 if a is b else [y - x for x, y in zip(a, b)]
        return diff[i]

    def get_rise(i):
        if i not in rise:
            before, here, after = get_diff(i - 1), get_diff(i), get_diff(i + 1)
            right = [face_rise(*t) for t in zip(before, here, after)]
            left = [None if r is None else h - r for h, r in zip(here, right)]
            rise[i] = (right, left)
        return rise[i]

    def get_edge(i):
        if i not in edge:
            q, right, left = get(i), get_rise(i)[0], get_rise(i - 1)[1]
            pairs = [edges(*t) for t in zip(q, right, left)]
            upper = [p[0] for p in pairs]
            lower = [p[1] for p in pairs]
            if all(u is w for u, w in zip(upper, lower)):
                one = state_flux(upper, *gam[zone(i)])
                edge[i] = (one, one, zone(i))
            else:
                edge[i] = [upper, lower, zone(i)]
        return edge[i]

    def side(i, which):
        e = get_edge(i)
        if isinstance(e, tuple):
            return e[which]
        return state_flux(e[which], *gam[e[2]])

    def face(i):
        if outflow and i < 0:
            whole = get_edge(0)
            return double_flux(whole[0], whole[0])
        if outflow and i == n - 1:
            whole = get_edge(n - 1)
            return double_flux(whole[1], whole[1])
        return double_flux(side(i, 0), side(i + 1, 1))

    previous = face(-1)
    for i in range(n):
        current = face(i)
        store(i, updated(cons[i], current, previous, normal))
        previous = current


def first_kernel(row_axis, state_ref, gamma_ref, swept_ref, one_ref, two_ref):
    nx, ny = gamma_ref.shape[0], gamma_ref.shape[1]

    def store(x, cons):
        for f in range(5):
            swept_ref[f, pl.ds(x, ny, stride=nx), :] = cons[f]

    sweep_rows(
        lambda x: [state_ref[f, x] for f in range(5)],
        lambda x: gamma_ref[x],
        store,
        nx,
        0,
    )
    for x in range(nx):
        swept_ref[5, pl.ds(x, ny, stride=nx), :] = gamma_ref[x]
    odd = lax.rem(lax.axis_index(row_axis), 2) == 1
    for base in range(0, nx, SUB):
        sides = []
        for zones, last in ((range(HALO), 0), (range(ny - HALO, ny), ny - 1)):
            rows = []
            for y in zones:
                at = pl.ds(y * nx + base, SUB)
                gamma = swept_ref[5, at, :]
                rows.append(primitives([swept_ref[f, at, :] for f in range(5)], gamma - 1.0, 1))
            rows = [row[k] for k in range(5) for row in rows]
            rows.append(swept_ref[5, pl.ds(last * nx + base, SUB), :])
            sides.append(rows)
        at = pl.ds(base, SUB)
        for k, (low, high) in enumerate(zip(*sides)):
            one_ref[k, at, :] = jnp.where(odd, low, high)
            two_ref[k, at, :] = jnp.where(odd, high, low)


def second_kernel(row_axis, rows, swept_ref, two_ref, one_ref, next_ref, window_ref):
    nx = swept_ref.shape[1] // SUB
    ny = SUB
    row = lax.axis_index(row_axis)
    odd = lax.rem(row, 2) == 1
    first, last = row == 0, row == rows - 1
    lane = lax.broadcasted_iota(jnp.int32, (SUB, LANES), 1)
    group = lane // GROUP
    for tile in range(nx // SUB):
        base = tile * SUB

        at_base = pl.ds(base, SUB)

        def own(f, y):
            return swept_ref[f, pl.ds(y * nx + base, SUB), :]

        def received(k, low_side):
            one, two = one_ref[k, at_base, :], two_ref[k, at_base, :]
            return jnp.where(odd, one, two) if low_side else jnp.where(odd, two, one)

        def halo(y, nearest):
            j, end = (y + HALO, first) if y < 0 else (y - ny, last)
            return [
                jnp.where(end, nearest[k], received(HALO * k + j, y < 0)) for k in range(5)
            ]

        def load_gamma(y):
            if 0 <= y < ny:
                return own(5, y)
            end, edge = (first, 0) if y < 0 else (last, ny - 1)
            return jnp.where(end, own(5, edge), received(5 * HALO, y < 0))

        windows = [None] * 6

        def into_window(f, y, value):
            turn = (GROUP * y + 6) % LANES
            rolled = pltpu.roll(value, turn, 1) if turn else value
            windows[f] = rolled if windows[f] is None else jnp.where(group == y, rolled, windows[f])

        def store(y, cons):
            for f in range(5):
                next_ref[f, pl.ds(y * nx + base, SUB), :] = cons[f]
                into_window(f, y, cons[f])

        sweep_rows(
            lambda y: [own(f, y) for f in range(5)],
            load_gamma,
            store,
            ny,
            1,
            halo,
        )
        for y in range(ny):
            into_window(5, y, own(5, y))
        for f in range(6):
            window_ref[f, pl.ds(base, SUB), :] = windows[f]


def sweep_lanes(cons, gamma, normal):
    def ahead(x):
        return pltpu.roll(x, LANES - 1, 1)

    def behind(x):
        return pltpu.roll(x, 1, 1)

    gam1 = gamma - 1.0
    inv_gam1 = recip(gam1)
    prim = primitives(cons, gam1, normal)
    upper, lower_next = [], []
    for q in prim:
        here = ahead(q) - q
        right = face_rise(behind(here), here, ahead(here))
        left = behind(here - right)
        up, low = edges(q, right, left)
        upper.append(up)
        lower_next.append(ahead(low))
    flux = double_flux(
        state_flux(upper, gamma, inv_gam1),
        state_flux(lower_next, ahead(gamma), ahead(inv_gam1)),
    )
    return updated(cons, flux, [behind(x) for x in flux], normal)


def sweep_window(cons, gamma, normal):
    def turned(x, by):
        return pltpu.roll(x, (LANES - by) % LANES, 1)

    gam1 = gamma - 1.0
    inv_gam1 = recip(gam1)
    upper, lower = [], []
    for q in primitives(cons, gam1, normal):
        line = [q if k == 0 else turned(q, k) for k in range(-2, 4)]
        diff = [b - a for a, b in zip(line, line[1:])]
        rise = [face_rise(*diff[k : k + 3]) for k in range(3)]
        upper.append(q + clamp_zero(rise[1], 2.0 * (diff[1] - rise[0])))
        lower.append(line[3] - clamp_zero(diff[2] - rise[1], 2.0 * rise[2]))
    flux = double_flux(
        state_flux(upper, gamma, inv_gam1),
        state_flux(lower, turned(gamma, 1), turned(inv_gam1, 1)),
    )
    return updated(cons, flux, [turned(x, -1) for x in flux], normal)


def third_kernel(swept_ref, gamma_ref, out_ref):
    ny = SUB
    nx = swept_ref.shape[1] // ny
    for tile in range(nx // SUB):
        base = tile * SUB
        for y in range(ny):
            at = pl.ds(y * nx + base, SUB)
            cons = [swept_ref[f, at, :] for f in range(5)]
            inner = sweep_lanes(cons, gamma_ref[5, at, :], 2)
            for f in range(5):
                out_ref[f, pl.ds(base * ny + y, SUB, stride=ny), :] = inner[f]


def edge_kernel(col_axis, cols, inner_ref, window_ref, one_ref, two_ref, out_ref, held, sems):
    nx = window_ref.shape[1]
    ny = SUB
    col = lax.axis_index(col_axis)
    odd = lax.rem(col, 2) == 1
    first, last = col == 0, col == cols - 1
    lane = lax.broadcasted_iota(jnp.int32, (SUB, LANES), 1)
    slot = lane % GROUP
    at_edge = (lane < HALO) | (lane >= LANES - HALO)
    edge_new = []
    for tile in range(nx // SUB):
        rows = pl.ds(tile * SUB, SUB)
        left_window, right_window = [], []
        for f in range(6):
            own, one, two = window_ref[f, rows, :], one_ref[f, rows, :], two_ref[f, rows, :]
            before = jnp.where(odd, one, two)
            after = jnp.where(odd, two, one)
            low = jnp.where(
                slot == 3,
                pltpu.roll(own, LANES - 3, 1),
                jnp.where(slot == 4, pltpu.roll(own, LANES - 2, 1), pltpu.roll(own, LANES - 1, 1)),
            )
            high = jnp.where(
                slot == 6,
                pltpu.roll(own, 1, 1),
                jnp.where(slot == 7, pltpu.roll(own, 2, 1), pltpu.roll(own, 3, 1)),
            )
            before = jnp.where(first, low, before)
            after = jnp.where(last, high, after)
            left_window.append(jnp.where((slot >= 3) & (slot <= 5), before, own))
            right_window.append(jnp.where((slot >= 6) & (slot <= 8), after, own))
        left_new = sweep_window(left_window[:5], left_window[5], 2)
        right_new = sweep_window(right_window[:5], right_window[5], 2)
        edge_new.append([jnp.where(slot >= 6, a, b) for a, b in zip(left_new, right_new)])
    copies = []
    for f in range(5):
        for tile in range(nx // SUB):
            for y in range(ny):
                turn = (LANES - 6 - GROUP * y) % LANES
                edge = pltpu.roll(edge_new[tile][f], turn, 1)
                at = pl.ds(tile * SUB * ny + y, SUB, stride=ny)
                held[f, at, :] = jnp.where(at_edge, edge, inner_ref[f, at, :])
        copy = pltpu.make_async_copy(held.at[f], out_ref.at[f], sems.at[f])
        copy.start()
        copies.append(copy)
    for copy in copies:
        copy.wait()


def swap_pairs(mesh, axis, inner):
    rows, cols = mesh.shape["row"], mesh.shape["col"]
    pairs = []
    for r in range(rows):
        for c in range(cols):
            k, n = (r, rows) if axis == "row" else (c, cols)
            if not inner:
                k ^= 1
            elif 0 < k < n - 1:
                k = ((k - 1) ^ 1) + 1
            else:
                k = None
            if axis == "row":
                to = (r, c ^ 1) if k is None else (k, c)
            else:
                to = (r, cols - 1 - c) if k is None else (r, k)
            pairs.append((r * cols + c, to[0] * cols + to[1]))
    return pairs


def body(mesh, state, gamma):
    rows, cols = mesh.shape["row"], mesh.shape["col"]
    _, nx, ny, nz = state.shape
    assert ny == SUB and nz == LANES and nx % SUB == 0 and rows % 2 == 0 and cols % 2 == 0
    here = lambda *dims: pltpu.VMEM(dims, jnp.float32)
    keep = lambda x: pltpu.with_memory_space_constraint(x, pltpu.VMEM)
    near = pl.BlockSpec(memory_space=pltpu.VMEM)
    swap = lambda x, axis, inner: lax.ppermute(x, ("row", "col"), swap_pairs(mesh, axis, inner))

    swept, one, two = pl.pallas_call(
        functools.partial(first_kernel, "row"),
        out_shape=(
            here(6, ny * nx, nz),
            here(5 * HALO + 1, nx, nz),
            here(5 * HALO + 1, nx, nz),
        ),
        out_specs=(near,) * 3,
        name="sweep_first",
    )(state, gamma)
    two = swap(two, "row", True)
    one = swap(one, "row", False)
    after, window = pl.pallas_call(
        functools.partial(second_kernel, "row", rows),
        out_shape=(here(5, ny * nx, nz), here(6, nx, nz)),
        in_specs=[near] * 3,
        out_specs=(near,) * 2,
        name="sweep_second",
    )(keep(swept), keep(two), keep(one))
    one, two = swap(window, "col", False), swap(window, "col", True)
    inner = pl.pallas_call(
        third_kernel,
        out_shape=here(5, nx * ny, nz),
        in_specs=[near] * 2,
        out_specs=near,
        name="sweep_third",
    )(keep(after), keep(swept))
    out = pl.pallas_call(
        functools.partial(edge_kernel, "col", cols),
        out_shape=jax.ShapeDtypeStruct((5, nx * ny, nz), jnp.float32),
        in_specs=[near] * 4,
        out_specs=pl.BlockSpec(memory_space=pltpu.HBM),
        scratch_shapes=[
            pltpu.VMEM((5, nx * ny, nz), jnp.float32),
            pltpu.SemaphoreType.DMA((5,)),
        ],
        name="third_edges",
    )(keep(inner), keep(window), keep(one), keep(two))
    return out.reshape(5, nx, ny, nz)


def solution(mesh):
    in_specs = (P(None, None, "row", "col"), P(None, "row", "col"))
    out_specs = P(None, None, "row", "col")
    return jax.shard_map(
        functools.partial(body, mesh),
        mesh=mesh,
        in_specs=in_specs,
        out_specs=out_specs,
        check_vma=False,
    )
```

```python
import functools

import jax
import jax.numpy as jnp
from jax import lax
from jax.experimental import pallas as pl
from jax.experimental.pallas import tpu as pltpu
from jax.sharding import PartitionSpec as P

STEP = 0.08
HALO = 3
SUB, LANES = 8, 128
GROUP = LANES // SUB


def recip(x):
    r = pl.reciprocal(x, approx=True)
    return r * (2.0 - x * r)


def clamp_zero(u, v):
    return jnp.maximum(jnp.minimum(u, jnp.maximum(v, 0.0)), jnp.minimum(v, 0.0))


def primitives(cons, gam1, normal):
    rho, m0, m1, m2, energy = cons
    inv = recip(rho)
    vel = [m0 * inv, m1 * inv, m2 * inv]
    kinetic = 0.5 * (m0 * vel[0] + m1 * vel[1] + m2 * vel[2])
    pressure = gam1 * (energy - kinetic)
    others = [c for c in range(3) if c != normal]
    return [rho, vel[normal], vel[others[0]], vel[others[1]], pressure]


def face_rise(before, here, after):
    if here is None:
        return None
    rise = 0.5 * here
    if before is not None and after is not None:
        rise = rise + (before - after) * (1.0 / 12.0)
    elif before is not None:
        rise = rise + before * (1.0 / 12.0)
    elif after is not None:
        rise = rise - after * (1.0 / 12.0)
    return clamp_zero(rise, here)


def edges(q, right, left):
    if right is None or left is None:
        return q, q
    return q + clamp_zero(right, 2.0 * left), q - clamp_zero(left, 2.0 * right)


def state_flux(prim, gamma, inv_gam1):
    rho, un, u1, u2, p = prim
    mn, m1, m2 = rho * un, rho * u1, rho * u2
    nn = mn * un
    energy = p * inv_gam1 + 0.5 * (nn + m1 * u1 + m2 * u2)
    flux = [mn, nn + p, mn * u1, mn * u2, un * (energy + p)]
    gp = gamma * p
    speed = jnp.abs(un) + gp * lax.rsqrt(jnp.maximum(gp * rho, 1e-30))
    return [rho, mn, m1, m2, energy], flux, speed


def double_flux(left, right):
    if left is right:
        return [f + f for f in left[1]]
    speed = jnp.maximum(left[2], right[2])
    return [
        (left[1][k] + right[1][k]) - speed * (right[0][k] - left[0][k]) for k in range(5)
    ]


def place(normal):
    others = [c for c in range(3) if c != normal]
    return [0, 1 + normal, 1 + others[0], 1 + others[1], 4]


def updated(cons, flux_right, flux_left, normal):
    out = list(cons)
    for k, field in enumerate(place(normal)):
        out[field] = cons[field] - (0.5 * STEP) * (flux_right[k] - flux_left[k])
    return out


class Sweep:
    def __init__(self, n, normal, load, load_gamma, halo=None):
        self.n, self.normal = n, normal
        self.load, self.load_gamma, self.halo = load, load_gamma, halo
        self.cons, self.gam, self.prim, self.diff, self.rise, self.state = {}, {}, {}, {}, {}, {}

    def zone(self, i):
        return i if self.halo else min(max(i, 0), self.n - 1)

    def get_gam(self, i):
        i = self.zone(i)
        if i not in self.gam:
            gamma = self.load_gamma(i)
            gam1 = gamma - 1.0
            self.gam[i] = (gamma, recip(gam1), gam1)
        return self.gam[i]

    def get_cons(self, i):
        if i not in self.cons:
            self.cons[i] = self.load(i)
        return self.cons[i]

    def get(self, i):
        i = self.zone(i)
        if i not in self.prim:
            if 0 <= i < self.n:
                self.prim[i] = primitives(self.get_cons(i), self.get_gam(i)[2], self.normal)
            else:
                self.prim[i] = self.halo(i)
        return self.prim[i]

    def get_diff(self, i):
        if i not in self.diff:
            a, b = self.get(i), self.get(i + 1)
            self.diff[i] = [None] * 5 if a is b else [y - x for x, y in zip(a, b)]
        return self.diff[i]

    def get_rise(self, i):
        if i not in self.rise:
            here = self.get_diff(i)
            right = [face_rise(*t) for t in zip(self.get_diff(i - 1), here, self.get_diff(i + 1))]
            self.rise[i] = (right, [None if r is None else h - r for h, r in zip(here, right)])
        return self.rise[i]

    def get_state(self, i, upper):
        i = self.zone(i)
        if (i, upper) not in self.state:
            q, right, left = self.get(i), self.get_rise(i)[0], self.get_rise(i - 1)[1]
            pairs = [edges(*t) for t in zip(q, right, left)]
            side = [p[0] if upper else p[1] for p in pairs]
            self.state[i, upper] = state_flux(side, *self.get_gam(i)[:2])
            if all(p[0] is p[1] for p in pairs):
                self.state[i, not upper] = self.state[i, upper]
        return self.state[i, upper]

    def face(self, i):
        if not self.halo and i < 0:
            return double_flux(self.get_state(0, True), self.get_state(0, True))
        if not self.halo and i == self.n - 1:
            return double_flux(self.get_state(i, True), self.get_state(i, True))
        return double_flux(self.get_state(i, True), self.get_state(i + 1, False))

    def run(self, zones, store, flux=None):
        flux = self.face(zones[0] - 1) if flux is None else flux
        for i in zones:
            before, flux = flux, self.face(i)
            store(i, updated(self.get_cons(i), flux, before, self.normal))
        return flux


def own_row(y):
    odd = lax.rem(lax.axis_index("row"), 2) == 1
    return jnp.where(odd, SUB - 1 - y, y)


def own_sign():
    return jnp.where(lax.rem(lax.axis_index("row"), 2) == 1, -1.0, 1.0)


def rows_at(y, base, nx):
    return pl.ds(pl.multiple_of(own_row(y) * nx + base, SUB), SUB)


def first_kernel(state_ref, gamma_ref, swept_ref, one_ref, two_ref):
    nx, ny = gamma_ref.shape[0], gamma_ref.shape[1]

    def store(x, cons):
        for f in range(5):
            swept_ref[f, pl.ds(x, ny, stride=nx), :] = cons[f]

    sweep = Sweep(nx, 0, lambda x: [state_ref[f, x] for f in range(5)], lambda x: gamma_ref[x])
    sweep.run(range(nx), store)
    for x in range(nx):
        swept_ref[5, pl.ds(x, ny, stride=nx), :] = gamma_ref[x]
    for base in range(0, nx, SUB):
        at = pl.ds(base, SUB)
        for out_ref, nearest in ((one_ref, range(ny - 1, ny - 1 - HALO, -1)), (two_ref, range(HALO))):
            for j, y in enumerate(nearest):
                row = rows_at(y, base, nx)
                gamma = swept_ref[5, row, :]
                prim = primitives([swept_ref[f, row, :] for f in range(5)], gamma - 1.0, 1)
                for k in range(5):
                    out_ref[HALO * k + j, at, :] = prim[k]
                if j == 0:
                    out_ref[5 * HALO, at, :] = gamma


def row_loads(swept_ref, base, nx, sign):
    def load(y):
        row = rows_at(y, base, nx)
        cons = [swept_ref[f, row, :] for f in range(5)]
        cons[2] = cons[2] * sign
        return cons

    return load, lambda y: swept_ref[5, rows_at(y, base, nx), :]


def into_window(window, y, value):
    turn = (GROUP * y + 6) % LANES
    rolled = pltpu.roll(value, turn, 1) if turn else value
    if window is None:
        return rolled
    group = lax.broadcasted_iota(jnp.int32, (SUB, LANES), 1) // GROUP
    return jnp.where(group == y, rolled, window)


SPLIT = 5


def kept_arrays(sweep, flux):
    cons, fluxes, speed = sweep.get_state(SPLIT, True)
    kept = [sweep.get(SPLIT + 1), sweep.get(SPLIT + 2), sweep.get_diff(SPLIT)]
    return sum(kept + [sweep.get_rise(SPLIT)[1], cons, fluxes, [speed], flux], [])


KEPT = 36


def second_near(rows, swept_ref, two_ref, next_ref, window_ref, kept_ref):
    nx = swept_ref.shape[1] // SUB
    row = lax.axis_index("row")
    end = (row == 0) | (row == rows - 1)
    sign = own_sign()
    for base in range(0, nx, SUB):
        at = pl.ds(base, SUB)
        load, load_own_gamma = row_loads(swept_ref, base, nx, sign)
        windows = [None] * 6

        def load_gamma(y):
            if y >= 0:
                return load_own_gamma(y)
            return jnp.where(end, load_own_gamma(0), two_ref[5 * HALO, at, :])

        def halo(y):
            got = [two_ref[HALO * k - 1 - y, at, :] for k in range(5)]
            got[1] = got[1] * sign
            return [jnp.where(end, p, q) for p, q in zip(sweep.get(0), got)]

        def store(y, cons):
            cons[2] = cons[2] * sign
            for f in range(5):
                next_ref[f, pl.ds(y * nx + base, SUB), :] = cons[f]
                windows[f] = into_window(windows[f], y, cons[f])

        sweep = Sweep(SUB, 1, load, load_gamma, halo)
        flux = sweep.run(range(SPLIT), store)
        for y in range(SUB):
            windows[5] = into_window(windows[5], y, load_own_gamma(y))
        for f in range(6):
            window_ref[f, at, :] = windows[f]
        kept = kept_arrays(sweep, flux)
        assert len(kept) == KEPT
        for k in range(KEPT):
            kept_ref[k, at, :] = kept[k]


def second_far(swept_ref, one_ref, part_ref, kept_ref, next_ref, window_ref):
    nx = swept_ref.shape[1] // SUB
    sign = own_sign()
    for base in range(0, nx, SUB):
        at = pl.ds(base, SUB)
        load, load_own_gamma = row_loads(swept_ref, base, nx, sign)
        windows = [part_ref[f, at, :] for f in range(6)]

        def load_gamma(y):
            return load_own_gamma(y) if y < SUB else one_ref[5 * HALO, at, :]

        def halo(y):
            got = [one_ref[HALO * k + y - SUB, at, :] for k in range(5)]
            got[1] = got[1] * sign
            return got

        def store(y, cons):
            cons[2] = cons[2] * sign
            for f in range(5):
                next_ref[f, pl.ds((y - SPLIT) * nx + base, SUB), :] = cons[f]
                windows[f] = into_window(windows[f], y, cons[f])

        kept = [kept_ref[k, at, :] for k in range(KEPT)]
        sweep = Sweep(SUB, 1, load, load_gamma, halo)
        sweep.prim[SPLIT + 1], sweep.prim[SPLIT + 2] = kept[0:5], kept[5:10]
        sweep.diff[SPLIT] = kept[10:15]
        sweep.rise[SPLIT] = (None, kept[15:20])
        sweep.state[SPLIT, True] = (kept[20:25], kept[25:30], kept[30])
        sweep.run(range(SPLIT, SUB), store, kept[31:36])
        for f in range(6):
            window_ref[f, at, :] = windows[f]


def sweep_lanes(cons, gamma, normal):
    def ahead(x):
        return pltpu.roll(x, LANES - 1, 1)

    def behind(x):
        return pltpu.roll(x, 1, 1)

    gam1 = gamma - 1.0
    inv_gam1 = recip(gam1)
    prim = primitives(cons, gam1, normal)
    upper, lower_next = [], []
    for q in prim:
        here = ahead(q) - q
        right = face_rise(behind(here), here, ahead(here))
        left = behind(here - right)
        up, low = edges(q, right, left)
        upper.append(up)
        lower_next.append(ahead(low))
    flux = double_flux(
        state_flux(upper, gamma, inv_gam1),
        state_flux(lower_next, ahead(gamma), ahead(inv_gam1)),
    )
    return updated(cons, flux, [behind(x) for x in flux], normal)


def sweep_window(cons, gamma, normal):
    def turned(x, by):
        return pltpu.roll(x, (LANES - by) % LANES, 1) if by else x

    gam1 = gamma - 1.0
    gam = {k: (turned(gamma, k), turned(recip(gam1), k)) for k in range(-1, 2)}
    states = {key: [] for key in ((-1, 0), (0, 1), (0, 0), (1, 1))}
    for q in primitives(cons, gam1, normal):
        line = {k: turned(q, k) for k in range(-3, 4)}
        diff = {k: line[k + 1] - line[k] for k in range(-3, 3)}
        rise = {k: face_rise(diff[k - 1], diff[k], diff[k + 1]) for k in range(-2, 2)}
        for k, which in states:
            right, left = rise[k], diff[k - 1] - rise[k - 1]
            if which == k + 1:
                states[k, which].append(line[k] + clamp_zero(right, 2.0 * left))
            else:
                states[k, which].append(line[k] - clamp_zero(left, 2.0 * right))
    side = {key: state_flux(prim, *gam[key[0]]) for key, prim in states.items()}
    before = double_flux(side[-1, 0], side[0, 0])
    after = double_flux(side[0, 1], side[1, 1])
    return updated(cons, after, before, normal)


def third_kernel(
    col_axis, cols, near_ref, far_ref, gamma_ref, window_ref, out_ref, left_ref, right_ref
):
    ny = SUB
    nx = window_ref.shape[1]
    col = lax.axis_index(col_axis)
    slot = lax.broadcasted_iota(jnp.int32, (SUB, LANES), 1) % GROUP
    at_first = (slot >= jnp.where(col == 0, 3, GROUP)) & (slot <= 5)
    at_last = (slot >= jnp.where(col == cols - 1, 6, GROUP)) & (slot <= 8)
    for tile in range(nx // SUB):
        base = tile * SUB
        rows = pl.ds(base, SUB)
        for f in range(6):
            own = window_ref[f, rows, :]
            turned = [pltpu.roll(own, by % LANES, 1) for by in (-3, -2, -1, 1, 2, 3)]
            low = jnp.where(slot == 3, turned[0], jnp.where(slot == 4, turned[1], turned[2]))
            high = jnp.where(slot == 6, turned[3], jnp.where(slot == 7, turned[4], turned[5]))
            left_ref[f, rows, :] = jnp.where(at_first, low, own)
            right_ref[f, rows, :] = jnp.where(at_last, high, own)
        for y in range(ny):
            rows_ref, start = (near_ref, y) if y < SPLIT else (far_ref, y - SPLIT)
            cons = [rows_ref[f, pl.ds(start * nx + base, SUB), :] for f in range(5)]
            inner = sweep_lanes(cons, gamma_ref[5, rows_at(y, base, nx), :], 2)
            for f in range(5):
                out_ref[f, pl.ds(base * ny + own_row(y), SUB, stride=ny), :] = inner[f]


def edge_kernel(
    col_axis, cols, inner_ref, left_ref, right_ref, one_ref, two_ref, out_ref, held, sems
):
    nx = left_ref.shape[1]
    ny = SUB
    col = lax.axis_index(col_axis)
    odd = lax.rem(col, 2) == 1
    lane = lax.broadcasted_iota(jnp.int32, (SUB, LANES), 1)
    slot = lane % GROUP
    at_edge = (lane < HALO) | (lane >= LANES - HALO)
    at_left = (slot >= jnp.where(col == 0, GROUP, 3)) & (slot <= 5)
    at_right = (slot >= jnp.where(col == cols - 1, GROUP, 6)) & (slot <= 8)
    edge_new = []
    for tile in range(nx // SUB):
        rows = pl.ds(tile * SUB, SUB)
        left_window, right_window = [], []
        for f in range(6):
            one, two = one_ref[f, rows, :], two_ref[f, rows, :]
            before = jnp.where(odd, one, two)
            after = jnp.where(odd, two, one)
            left_window.append(jnp.where(at_left, before, left_ref[f, rows, :]))
            right_window.append(jnp.where(at_right, after, right_ref[f, rows, :]))
        left_new = sweep_window(left_window[:5], left_window[5], 2)
        right_new = sweep_window(right_window[:5], right_window[5], 2)
        edge_new.append([jnp.where(slot >= 6, a, b) for a, b in zip(left_new, right_new)])
    copies = []
    for f in range(5):
        for tile in range(nx // SUB):
            for y in range(ny):
                turn = (LANES - 6 - GROUP * y) % LANES
                edge = pltpu.roll(edge_new[tile][f], turn, 1)
                at = pl.ds(tile * SUB * ny + own_row(y), SUB, stride=ny)
                held[f, at, :] = jnp.where(at_edge, edge, inner_ref[f, at, :])
        copy = pltpu.make_async_copy(held.at[f], out_ref.at[f], sems.at[f])
        copy.start()
        copies.append(copy)
    for copy in copies:
        copy.wait()


def swap_pairs(mesh, axis, inner):
    rows, cols = mesh.shape["row"], mesh.shape["col"]
    pairs = []
    for r in range(rows):
        for c in range(cols):
            k, n = (r, rows) if axis == "row" else (c, cols)
            if not inner:
                k ^= 1
            elif 0 < k < n - 1:
                k = ((k - 1) ^ 1) + 1
            else:
                k = None
            if axis == "row":
                to = (r, c ^ 1) if k is None else (k, c)
            else:
                to = (r, cols - 1 - c) if k is None else (r, k)
            pairs.append((r * cols + c, to[0] * cols + to[1]))
    return pairs


def body(mesh, state, gamma):
    rows, cols = mesh.shape["row"], mesh.shape["col"]
    _, nx, ny, nz = state.shape
    assert ny == SUB and nz == LANES and nx % SUB == 0 and rows % 2 == 0 and cols % 2 == 0
    here = lambda *dims: pltpu.VMEM(dims, jnp.float32)
    keep = lambda x: pltpu.with_memory_space_constraint(x, pltpu.VMEM)
    near = pl.BlockSpec(memory_space=pltpu.VMEM)
    swap = lambda x, axis, inner: lax.ppermute(x, ("row", "col"), swap_pairs(mesh, axis, inner))

    swept, one, two = pl.pallas_call(
        first_kernel,
        out_shape=(
            here(6, ny * nx, nz),
            here(5 * HALO + 1, nx, nz),
            here(5 * HALO + 1, nx, nz),
        ),
        out_specs=(near,) * 3,
        name="sweep_first",
    )(state, gamma)
    two = swap(two, "row", True)
    one = swap(one, "row", False)
    near_rows, window, kept = pl.pallas_call(
        functools.partial(second_near, rows),
        out_shape=(here(5, SPLIT * nx, nz), here(6, nx, nz), here(KEPT, nx, nz)),
        in_specs=[near] * 2,
        out_specs=(near,) * 3,
        name="second_near",
    )(keep(swept), keep(two))
    far_rows, window = pl.pallas_call(
        second_far,
        out_shape=(here(5, (ny - SPLIT) * nx, nz), here(6, nx, nz)),
        in_specs=[near] * 4,
        out_specs=(near,) * 2,
        name="second_far",
    )(keep(swept), keep(one), keep(window), keep(kept))
    one, two = swap(window, "col", False), swap(window, "col", True)
    inner, left, right = pl.pallas_call(
        functools.partial(third_kernel, "col", cols),
        out_shape=(here(5, nx * ny, nz), here(6, nx, nz), here(6, nx, nz)),
        in_specs=[near] * 4,
        out_specs=(near,) * 3,
        name="sweep_third",
    )(keep(near_rows), keep(far_rows), keep(swept), keep(window))
    out = pl.pallas_call(
        functools.partial(edge_kernel, "col", cols),
        out_shape=jax.ShapeDtypeStruct((5, nx * ny, nz), jnp.float32),
        in_specs=[near] * 5,
        out_specs=pl.BlockSpec(memory_space=pltpu.HBM),
        scratch_shapes=[
            pltpu.VMEM((5, nx * ny, nz), jnp.float32),
            pltpu.SemaphoreType.DMA((5,)),
        ],
        name="third_edges",
    )(keep(inner), keep(left), keep(right), keep(one), keep(two))
    return out.reshape(5, nx, ny, nz)


def solution(mesh):
    in_specs = (P(None, None, "row", "col"), P(None, "row", "col"))
    out_specs = P(None, None, "row", "col")
    return jax.shard_map(
        functools.partial(body, mesh),
        mesh=mesh,
        in_specs=in_specs,
        out_specs=out_specs,
        check_vma=False,
    )
```

```python
import functools

import jax
import jax.numpy as jnp
from jax import lax
from jax.experimental import pallas as pl
from jax.experimental.pallas import tpu as pltpu
from jax.sharding import PartitionSpec as P

STEP = 0.08
HALO = 3
SUB, LANES = 8, 128
GROUP = LANES // SUB


def recip(x):
    r = pl.reciprocal(x, approx=True)
    return r * (2.0 - x * r)


def clamp_zero(u, v):
    return jnp.maximum(jnp.minimum(u, jnp.maximum(v, 0.0)), jnp.minimum(v, 0.0))


def primitives(cons, gam1, normal):
    rho, m0, m1, m2, energy = cons
    inv = recip(rho)
    vel = [m0 * inv, m1 * inv, m2 * inv]
    kinetic = 0.5 * (m0 * vel[0] + m1 * vel[1] + m2 * vel[2])
    pressure = gam1 * (energy - kinetic)
    others = [c for c in range(3) if c != normal]
    return [rho, vel[normal], vel[others[0]], vel[others[1]], pressure]


def face_rise(before, here, after):
    if here is None:
        return None
    rise = 0.5 * here
    if before is not None and after is not None:
        rise = rise + (before - after) * (1.0 / 12.0)
    elif before is not None:
        rise = rise + before * (1.0 / 12.0)
    elif after is not None:
        rise = rise - after * (1.0 / 12.0)
    return clamp_zero(rise, here)


def edges(q, right, left):
    if right is None or left is None:
        return q, q
    return q + clamp_zero(right, 2.0 * left), q - clamp_zero(left, 2.0 * right)


def state_flux(prim, gamma, inv_gam1):
    rho, un, u1, u2, p = prim
    mn, m1, m2 = rho * un, rho * u1, rho * u2
    nn = mn * un
    energy = p * inv_gam1 + 0.5 * (nn + m1 * u1 + m2 * u2)
    flux = [mn, nn + p, mn * u1, mn * u2, un * (energy + p)]
    gp = gamma * p
    speed = jnp.abs(un) + gp * lax.rsqrt(jnp.maximum(gp * rho, 1e-30))
    return [rho, mn, m1, m2, energy], flux, speed


def double_flux(left, right):
    if left is right:
        return [f + f for f in left[1]]
    speed = jnp.maximum(left[2], right[2])
    return [
        (left[1][k] + right[1][k]) - speed * (right[0][k] - left[0][k]) for k in range(5)
    ]


def place(normal):
    others = [c for c in range(3) if c != normal]
    return [0, 1 + normal, 1 + others[0], 1 + others[1], 4]


def updated(cons, flux_right, flux_left, normal):
    out = list(cons)
    for k, field in enumerate(place(normal)):
        out[field] = cons[field] - (0.5 * STEP) * (flux_right[k] - flux_left[k])
    return out


class Sweep:
    def __init__(self, n, normal, load, load_gamma, halo=None):
        self.n, self.normal = n, normal
        self.load, self.load_gamma, self.halo = load, load_gamma, halo
        self.cons, self.gam, self.prim, self.diff, self.rise, self.state = {}, {}, {}, {}, {}, {}

    def zone(self, i):
        return i if self.halo else min(max(i, 0), self.n - 1)

    def get_gam(self, i):
        i = self.zone(i)
        if i not in self.gam:
            gamma = self.load_gamma(i)
            gam1 = gamma - 1.0
            self.gam[i] = (gamma, recip(gam1), gam1)
        return self.gam[i]

    def get_cons(self, i):
        if i not in self.cons:
            self.cons[i] = self.load(i)
        return self.cons[i]

    def get(self, i):
        i = self.zone(i)
        if i not in self.prim:
            if 0 <= i < self.n:
                self.prim[i] = primitives(self.get_cons(i), self.get_gam(i)[2], self.normal)
            else:
                self.prim[i] = self.halo(i)
        return self.prim[i]

    def get_diff(self, i):
        if i not in self.diff:
            a, b = self.get(i), self.get(i + 1)
            self.diff[i] = [None] * 5 if a is b else [y - x for x, y in zip(a, b)]
        return self.diff[i]

    def get_rise(self, i):
        if i not in self.rise:
            here = self.get_diff(i)
            right = [face_rise(*t) for t in zip(self.get_diff(i - 1), here, self.get_diff(i + 1))]
            self.rise[i] = (right, [None if r is None else h - r for h, r in zip(here, right)])
        return self.rise[i]

    def get_state(self, i, upper):
        i = self.zone(i)
        if (i, upper) not in self.state:
            q, right, left = self.get(i), self.get_rise(i)[0], self.get_rise(i - 1)[1]
            pairs = [edges(*t) for t in zip(q, right, left)]
            side = [p[0] if upper else p[1] for p in pairs]
            self.state[i, upper] = state_flux(side, *self.get_gam(i)[:2])
            if all(p[0] is p[1] for p in pairs):
                self.state[i, not upper] = self.state[i, upper]
        return self.state[i, upper]

    def face(self, i):
        if not self.halo and i < 0:
            return double_flux(self.get_state(0, True), self.get_state(0, True))
        if not self.halo and i == self.n - 1:
            return double_flux(self.get_state(i, True), self.get_state(i, True))
        return double_flux(self.get_state(i, True), self.get_state(i + 1, False))

    def run(self, zones, store, flux=None):
        flux = self.face(zones[0] - 1) if flux is None else flux
        for i in zones:
            before, flux = flux, self.face(i)
            store(i, updated(self.get_cons(i), flux, before, self.normal))
        return flux


def own_row(y):
    odd = lax.rem(lax.axis_index("row"), 2) == 1
    return jnp.where(odd, SUB - 1 - y, y)


def own_sign():
    return jnp.where(lax.rem(lax.axis_index("row"), 2) == 1, -1.0, 1.0)


def rows_at(y, base, nx):
    return pl.ds(pl.multiple_of(own_row(y) * nx + base, SUB), SUB)


def first_kernel(state_ref, gamma_ref, swept_ref, one_ref, two_ref):
    nx, ny = gamma_ref.shape[0], gamma_ref.shape[1]

    def store(x, cons):
        for f in range(5):
            swept_ref[f, pl.ds(x, ny, stride=nx), :] = cons[f]

    sweep = Sweep(nx, 0, lambda x: [state_ref[f, x] for f in range(5)], lambda x: gamma_ref[x])
    sweep.run(range(nx), store)
    for x in range(nx):
        swept_ref[5, pl.ds(x, ny, stride=nx), :] = gamma_ref[x]
    for base in range(0, nx, SUB):
        at = pl.ds(base, SUB)
        for out_ref, nearest in ((one_ref, range(ny - 1, ny - 1 - HALO, -1)), (two_ref, range(HALO))):
            for j, y in enumerate(nearest):
                row = rows_at(y, base, nx)
                gamma = swept_ref[5, row, :]
                prim = primitives([swept_ref[f, row, :] for f in range(5)], gamma - 1.0, 1)
                for k in range(5):
                    out_ref[HALO * k + j, at, :] = prim[k]
                if j == 0:
                    out_ref[5 * HALO, at, :] = gamma


def row_loads(swept_ref, base, nx, sign):
    def load(y):
        row = rows_at(y, base, nx)
        cons = [swept_ref[f, row, :] for f in range(5)]
        cons[2] = cons[2] * sign
        return cons

    return load, lambda y: swept_ref[5, rows_at(y, base, nx), :]


def into_window(window, y, value):
    turn = (GROUP * y + 6) % LANES
    rolled = pltpu.roll(value, turn, 1) if turn else value
    if window is None:
        return rolled
    group = lax.broadcasted_iota(jnp.int32, (SUB, LANES), 1) // GROUP
    return jnp.where(group == y, rolled, window)


class EdgePack:
    def __init__(self, lower=None, upper=None):
        self.pack = [lower, upper]

    def add(self, y, cons, gamma):
        prim = primitives(cons, gamma - 1.0, 2)
        lane = lax.broadcasted_iota(jnp.int32, (SUB, LANES), 1)
        rolls = [turned(p, -(GROUP * y + 3 * k + 3)) for k, p in enumerate(prim)]
        for side in range(2):
            place = (lane + LANES - 3 * (1 - side)) % LANES
            slot, group = place % GROUP, place // GROUP
            value = turned(gamma, -(GROUP * y + (16 if side else 18)))
            for k in reversed(range(5)):
                value = jnp.where(slot < 3 * (k + 1), rolls[k], value)
            old = self.pack[side]
            self.pack[side] = value if old is None else jnp.where(group == y, value, old)


SPLIT = 5


def kept_arrays(sweep, flux):
    cons, fluxes, speed = sweep.get_state(SPLIT, True)
    kept = [sweep.get(SPLIT + 1), sweep.get(SPLIT + 2), sweep.get_diff(SPLIT)]
    return sum(kept + [sweep.get_rise(SPLIT)[1], cons, fluxes, [speed], flux], [])


KEPT = 36


def second_near(rows, swept_ref, two_ref, next_ref, lower_ref, upper_ref, kept_ref):
    nx = swept_ref.shape[1] // SUB
    row = lax.axis_index("row")
    end = (row == 0) | (row == rows - 1)
    sign = own_sign()
    for base in range(0, nx, SUB):
        at = pl.ds(base, SUB)
        load, load_own_gamma = row_loads(swept_ref, base, nx, sign)
        pack = EdgePack()

        def load_gamma(y):
            if y >= 0:
                return load_own_gamma(y)
            return jnp.where(end, load_own_gamma(0), two_ref[5 * HALO, at, :])

        def halo(y):
            got = [two_ref[HALO * k - 1 - y, at, :] for k in range(5)]
            got[1] = got[1] * sign
            return [jnp.where(end, p, q) for p, q in zip(sweep.get(0), got)]

        def store(y, cons):
            cons[2] = cons[2] * sign
            for f in range(5):
                next_ref[f, pl.ds(y * nx + base, SUB), :] = cons[f]
            pack.add(y, cons, load_own_gamma(y))

        sweep = Sweep(SUB, 1, load, load_gamma, halo)
        flux = sweep.run(range(SPLIT), store)
        lower_ref[at, :], upper_ref[at, :] = pack.pack
        kept = kept_arrays(sweep, flux)
        assert len(kept) == KEPT
        for k in range(KEPT):
            kept_ref[k, at, :] = kept[k]


def second_far(
    swept_ref, one_ref, lower_ref, upper_ref, kept_ref, next_ref, to_one_ref, to_two_ref
):
    nx = swept_ref.shape[1] // SUB
    sign = own_sign()
    for base in range(0, nx, SUB):
        at = pl.ds(base, SUB)
        load, load_own_gamma = row_loads(swept_ref, base, nx, sign)
        pack = EdgePack(lower_ref[at, :], upper_ref[at, :])

        def load_gamma(y):
            return load_own_gamma(y) if y < SUB else one_ref[5 * HALO, at, :]

        def halo(y):
            got = [one_ref[HALO * k + y - SUB, at, :] for k in range(5)]
            got[1] = got[1] * sign
            return got

        def store(y, cons):
            cons[2] = cons[2] * sign
            for f in range(5):
                next_ref[f, pl.ds((y - SPLIT) * nx + base, SUB), :] = cons[f]
            pack.add(y, cons, load_own_gamma(y))

        kept = [kept_ref[k, at, :] for k in range(KEPT)]
        sweep = Sweep(SUB, 1, load, load_gamma, halo)
        sweep.prim[SPLIT + 1], sweep.prim[SPLIT + 2] = kept[0:5], kept[5:10]
        sweep.diff[SPLIT] = kept[10:15]
        sweep.rise[SPLIT] = (None, kept[15:20])
        sweep.state[SPLIT, True] = (kept[20:25], kept[25:30], kept[30])
        sweep.run(range(SPLIT, SUB), store, kept[31:36])
        lower, upper = pack.pack
        odd = lax.rem(lax.axis_index("col"), 2) == 1
        to_one_ref[at, :] = jnp.where(odd, lower, upper)
        to_two_ref[at, :] = jnp.where(odd, upper, lower)


def sweep_lanes(cons, prim, gamma, normal):
    def ahead(x):
        return pltpu.roll(x, LANES - 1, 1)

    def behind(x):
        return pltpu.roll(x, 1, 1)

    inv_gam1 = recip(gamma - 1.0)
    upper, lower_next = [], []
    for q in prim:
        here = ahead(q) - q
        right = face_rise(behind(here), here, ahead(here))
        left = behind(here - right)
        up, low = edges(q, right, left)
        upper.append(up)
        lower_next.append(ahead(low))
    flux = double_flux(
        state_flux(upper, gamma, inv_gam1),
        state_flux(lower_next, ahead(gamma), ahead(inv_gam1)),
    )
    return updated(cons, flux, [behind(x) for x in flux], normal)


def sweep_lines(cons, lines, gammas, normal):
    gam = {k: (g, recip(g - 1.0)) for k, g in gammas.items()}
    states = {key: [] for key in ((-1, 0), (0, 1), (0, 0), (1, 1))}
    for line in lines:
        diff = {k: line[k + 1] - line[k] for k in range(-3, 3)}
        rise = {k: face_rise(diff[k - 1], diff[k], diff[k + 1]) for k in range(-2, 2)}
        for k, which in states:
            right, left = rise[k], diff[k - 1] - rise[k - 1]
            if which == k + 1:
                states[k, which].append(line[k] + clamp_zero(right, 2.0 * left))
            else:
                states[k, which].append(line[k] - clamp_zero(left, 2.0 * right))
    side = {key: state_flux(prim, *gam[key[0]]) for key, prim in states.items()}
    before = double_flux(side[-1, 0], side[0, 0])
    after = double_flux(side[0, 1], side[1, 1])
    return updated(cons, after, before, normal)


def turned(x, by):
    by %= LANES
    return pltpu.roll(x, LANES - by, 1) if by else x


REACH = range(-HALO, HALO + 1)
LINES = 5 * len(REACH)
EDGE_ARRAYS = LINES + 3 + 5


def beyond(slot, k, cols):
    col = lax.axis_index("col")
    if k < 0:
        return (slot >= 6) & (slot < 6 - k), col == 0
    return (slot >= 6 - k) & (slot < 6), col == cols - 1


def third_kernel(cols, near_ref, far_ref, gamma_ref, out_ref, edge_ref):
    ny = SUB
    nx = edge_ref.shape[1]
    slot = lax.broadcasted_iota(jnp.int32, (SUB, LANES), 1) % GROUP
    for base in range(0, nx, SUB):
        windows = [None] * 11
        for y in range(ny):
            rows_ref, start = (near_ref, y) if y < SPLIT else (far_ref, y - SPLIT)
            cons = [rows_ref[f, pl.ds(start * nx + base, SUB), :] for f in range(5)]
            gamma = gamma_ref[5, rows_at(y, base, nx), :]
            prim = primitives(cons, gamma - 1.0, 2)
            for k, value in enumerate(prim + [gamma] + cons):
                windows[k] = into_window(windows[k], y, value)
            inner = sweep_lanes(cons, prim, gamma, 2)
            for f in range(5):
                out_ref[f, pl.ds(base * ny + own_row(y), SUB, stride=ny), :] = inner[f]
        at = pl.ds(base, SUB)
        for q, own in enumerate(windows[:6]):
            line = {k: turned(own, k) for k in (REACH if q < 5 else (-1, 0, 1))}
            for n, k in enumerate(line):
                value = line[k]
                if k:
                    where, end = beyond(slot, k, cols)
                    if abs(k) == 1:
                        last = own
                    elif k < 0:
                        last = jnp.where(slot == 6, own, jnp.where(slot == 7, line[-1], line[-2]))
                    else:
                        last = jnp.where(slot == 5, own, jnp.where(slot == 4, line[1], line[2]))
                    value = jnp.where(where & end, last, value)
                edge_ref[len(REACH) * q + n, at, :] = value
        for f in range(5):
            edge_ref[LINES + 3 + f, at, :] = windows[6 + f]


def edge_kernel(cols, inner_ref, edge_ref, one_ref, two_ref, out_ref, held, sems):
    nx = edge_ref.shape[1]
    ny = SUB
    odd = lax.rem(lax.axis_index("col"), 2) == 1
    lane = lax.broadcasted_iota(jnp.int32, (SUB, LANES), 1)
    slot = lane % GROUP
    at_edge = (lane < HALO) | (lane >= LANES - HALO)
    edge_new = []
    for base in range(0, nx, SUB):
        at = pl.ds(base, SUB)
        one, two = one_ref[at, :], two_ref[at, :]
        lower, upper = jnp.where(odd, one, two), jnp.where(odd, two, one)

        def joined(index, k, lane_by):
            own = edge_ref[index, at, :]
            if not k:
                return own
            where, end = beyond(slot, k, cols)
            got = turned(lower if k < 0 else upper, lane_by)
            return jnp.where(where & jnp.logical_not(end), got, own)

        lines = [
            {k: joined(len(REACH) * q + n, k, 3 * q + k - 3) for n, k in enumerate(REACH)}
            for q in range(5)
        ]
        gammas = {-1: joined(LINES, -1, 9), 0: joined(LINES + 1, 0, 0), 1: joined(LINES + 2, 1, 13)}
        cons = [edge_ref[LINES + 3 + f, at, :] for f in range(5)]
        edge_new.append(sweep_lines(cons, lines, gammas, 2))
    copies = []
    for f in range(5):
        for tile, new in enumerate(edge_new):
            for y in range(ny):
                edge = turned(new[f], GROUP * y + 6)
                at = pl.ds(tile * SUB * ny + own_row(y), SUB, stride=ny)
                held[f, at, :] = jnp.where(at_edge, edge, inner_ref[f, at, :])
        copy = pltpu.make_async_copy(held.at[f], out_ref.at[f], sems.at[f])
        copy.start()
        copies.append(copy)
    for copy in copies:
        copy.wait()


def swap_pairs(mesh, axis, inner):
    rows, cols = mesh.shape["row"], mesh.shape["col"]
    pairs = []
    for r in range(rows):
        for c in range(cols):
            k, n = (r, rows) if axis == "row" else (c, cols)
            if not inner:
                k ^= 1
            elif 0 < k < n - 1:
                k = ((k - 1) ^ 1) + 1
            else:
                k = None
            if axis == "row":
                to = (r, c ^ 1) if k is None else (k, c)
            else:
                to = (r, cols - 1 - c) if k is None else (r, k)
            pairs.append((r * cols + c, to[0] * cols + to[1]))
    return pairs


def body(mesh, state, gamma):
    rows, cols = mesh.shape["row"], mesh.shape["col"]
    _, nx, ny, nz = state.shape
    assert ny == SUB and nz == LANES and nx % SUB == 0 and rows % 2 == 0 and cols % 2 == 0
    here = lambda *dims: pltpu.VMEM(dims, jnp.float32)
    keep = lambda x: pltpu.with_memory_space_constraint(x, pltpu.VMEM)
    near = pl.BlockSpec(memory_space=pltpu.VMEM)
    swap = lambda x, axis, inner: lax.ppermute(x, ("row", "col"), swap_pairs(mesh, axis, inner))

    swept, one, two = pl.pallas_call(
        first_kernel,
        out_shape=(
            here(6, ny * nx, nz),
            here(5 * HALO + 1, nx, nz),
            here(5 * HALO + 1, nx, nz),
        ),
        out_specs=(near,) * 3,
        name="sweep_first",
    )(state, gamma)
    two = swap(two, "row", True)
    one = swap(one, "row", False)
    near_rows, lower, upper, kept = pl.pallas_call(
        functools.partial(second_near, rows),
        out_shape=(here(5, SPLIT * nx, nz), here(nx, nz), here(nx, nz), here(KEPT, nx, nz)),
        in_specs=[near] * 2,
        out_specs=(near,) * 4,
        name="second_near",
    )(keep(swept), keep(two))
    far_rows, one, two = pl.pallas_call(
        second_far,
        out_shape=(here(5, (ny - SPLIT) * nx, nz), here(nx, nz), here(nx, nz)),
        in_specs=[near] * 5,
        out_specs=(near,) * 3,
        name="second_far",
    )(keep(swept), keep(one), keep(lower), keep(upper), keep(kept))
    one, two = swap(one, "col", False), swap(two, "col", True)
    inner, edge = pl.pallas_call(
        functools.partial(third_kernel, cols),
        out_shape=(here(5, nx * ny, nz), here(EDGE_ARRAYS, nx, nz)),
        in_specs=[near] * 3,
        out_specs=(near,) * 2,
        name="sweep_third",
    )(keep(near_rows), keep(far_rows), keep(swept))
    out = pl.pallas_call(
        functools.partial(edge_kernel, cols),
        out_shape=jax.ShapeDtypeStruct((5, nx * ny, nz), jnp.float32),
        in_specs=[near] * 4,
        out_specs=pl.BlockSpec(memory_space=pltpu.HBM),
        scratch_shapes=[
            pltpu.VMEM((5, nx * ny, nz), jnp.float32),
            pltpu.SemaphoreType.DMA((5,)),
        ],
        name="third_edges",
    )(keep(inner), keep(edge), keep(one), keep(two))
    return out.reshape(5, nx, ny, nz)


def solution(mesh):
    in_specs = (P(None, None, "row", "col"), P(None, "row", "col"))
    out_specs = P(None, None, "row", "col")
    return jax.shard_map(
        functools.partial(body, mesh),
        mesh=mesh,
        in_specs=in_specs,
        out_specs=out_specs,
        check_vma=False,
    )
```

```python
import functools

import jax
import jax.numpy as jnp
from jax import lax
from jax.experimental import pallas as pl
from jax.experimental.pallas import tpu as pltpu
from jax.sharding import PartitionSpec as P

STEP = 0.08
HALO = 3
SUB, LANES = 8, 128
GROUP = LANES // SUB


def recip(x):
    r = pl.reciprocal(x, approx=True)
    return r * (2.0 - x * r)


def clamp_zero(u, v):
    return jnp.maximum(jnp.minimum(u, jnp.maximum(v, 0.0)), jnp.minimum(v, 0.0))


def primitives(cons, gam1, normal):
    rho, m0, m1, m2, energy = cons
    inv = recip(rho)
    vel = [m0 * inv, m1 * inv, m2 * inv]
    kinetic = 0.5 * (m0 * vel[0] + m1 * vel[1] + m2 * vel[2])
    pressure = gam1 * (energy - kinetic)
    others = [c for c in range(3) if c != normal]
    return [rho, vel[normal], vel[others[0]], vel[others[1]], pressure]


def face_rise(before, here, after):
    if here is None:
        return None
    rise = 0.5 * here
    if before is not None and after is not None:
        rise = rise + (before - after) * (1.0 / 12.0)
    elif before is not None:
        rise = rise + before * (1.0 / 12.0)
    elif after is not None:
        rise = rise - after * (1.0 / 12.0)
    return clamp_zero(rise, here)


def edges(q, right, left):
    if right is None or left is None:
        return q, q
    return q + clamp_zero(right, 2.0 * left), q - clamp_zero(left, 2.0 * right)


def state_flux(prim, gamma, inv_gam1):
    rho, un, u1, u2, p = prim
    mn, m1, m2 = rho * un, rho * u1, rho * u2
    nn = mn * un
    energy = p * inv_gam1 + 0.5 * (nn + m1 * u1 + m2 * u2)
    flux = [mn, nn + p, mn * u1, mn * u2, un * (energy + p)]
    gp = gamma * p
    speed = jnp.abs(un) + gp * lax.rsqrt(jnp.maximum(gp * rho, 1e-30))
    return [rho, mn, m1, m2, energy], flux, speed


def double_flux(left, right):
    if left is right:
        return [f + f for f in left[1]]
    speed = jnp.maximum(left[2], right[2])
    return [
        (left[1][k] + right[1][k]) - speed * (right[0][k] - left[0][k]) for k in range(5)
    ]


def place(normal):
    others = [c for c in range(3) if c != normal]
    return [0, 1 + normal, 1 + others[0], 1 + others[1], 4]


def updated(cons, flux_right, flux_left, normal):
    out = list(cons)
    for k, field in enumerate(place(normal)):
        out[field] = cons[field] - (0.5 * STEP) * (flux_right[k] - flux_left[k])
    return out


class Sweep:
    def __init__(self, n, normal, load, load_gamma, halo=None):
        self.n, self.normal = n, normal
        self.load, self.load_gamma, self.halo = load, load_gamma, halo
        self.cons, self.gam, self.prim, self.diff, self.rise, self.state = {}, {}, {}, {}, {}, {}

    def zone(self, i):
        return i if self.halo else min(max(i, 0), self.n - 1)

    def get_gam(self, i):
        i = self.zone(i)
        if i not in self.gam:
            gamma = self.load_gamma(i)
            gam1 = gamma - 1.0
            self.gam[i] = (gamma, recip(gam1), gam1)
        return self.gam[i]

    def get_cons(self, i):
        if i not in self.cons:
            self.cons[i] = self.load(i)
        return self.cons[i]

    def get(self, i):
        i = self.zone(i)
        if i not in self.prim:
            if 0 <= i < self.n:
                self.prim[i] = primitives(self.get_cons(i), self.get_gam(i)[2], self.normal)
            else:
                self.prim[i] = self.halo(i)
        return self.prim[i]

    def get_diff(self, i):
        if i not in self.diff:
            a, b = self.get(i), self.get(i + 1)
            self.diff[i] = [None] * 5 if a is b else [y - x for x, y in zip(a, b)]
        return self.diff[i]

    def get_rise(self, i):
        if i not in self.rise:
            here = self.get_diff(i)
            right = [face_rise(*t) for t in zip(self.get_diff(i - 1), here, self.get_diff(i + 1))]
            self.rise[i] = (right, [None if r is None else h - r for h, r in zip(here, right)])
        return self.rise[i]

    def get_state(self, i, upper):
        i = self.zone(i)
        if (i, upper) not in self.state:
            q, right, left = self.get(i), self.get_rise(i)[0], self.get_rise(i - 1)[1]
            pairs = [edges(*t) for t in zip(q, right, left)]
            side = [p[0] if upper else p[1] for p in pairs]
            self.state[i, upper] = state_flux(side, *self.get_gam(i)[:2])
            if all(p[0] is p[1] for p in pairs):
                self.state[i, not upper] = self.state[i, upper]
        return self.state[i, upper]

    def face(self, i):
        if not self.halo and i < 0:
            return double_flux(self.get_state(0, True), self.get_state(0, True))
        if not self.halo and i == self.n - 1:
            return double_flux(self.get_state(i, True), self.get_state(i, True))
        return double_flux(self.get_state(i, True), self.get_state(i + 1, False))

    def run(self, zones, store, flux=None):
        flux = self.face(zones[0] - 1) if flux is None else flux
        for i in zones:
            before, flux = flux, self.face(i)
            store(i, updated(self.get_cons(i), flux, before, self.normal))
        return flux


def own_row(y):
    odd = lax.rem(lax.axis_index("row"), 2) == 1
    return jnp.where(odd, SUB - 1 - y, y)


def own_sign():
    return jnp.where(lax.rem(lax.axis_index("row"), 2) == 1, -1.0, 1.0)


def rows_at(y, base, nx):
    return pl.ds(pl.multiple_of(own_row(y) * nx + base, SUB), SUB)


def first_kernel(state_ref, gamma_ref, swept_ref, one_ref, two_ref):
    nx, ny = gamma_ref.shape[0], gamma_ref.shape[1]

    def store(x, cons):
        for f in range(5):
            swept_ref[f, pl.ds(x, ny, stride=nx), :] = cons[f]

    sweep = Sweep(nx, 0, lambda x: [state_ref[f, x] for f in range(5)], lambda x: gamma_ref[x])
    sweep.run(range(nx), store)
    for x in range(nx):
        swept_ref[5, pl.ds(x, ny, stride=nx), :] = gamma_ref[x]
    for base in range(0, nx, SUB):
        at = pl.ds(base, SUB)
        for out_ref, nearest in ((one_ref, range(ny - 1, ny - 1 - HALO, -1)), (two_ref, range(HALO))):
            for j, y in enumerate(nearest):
                row = rows_at(y, base, nx)
                gamma = swept_ref[5, row, :]
                prim = primitives([swept_ref[f, row, :] for f in range(5)], gamma - 1.0, 1)
                for k in range(5):
                    out_ref[HALO * k + j, at, :] = prim[k]
                if j == 0:
                    out_ref[5 * HALO, at, :] = gamma


def row_loads(swept_ref, base, nx, sign):
    def load(y):
        row = rows_at(y, base, nx)
        cons = [swept_ref[f, row, :] for f in range(5)]
        cons[2] = cons[2] * sign
        return cons

    return load, lambda y: swept_ref[5, rows_at(y, base, nx), :]


def into_window(window, y, value):
    turn = (GROUP * y + 6) % LANES
    rolled = pltpu.roll(value, turn, 1) if turn else value
    if window is None:
        return rolled
    group = lax.broadcasted_iota(jnp.int32, (SUB, LANES), 1) // GROUP
    return jnp.where(group == y, rolled, window)


class EdgePack:
    def __init__(self, lower=None, upper=None):
        self.pack = [lower, upper]

    def add(self, y, cons, gamma):
        prim = primitives(cons, gamma - 1.0, 2)
        lane = lax.broadcasted_iota(jnp.int32, (SUB, LANES), 1)
        rolls = [turned(p, -(GROUP * y + 3 * k + 3)) for k, p in enumerate(prim)]
        for side in range(2):
            place = (lane + LANES - 3 * (1 - side)) % LANES
            slot, group = place % GROUP, place // GROUP
            value = turned(gamma, -(GROUP * y + (16 if side else 18)))
            for k in reversed(range(5)):
                value = jnp.where(slot < 3 * (k + 1), rolls[k], value)
            old = self.pack[side]
            self.pack[side] = value if old is None else jnp.where(group == y, value, old)


SPLIT = 5


def kept_arrays(sweep, flux):
    cons, fluxes, speed = sweep.get_state(SPLIT, True)
    kept = [sweep.get(SPLIT + 1), sweep.get(SPLIT + 2), sweep.get_diff(SPLIT)]
    return sum(kept + [sweep.get_rise(SPLIT)[1], cons, fluxes, [speed], flux], [])


KEPT = 36


def second_near(rows, swept_ref, two_ref, next_ref, lower_ref, upper_ref, kept_ref):
    nx = swept_ref.shape[1] // SUB
    row = lax.axis_index("row")
    end = (row == 0) | (row == rows - 1)
    sign = own_sign()
    for base in range(0, nx, SUB):
        at = pl.ds(base, SUB)
        load, load_own_gamma = row_loads(swept_ref, base, nx, sign)
        pack = EdgePack()

        def load_gamma(y):
            if y >= 0:
                return load_own_gamma(y)
            return jnp.where(end, load_own_gamma(0), two_ref[5 * HALO, at, :])

        def halo(y):
            got = [two_ref[HALO * k - 1 - y, at, :] for k in range(5)]
            got[1] = got[1] * sign
            return [jnp.where(end, p, q) for p, q in zip(sweep.get(0), got)]

        def store(y, cons):
            cons[2] = cons[2] * sign
            for f in range(5):
                next_ref[f, pl.ds(y * nx + base, SUB), :] = cons[f]
            pack.add(y, cons, load_own_gamma(y))

        sweep = Sweep(SUB, 1, load, load_gamma, halo)
        flux = sweep.run(range(SPLIT), store)
        lower_ref[at, :], upper_ref[at, :] = pack.pack
        kept = kept_arrays(sweep, flux)
        assert len(kept) == KEPT
        for k in range(KEPT):
            kept_ref[k, at, :] = kept[k]


def second_far(
    swept_ref, one_ref, lower_ref, upper_ref, kept_ref, next_ref, to_one_ref, to_two_ref
):
    nx = swept_ref.shape[1] // SUB
    sign = own_sign()
    for base in range(0, nx, SUB):
        at = pl.ds(base, SUB)
        load, load_own_gamma = row_loads(swept_ref, base, nx, sign)
        pack = EdgePack(lower_ref[at, :], upper_ref[at, :])

        def load_gamma(y):
            return load_own_gamma(y) if y < SUB else one_ref[5 * HALO, at, :]

        def halo(y):
            got = [one_ref[HALO * k + y - SUB, at, :] for k in range(5)]
            got[1] = got[1] * sign
            return got

        def store(y, cons):
            cons[2] = cons[2] * sign
            for f in range(5):
                next_ref[f, pl.ds((y - SPLIT) * nx + base, SUB), :] = cons[f]
            pack.add(y, cons, load_own_gamma(y))

        kept = [kept_ref[k, at, :] for k in range(KEPT)]
        sweep = Sweep(SUB, 1, load, load_gamma, halo)
        sweep.prim[SPLIT + 1], sweep.prim[SPLIT + 2] = kept[0:5], kept[5:10]
        sweep.diff[SPLIT] = kept[10:15]
        sweep.rise[SPLIT] = (None, kept[15:20])
        sweep.state[SPLIT, True] = (kept[20:25], kept[25:30], kept[30])
        sweep.run(range(SPLIT, SUB), store, kept[31:36])
        lower, upper = pack.pack
        odd = lax.rem(lax.axis_index("col"), 2) == 1
        to_one_ref[at, :] = jnp.where(odd, lower, upper)
        to_two_ref[at, :] = jnp.where(odd, upper, lower)


def sweep_lanes(cons, prim, gamma, normal):
    def ahead(x):
        return pltpu.roll(x, LANES - 1, 1)

    def behind(x):
        return pltpu.roll(x, 1, 1)

    inv_gam1 = recip(gamma - 1.0)
    upper, lower_next = [], []
    for q in prim:
        here = ahead(q) - q
        right = face_rise(behind(here), here, ahead(here))
        left = behind(here - right)
        up, low = edges(q, right, left)
        upper.append(up)
        lower_next.append(ahead(low))
    flux = double_flux(
        state_flux(upper, gamma, inv_gam1),
        state_flux(lower_next, ahead(gamma), ahead(inv_gam1)),
    )
    return updated(cons, flux, [behind(x) for x in flux], normal)


def sweep_lines(cons, lines, gammas, normal):
    gam = {k: (g, recip(g - 1.0)) for k, g in gammas.items()}
    states = {key: [] for key in ((-1, 0), (0, 1), (0, 0), (1, 1))}
    for line in lines:
        diff = {k: line[k + 1] - line[k] for k in range(-3, 3)}
        rise = {k: face_rise(diff[k - 1], diff[k], diff[k + 1]) for k in range(-2, 2)}
        for k, which in states:
            right, left = rise[k], diff[k - 1] - rise[k - 1]
            if which == k + 1:
                states[k, which].append(line[k] + clamp_zero(right, 2.0 * left))
            else:
                states[k, which].append(line[k] - clamp_zero(left, 2.0 * right))
    side = {key: state_flux(prim, *gam[key[0]]) for key, prim in states.items()}
    before = double_flux(side[-1, 0], side[0, 0])
    after = double_flux(side[0, 1], side[1, 1])
    return updated(cons, after, before, normal)


def turned(x, by):
    by %= LANES
    return pltpu.roll(x, LANES - by, 1) if by else x


REACH = range(-HALO, HALO + 1)
LINES = 5 * len(REACH)
EDGE_ARRAYS = LINES + 3 + 5


def beyond(slot, k, cols):
    col = lax.axis_index("col")
    if k < 0:
        return (slot >= 6) & (slot < 6 - k), col == 0
    return (slot >= 6 - k) & (slot < 6), col == cols - 1


def third_kernel(cols, near_ref, far_ref, gamma_ref, out_ref, edge_ref):
    ny = SUB
    nx = edge_ref.shape[1]
    slot = lax.broadcasted_iota(jnp.int32, (SUB, LANES), 1) % GROUP
    for base in range(0, nx, SUB):
        windows = [None] * 11
        for y in range(ny):
            rows_ref, start = (near_ref, y) if y < SPLIT else (far_ref, y - SPLIT)
            cons = [rows_ref[f, pl.ds(start * nx + base, SUB), :] for f in range(5)]
            gamma = gamma_ref[5, rows_at(y, base, nx), :]
            prim = primitives(cons, gamma - 1.0, 2)
            for k, value in enumerate(prim + [gamma] + cons):
                windows[k] = into_window(windows[k], y, value)
            inner = sweep_lanes(cons, prim, gamma, 2)
            for f in range(5):
                out_ref[f, pl.ds(base * ny + own_row(y), SUB, stride=ny), :] = inner[f]
        at = pl.ds(base, SUB)
        for q, own in enumerate(windows[:6]):
            line = {k: turned(own, k) for k in (REACH if q < 5 else (-1, 0, 1))}
            for n, k in enumerate(line):
                value = line[k]
                if k:
                    where, end = beyond(slot, k, cols)
                    if abs(k) == 1:
                        last = own
                    elif k < 0:
                        last = jnp.where(slot == 6, own, jnp.where(slot == 7, line[-1], line[-2]))
                    else:
                        last = jnp.where(slot == 5, own, jnp.where(slot == 4, line[1], line[2]))
                    value = jnp.where(where & end, last, value)
                edge_ref[len(REACH) * q + n, at, :] = value
        for f in range(5):
            edge_ref[LINES + 3 + f, at, :] = windows[6 + f]


def edge_kernel(cols, inner_ref, edge_ref, two_ref, one_ref, out_ref, held, sems):
    nx = edge_ref.shape[1]
    ny = SUB
    odd = lax.rem(lax.axis_index("col"), 2) == 1
    lane = lax.broadcasted_iota(jnp.int32, (SUB, LANES), 1)
    slot = lane % GROUP
    at_edge = (lane < HALO) | (lane >= LANES - HALO)
    edge_new = []
    for base in range(0, nx, SUB):
        at = pl.ds(base, SUB)
        one, two = one_ref[at, :], two_ref[at, :]
        lower, upper = jnp.where(odd, one, two), jnp.where(odd, two, one)

        def joined(index, k, lane_by):
            own = edge_ref[index, at, :]
            if not k:
                return own
            where, end = beyond(slot, k, cols)
            got = turned(lower if k < 0 else upper, lane_by)
            return jnp.where(where & jnp.logical_not(end), got, own)

        lines = [
            {k: joined(len(REACH) * q + n, k, 3 * q + k - 3) for n, k in enumerate(REACH)}
            for q in range(5)
        ]
        gammas = {-1: joined(LINES, -1, 9), 0: joined(LINES + 1, 0, 0), 1: joined(LINES + 2, 1, 13)}
        cons = [edge_ref[LINES + 3 + f, at, :] for f in range(5)]
        edge_new.append(sweep_lines(cons, lines, gammas, 2))
    copies = []
    for f in range(5):
        for tile, new in enumerate(edge_new):
            for y in range(ny):
                edge = turned(new[f], GROUP * y + 6)
                at = pl.ds(tile * SUB * ny + own_row(y), SUB, stride=ny)
                held[f, at, :] = jnp.where(at_edge, edge, inner_ref[f, at, :])
        copy = pltpu.make_async_copy(held.at[f], out_ref.at[f], sems.at[f])
        copy.start()
        copies.append(copy)
    for copy in copies:
        copy.wait()


def swap_pairs(mesh, axis, inner):
    rows, cols = mesh.shape["row"], mesh.shape["col"]
    pairs = []
    for r in range(rows):
        for c in range(cols):
            k, n = (r, rows) if axis == "row" else (c, cols)
            if not inner:
                k ^= 1
            elif 0 < k < n - 1:
                k = ((k - 1) ^ 1) + 1
            else:
                k = None
            if axis == "row":
                to = (r, c ^ 1) if k is None else (k, c)
            else:
                to = (r, cols - 1 - c) if k is None else (r, k)
            pairs.append((r * cols + c, to[0] * cols + to[1]))
    return pairs


def body(mesh, state, gamma):
    rows, cols = mesh.shape["row"], mesh.shape["col"]
    _, nx, ny, nz = state.shape
    assert ny == SUB and nz == LANES and nx % SUB == 0 and rows % 2 == 0 and cols % 2 == 0
    here = lambda *dims: pltpu.VMEM(dims, jnp.float32)
    keep = lambda x: pltpu.with_memory_space_constraint(x, pltpu.VMEM)
    near = pl.BlockSpec(memory_space=pltpu.VMEM)
    swap = lambda x, axis, inner: lax.ppermute(x, ("row", "col"), swap_pairs(mesh, axis, inner))

    swept, one, two = pl.pallas_call(
        first_kernel,
        out_shape=(
            here(6, ny * nx, nz),
            here(5 * HALO + 1, nx, nz),
            here(5 * HALO + 1, nx, nz),
        ),
        out_specs=(near,) * 3,
        name="sweep_first",
    )(state, gamma)
    two = swap(two, "row", True)
    one = swap(one, "row", False)
    near_rows, lower, upper, kept = pl.pallas_call(
        functools.partial(second_near, rows),
        out_shape=(here(5, SPLIT * nx, nz), here(nx, nz), here(nx, nz), here(KEPT, nx, nz)),
        in_specs=[near] * 2,
        out_specs=(near,) * 4,
        name="second_near",
    )(keep(swept), keep(two))
    far_rows, one, two = pl.pallas_call(
        second_far,
        out_shape=(here(5, (ny - SPLIT) * nx, nz), here(nx, nz), here(nx, nz)),
        in_specs=[near] * 5,
        out_specs=(near,) * 3,
        name="second_far",
    )(keep(swept), keep(one), keep(lower), keep(upper), keep(kept))
    two = swap(two, "col", True)
    one = swap(one, "col", False)
    inner, edge = pl.pallas_call(
        functools.partial(third_kernel, cols),
        out_shape=(here(5, nx * ny, nz), here(EDGE_ARRAYS, nx, nz)),
        in_specs=[near] * 3,
        out_specs=(near,) * 2,
        name="sweep_third",
    )(keep(near_rows), keep(far_rows), keep(swept))
    out = pl.pallas_call(
        functools.partial(edge_kernel, cols),
        out_shape=jax.ShapeDtypeStruct((5, nx * ny, nz), jnp.float32),
        in_specs=[near] * 4,
        out_specs=pl.BlockSpec(memory_space=pltpu.HBM),
        scratch_shapes=[
            pltpu.VMEM((5, nx * ny, nz), jnp.float32),
            pltpu.SemaphoreType.DMA((5,)),
        ],
        name="third_edges",
    )(keep(inner), keep(edge), keep(two), keep(one))
    return out.reshape(5, nx, ny, nz)


def solution(mesh):
    in_specs = (P(None, None, "row", "col"), P(None, "row", "col"))
    out_specs = P(None, None, "row", "col")
    return jax.shard_map(
        functools.partial(body, mesh),
        mesh=mesh,
        in_specs=in_specs,
        out_specs=out_specs,
        check_vma=False,
    )
```

```python
import functools

import jax
import jax.numpy as jnp
from jax import lax
from jax.experimental import pallas as pl
from jax.experimental.pallas import tpu as pltpu
from jax.sharding import PartitionSpec as P

STEP = 0.08
HALO = 3
SUB, LANES = 8, 128
GROUP_BITS = 4
GROUP = 1 << GROUP_BITS


def recip(x):
    r = pl.reciprocal(x, approx=True)
    return r * (2.0 - x * r)


def clamp_zero(u, v):
    return jnp.maximum(jnp.minimum(u, jnp.maximum(v, 0.0)), jnp.minimum(v, 0.0))


def primitives(cons, gam1, normal):
    rho, m0, m1, m2, energy = cons
    inv = recip(rho)
    vel = [m0 * inv, m1 * inv, m2 * inv]
    kinetic = 0.5 * (m0 * vel[0] + m1 * vel[1] + m2 * vel[2])
    pressure = gam1 * (energy - kinetic)
    others = [c for c in range(3) if c != normal]
    return [rho, vel[normal], vel[others[0]], vel[others[1]], pressure]


def face_rise(before, here, after):
    if here is None:
        return None
    rise = 0.5 * here
    if before is not None and after is not None:
        rise = rise + (before - after) * (1.0 / 12.0)
    elif before is not None:
        rise = rise + before * (1.0 / 12.0)
    elif after is not None:
        rise = rise - after * (1.0 / 12.0)
    return clamp_zero(rise, here)


def edges(q, right, left):
    if right is None or left is None:
        return q, q
    return q + clamp_zero(right, 2.0 * left), q - clamp_zero(left, 2.0 * right)


def state_flux(prim, gamma, inv_gam1):
    rho, un, u1, u2, p = prim
    mn, m1, m2 = rho * un, rho * u1, rho * u2
    nn = mn * un
    energy = p * inv_gam1 + 0.5 * (nn + m1 * u1 + m2 * u2)
    flux = [mn, nn + p, mn * u1, mn * u2, un * (energy + p)]
    gp = gamma * p
    speed = jnp.abs(un) + gp * lax.rsqrt(jnp.maximum(gp * rho, 1e-30))
    return [rho, mn, m1, m2, energy], flux, speed


def double_flux(left, right):
    if left is right:
        return [f + f for f in left[1]]
    speed = jnp.maximum(left[2], right[2])
    return [
        (left[1][k] + right[1][k]) - speed * (right[0][k] - left[0][k]) for k in range(5)
    ]


def place(normal):
    others = [c for c in range(3) if c != normal]
    return [0, 1 + normal, 1 + others[0], 1 + others[1], 4]


def updated(cons, flux_right, flux_left, normal):
    out = list(cons)
    for k, field in enumerate(place(normal)):
        out[field] = cons[field] - (0.5 * STEP) * (flux_right[k] - flux_left[k])
    return out


class Sweep:
    def __init__(self, n, normal, load, load_gamma, halo=None):
        self.n, self.normal = n, normal
        self.load, self.load_gamma, self.halo = load, load_gamma, halo
        self.cons, self.gam, self.prim, self.diff, self.rise, self.state = {}, {}, {}, {}, {}, {}

    def zone(self, i):
        return i if self.halo else min(max(i, 0), self.n - 1)

    def get_gam(self, i):
        i = self.zone(i)
        if i not in self.gam:
            gamma = self.load_gamma(i)
            gam1 = gamma - 1.0
            self.gam[i] = (gamma, recip(gam1), gam1)
        return self.gam[i]

    def get_cons(self, i):
        if i not in self.cons:
            self.cons[i] = self.load(i)
        return self.cons[i]

    def get(self, i):
        i = self.zone(i)
        if i not in self.prim:
            if 0 <= i < self.n:
                self.prim[i] = primitives(self.get_cons(i), self.get_gam(i)[2], self.normal)
            else:
                self.prim[i] = self.halo(i)
        return self.prim[i]

    def get_diff(self, i):
        if i not in self.diff:
            a, b = self.get(i), self.get(i + 1)
            self.diff[i] = [None] * 5 if a is b else [y - x for x, y in zip(a, b)]
        return self.diff[i]

    def get_rise(self, i):
        if i not in self.rise:
            here = self.get_diff(i)
            right = [face_rise(*t) for t in zip(self.get_diff(i - 1), here, self.get_diff(i + 1))]
            self.rise[i] = (right, [None if r is None else h - r for h, r in zip(here, right)])
        return self.rise[i]

    def get_state(self, i, upper):
        i = self.zone(i)
        if (i, upper) not in self.state:
            q, right, left = self.get(i), self.get_rise(i)[0], self.get_rise(i - 1)[1]
            pairs = [edges(*t) for t in zip(q, right, left)]
            side = [p[0] if upper else p[1] for p in pairs]
            self.state[i, upper] = state_flux(side, *self.get_gam(i)[:2])
            if all(p[0] is p[1] for p in pairs):
                self.state[i, not upper] = self.state[i, upper]
        return self.state[i, upper]

    def face(self, i):
        if not self.halo and i < 0:
            return double_flux(self.get_state(0, True), self.get_state(0, True))
        if not self.halo and i == self.n - 1:
            return double_flux(self.get_state(i, True), self.get_state(i, True))
        return double_flux(self.get_state(i, True), self.get_state(i + 1, False))

    def run(self, zones, store, flux=None):
        flux = self.face(zones[0] - 1) if flux is None else flux
        for i in zones:
            before, flux = flux, self.face(i)
            store(i, updated(self.get_cons(i), flux, before, self.normal))
        return flux


def own_row(y):
    odd = lax.rem(lax.axis_index("row"), 2) == 1
    return jnp.where(odd, SUB - 1 - y, y)


def own_sign():
    return jnp.where(lax.rem(lax.axis_index("row"), 2) == 1, -1.0, 1.0)


def rows_at(y, base, nx):
    return pl.ds(pl.multiple_of(own_row(y) * nx + base, SUB), SUB)


def first_kernel(state_hbm, gamma_hbm, swept_ref, one_ref, two_ref, state_ref, gamma_ref, sems):
    nx, ny = gamma_ref.shape[0], gamma_ref.shape[1]
    copies = [
        pltpu.make_async_copy(state_hbm.at[f], state_ref.at[f], sems.at[f]) for f in range(5)
    ]
    copies.append(pltpu.make_async_copy(gamma_hbm, gamma_ref, sems.at[5]))
    for f, copy in enumerate(copies):
        copy.start(priority=f % 2)
    for copy in copies:
        copy.wait()

    def store(x, cons):
        for f in range(5):
            swept_ref[f, pl.ds(x, ny, stride=nx), :] = cons[f]

    sweep = Sweep(nx, 0, lambda x: [state_ref[f, x] for f in range(5)], lambda x: gamma_ref[x])
    sweep.run(range(nx), store)
    for x in range(nx):
        swept_ref[5, pl.ds(x, ny, stride=nx), :] = gamma_ref[x]
    for base in range(0, nx, SUB):
        at = pl.ds(base, SUB)
        for out_ref, nearest in ((one_ref, range(ny - 1, ny - 1 - HALO, -1)), (two_ref, range(HALO))):
            for j, y in enumerate(nearest):
                row = rows_at(y, base, nx)
                gamma = swept_ref[5, row, :]
                prim = primitives([swept_ref[f, row, :] for f in range(5)], gamma - 1.0, 1)
                for k in range(5):
                    out_ref[HALO * k + j, at, :] = prim[k]
                if j == 0:
                    out_ref[5 * HALO, at, :] = gamma


def row_loads(swept_ref, base, nx, sign):
    def load(y):
        row = rows_at(y, base, nx)
        cons = [swept_ref[f, row, :] for f in range(5)]
        cons[2] = cons[2] * sign
        return cons

    return load, lambda y: swept_ref[5, rows_at(y, base, nx), :]


def lanes():
    return lax.broadcasted_iota(jnp.int32, (SUB, LANES), 1)


def groups(by=0):
    return ((lanes() - by) & (LANES - 1)) >> GROUP_BITS


def slots(by=0):
    return (lanes() - by) & (GROUP - 1)


def into_window(window, y, value):
    turn = (GROUP * y + 6) % LANES
    rolled = pltpu.roll(value, turn, 1) if turn else value
    if window is None:
        return rolled
    return jnp.where(groups() == y, rolled, window)


class EdgePack:
    def __init__(self, lower=None, upper=None):
        self.pack = [lower, upper]

    def add(self, y, cons, gamma):
        prim = primitives(cons, gamma - 1.0, 2)
        rolls = [turned(p, -(GROUP * y + 3 * k + 3)) for k, p in enumerate(prim)]
        for side in range(2):
            slot, group = slots(3 * (1 - side)), groups(3 * (1 - side))
            value = turned(gamma, -(GROUP * y + (16 if side else 18)))
            for k in reversed(range(5)):
                value = jnp.where(slot < 3 * (k + 1), rolls[k], value)
            old = self.pack[side]
            self.pack[side] = value if old is None else jnp.where(group == y, value, old)


SPLIT = 5


def kept_arrays(sweep, flux):
    cons, fluxes, speed = sweep.get_state(SPLIT, True)
    kept = [sweep.get(SPLIT + 1), sweep.get(SPLIT + 2), sweep.get_diff(SPLIT)]
    return sum(kept + [sweep.get_rise(SPLIT)[1], cons, fluxes, [speed], flux], [])


KEPT = 36


def second_near(rows, swept_ref, two_ref, next_ref, lower_ref, upper_ref, kept_ref):
    nx = swept_ref.shape[1] // SUB
    row = lax.axis_index("row")
    end = (row == 0) | (row == rows - 1)
    sign = own_sign()
    for base in range(0, nx, SUB):
        at = pl.ds(base, SUB)
        load, load_own_gamma = row_loads(swept_ref, base, nx, sign)
        pack = EdgePack()

        def load_gamma(y):
            if y >= 0:
                return load_own_gamma(y)
            return jnp.where(end, load_own_gamma(0), two_ref[5 * HALO, at, :])

        def halo(y):
            got = [two_ref[HALO * k - 1 - y, at, :] for k in range(5)]
            got[1] = got[1] * sign
            return [jnp.where(end, p, q) for p, q in zip(sweep.get(0), got)]

        def store(y, cons):
            cons[2] = cons[2] * sign
            for f in range(5):
                next_ref[f, pl.ds(y * nx + base, SUB), :] = cons[f]
            pack.add(y, cons, load_own_gamma(y))

        sweep = Sweep(SUB, 1, load, load_gamma, halo)
        flux = sweep.run(range(SPLIT), store)
        lower_ref[at, :], upper_ref[at, :] = pack.pack
        kept = kept_arrays(sweep, flux)
        assert len(kept) == KEPT
        for k in range(KEPT):
            kept_ref[k, at, :] = kept[k]


def second_far(
    swept_ref, one_ref, lower_ref, upper_ref, kept_ref, next_ref, to_one_ref, to_two_ref
):
    nx = swept_ref.shape[1] // SUB
    sign = own_sign()
    for base in range(0, nx, SUB):
        at = pl.ds(base, SUB)
        load, load_own_gamma = row_loads(swept_ref, base, nx, sign)
        pack = EdgePack(lower_ref[at, :], upper_ref[at, :])

        def load_gamma(y):
            return load_own_gamma(y) if y < SUB else one_ref[5 * HALO, at, :]

        def halo(y):
            got = [one_ref[HALO * k + y - SUB, at, :] for k in range(5)]
            got[1] = got[1] * sign
            return got

        def store(y, cons):
            cons[2] = cons[2] * sign
            for f in range(5):
                next_ref[f, pl.ds((y - SPLIT) * nx + base, SUB), :] = cons[f]
            pack.add(y, cons, load_own_gamma(y))

        kept = [kept_ref[k, at, :] for k in range(KEPT)]
        sweep = Sweep(SUB, 1, load, load_gamma, halo)
        sweep.prim[SPLIT + 1], sweep.prim[SPLIT + 2] = kept[0:5], kept[5:10]
        sweep.diff[SPLIT] = kept[10:15]
        sweep.rise[SPLIT] = (None, kept[15:20])
        sweep.state[SPLIT, True] = (kept[20:25], kept[25:30], kept[30])
        sweep.run(range(SPLIT, SUB), store, kept[31:36])
        lower, upper = pack.pack
        odd = lax.rem(lax.axis_index("col"), 2) == 1
        to_one_ref[at, :] = jnp.where(odd, lower, upper)
        to_two_ref[at, :] = jnp.where(odd, upper, lower)
        to_two_ref[pl.ds(nx + base, SUB), :] = lower


def sweep_lanes(cons, prim, gamma, normal):
    def ahead(x):
        return pltpu.roll(x, LANES - 1, 1)

    def behind(x):
        return pltpu.roll(x, 1, 1)

    inv_gam1 = recip(gamma - 1.0)
    upper, lower_next = [], []
    for q in prim:
        here = ahead(q) - q
        right = face_rise(behind(here), here, ahead(here))
        left = behind(here - right)
        up, low = edges(q, right, left)
        upper.append(up)
        lower_next.append(ahead(low))
    flux = double_flux(
        state_flux(upper, gamma, inv_gam1),
        state_flux(lower_next, ahead(gamma), ahead(inv_gam1)),
    )
    return updated(cons, flux, [behind(x) for x in flux], normal)


def sweep_lines(cons, lines, gammas, normal):
    gam = {k: (g, recip(g - 1.0)) for k, g in gammas.items()}
    states = {key: [] for key in ((-1, 0), (0, 1), (0, 0), (1, 1))}
    for line in lines:
        diff = {k: line[k + 1] - line[k] for k in range(-3, 3)}
        rise = {k: face_rise(diff[k - 1], diff[k], diff[k + 1]) for k in range(-2, 2)}
        for k, which in states:
            right, left = rise[k], diff[k - 1] - rise[k - 1]
            if which == k + 1:
                states[k, which].append(line[k] + clamp_zero(right, 2.0 * left))
            else:
                states[k, which].append(line[k] - clamp_zero(left, 2.0 * right))
    side = {key: state_flux(prim, *gam[key[0]]) for key, prim in states.items()}
    before = double_flux(side[-1, 0], side[0, 0])
    after = double_flux(side[0, 1], side[1, 1])
    return updated(cons, after, before, normal)


def turned(x, by):
    by %= LANES
    return pltpu.roll(x, LANES - by, 1) if by else x


REACH = range(-HALO, HALO + 1)
LINES = 5 * len(REACH)
EDGE_ARRAYS = LINES + 3 + 5


def beyond(slot, k, cols):
    col = lax.axis_index("col")
    if k < 0:
        return (slot >= 6) & (slot < 6 - k), col == 0
    return (slot >= 6 - k) & (slot < 6), col == cols - 1


def zone_loads(near_ref, far_ref, gamma_ref, base, nx):
    def load(y):
        rows_ref, start = (near_ref, y) if y < SPLIT else (far_ref, y - SPLIT)
        cons = [rows_ref[f, pl.ds(start * nx + base, SUB), :] for f in range(5)]
        gamma = gamma_ref[5, rows_at(y, base, nx), :]
        return cons, primitives(cons, gamma - 1.0, 2), gamma

    return load


def third_kernel(near_ref, far_ref, gamma_ref, out_ref):
    ny = SUB
    nx = out_ref.shape[1] // ny
    for base in range(0, nx, SUB):
        load = zone_loads(near_ref, far_ref, gamma_ref, base, nx)
        for y in range(ny):
            inner = sweep_lanes(*load(y), 2)
            for f in range(5):
                out_ref[f, pl.ds(base * ny + own_row(y), SUB, stride=ny), :] = inner[f]


def window_kernel(cols, near_ref, far_ref, gamma_ref, edge_ref):
    nx = edge_ref.shape[1]
    slot = slots()
    for base in range(0, nx, SUB):
        load = zone_loads(near_ref, far_ref, gamma_ref, base, nx)
        windows = [None] * 11
        for y in range(SUB):
            cons, prim, gamma = load(y)
            for k, value in enumerate(prim + [gamma] + cons):
                windows[k] = into_window(windows[k], y, value)
        at = pl.ds(base, SUB)
        for q, own in enumerate(windows[:6]):
            line = {k: turned(own, k) for k in (REACH if q < 5 else (-1, 0, 1))}
            for n, k in enumerate(line):
                value = line[k]
                if k:
                    where, end = beyond(slot, k, cols)
                    if abs(k) == 1:
                        last = own
                    elif k < 0:
                        last = jnp.where(slot == 6, own, jnp.where(slot == 7, line[-1], line[-2]))
                    else:
                        last = jnp.where(slot == 5, own, jnp.where(slot == 4, line[1], line[2]))
                    value = jnp.where(where & end, last, value)
                edge_ref[len(REACH) * q + n, at, :] = value
        for f in range(5):
            edge_ref[LINES + 3 + f, at, :] = windows[6 + f]


def mend_edges(cols, inner_ref, edge_ref, one_ref, two_ref, out_ref, held, sems):
    nx = edge_ref.shape[1]
    ny = SUB
    odd = lax.rem(lax.axis_index("col"), 2) == 1
    lane = lanes()
    slot = slots()
    at_edge = (lane < HALO) | (lane >= LANES - HALO)
    edge_new = []
    for base in range(0, nx, SUB):
        at = pl.ds(base, SUB)
        one, two = one_ref[at, :], two_ref[at, :]
        lower, upper = jnp.where(odd, one, two), jnp.where(odd, two, one)

        def joined(index, k, lane_by):
            own = edge_ref[index, at, :]
            if not k:
                return own
            where, end = beyond(slot, k, cols)
            got = turned(lower if k < 0 else upper, lane_by)
            return jnp.where(where & jnp.logical_not(end), got, own)

        lines = [
            {k: joined(len(REACH) * q + n, k, 3 * q + k - 3) for n, k in enumerate(REACH)}
            for q in range(5)
        ]
        gammas = {-1: joined(LINES, -1, 9), 0: joined(LINES + 1, 0, 0), 1: joined(LINES + 2, 1, 13)}
        cons = [edge_ref[LINES + 3 + f, at, :] for f in range(5)]
        edge_new.append(sweep_lines(cons, lines, gammas, 2))
    copies = []
    for f in range(5):
        for tile, new in enumerate(edge_new):
            for y in range(ny):
                edge = turned(new[f], GROUP * y + 6)
                at = pl.ds(tile * SUB * ny + own_row(y), SUB, stride=ny)
                held[f, at, :] = jnp.where(at_edge, edge, inner_ref[f, at, :])
        copy = pltpu.make_async_copy(held.at[f], out_ref.at[f], sems.at[f])
        copy.start(priority=f % 2)
        copies.append(copy)
    for copy in copies:
        copy.wait()


def at_end(cols):
    col = lax.axis_index("col")
    return (col == 0) | (col == cols - 1)


def end_kernel(cols, inner_ref, edge_ref, one_ref, out_ref, held, sems):
    @pl.when(at_end(cols))
    def _():
        mend_edges(cols, inner_ref, edge_ref, one_ref, one_ref, out_ref, held, sems)


def middle_kernel(cols, ends_ref, inner_ref, edge_ref, one_ref, two_ref, out_ref, held, sems):
    @pl.when(jnp.logical_not(at_end(cols)))
    def _():
        mend_edges(cols, inner_ref, edge_ref, one_ref, two_ref, out_ref, held, sems)


def swap_pairs(mesh, axis, inner):
    rows, cols = mesh.shape["row"], mesh.shape["col"]
    pairs = []
    for r in range(rows):
        for c in range(cols):
            k, n = (r, rows) if axis == "row" else (c, cols)
            if not inner:
                k ^= 1
            elif 0 < k < n - 1:
                k = ((k - 1) ^ 1) + 1
            else:
                k = None
            if axis == "row":
                to = (r, c ^ 1) if k is None else (k, c)
            else:
                to = (r, cols - 1 - c) if k is None else (r, k)
            pairs.append((r * cols + c, to[0] * cols + to[1]))
    return pairs


def body(mesh, state, gamma):
    rows, cols = mesh.shape["row"], mesh.shape["col"]
    _, nx, ny, nz = state.shape
    assert ny == SUB and nz == LANES and nx % SUB == 0 and rows % 2 == 0 and cols % 2 == 0
    here = lambda *dims: pltpu.VMEM(dims, jnp.float32)
    keep = lambda x: pltpu.with_memory_space_constraint(x, pltpu.VMEM)
    near = pl.BlockSpec(memory_space=pltpu.VMEM)
    swap = lambda x, axis, inner: lax.ppermute(x, ("row", "col"), swap_pairs(mesh, axis, inner))

    swept, one, two = pl.pallas_call(
        first_kernel,
        out_shape=(
            here(6, ny * nx, nz),
            here(5 * HALO + 1, nx, nz),
            here(5 * HALO + 1, nx, nz),
        ),
        in_specs=[pl.BlockSpec(memory_space=pltpu.HBM)] * 2,
        out_specs=(near,) * 3,
        scratch_shapes=[
            pltpu.VMEM(state.shape, jnp.float32),
            pltpu.VMEM(gamma.shape, jnp.float32),
            pltpu.SemaphoreType.DMA((6,)),
        ],
        name="sweep_first",
    )(state, gamma)
    two = swap(two, "row", True)
    one = swap(one, "row", False)
    near_rows, lower, upper, kept = pl.pallas_call(
        functools.partial(second_near, rows),
        out_shape=(here(5, SPLIT * nx, nz), here(nx, nz), here(nx, nz), here(KEPT, nx, nz)),
        in_specs=[near] * 2,
        out_specs=(near,) * 4,
        name="second_near",
    )(keep(swept), keep(two))
    far_rows, one, two = pl.pallas_call(
        second_far,
        out_shape=(here(5, (ny - SPLIT) * nx, nz), here(nx, nz), here(2 * nx, nz)),
        in_specs=[near] * 5,
        out_specs=(near,) * 3,
        name="second_far",
    )(keep(swept), keep(one), keep(lower), keep(upper), keep(kept))
    two = swap(two, "col", True)
    one = swap(one, "col", False)
    rows_in = (keep(near_rows), keep(far_rows), keep(swept))
    inner = pl.pallas_call(
        third_kernel,
        out_shape=here(5, nx * ny, nz),
        in_specs=[near] * 3,
        out_specs=near,
        name="sweep_third",
    )(*rows_in)
    edge = pl.pallas_call(
        functools.partial(window_kernel, cols),
        out_shape=here(EDGE_ARRAYS, nx, nz),
        in_specs=[near] * 3,
        out_specs=near,
        name="third_windows",
    )(*rows_in)
    far = pl.BlockSpec(memory_space=pltpu.HBM)
    whole = jax.ShapeDtypeStruct((5, nx * ny, nz), jnp.float32)
    scratch = [pltpu.VMEM(whole.shape, jnp.float32), pltpu.SemaphoreType.DMA((5,))]
    ends = pl.pallas_call(
        functools.partial(end_kernel, cols),
        out_shape=whole,
        in_specs=[near] * 3,
        out_specs=far,
        scratch_shapes=scratch,
        name="third_ends",
    )(keep(inner), keep(edge), keep(one))
    out = pl.pallas_call(
        functools.partial(middle_kernel, cols),
        out_shape=whole,
        in_specs=[far] + [near] * 4,
        out_specs=far,
        input_output_aliases={0: 0},
        scratch_shapes=scratch,
        name="third_middle",
    )(ends, keep(inner), keep(edge), keep(one), keep(two))
    return out.reshape(5, nx, ny, nz)


def solution(mesh):
    in_specs = (P(None, None, "row", "col"), P(None, "row", "col"))
    out_specs = P(None, None, "row", "col")
    return jax.shard_map(
        functools.partial(body, mesh),
        mesh=mesh,
        in_specs=in_specs,
        out_specs=out_specs,
        check_vma=False,
    )
```

```python
import functools

import jax
import jax.numpy as jnp
from jax import lax
from jax.experimental import pallas as pl
from jax.experimental.pallas import tpu as pltpu
from jax.sharding import PartitionSpec as P

STEP = 0.08
HALO = 3
SUB, LANES = 8, 128
GROUP_BITS = 4
GROUP = 1 << GROUP_BITS


def recip(x):
    r = pl.reciprocal(x, approx=True)
    return r * (2.0 - x * r)


def clamp_zero(u, v):
    return jnp.maximum(jnp.minimum(u, jnp.maximum(v, 0.0)), jnp.minimum(v, 0.0))


def primitives(cons, gam1, normal):
    rho, m0, m1, m2, energy = cons
    inv = recip(rho)
    vel = [m0 * inv, m1 * inv, m2 * inv]
    kinetic = 0.5 * (m0 * vel[0] + m1 * vel[1] + m2 * vel[2])
    pressure = gam1 * (energy - kinetic)
    others = [c for c in range(3) if c != normal]
    return [rho, vel[normal], vel[others[0]], vel[others[1]], pressure]


def face_rise(before, here, after):
    if here is None:
        return None
    rise = 0.5 * here
    if before is not None and after is not None:
        rise = rise + (before - after) * (1.0 / 12.0)
    elif before is not None:
        rise = rise + before * (1.0 / 12.0)
    elif after is not None:
        rise = rise - after * (1.0 / 12.0)
    return clamp_zero(rise, here)


def edges(q, right, left):
    if right is None or left is None:
        return q, q
    return q + clamp_zero(right, 2.0 * left), q - clamp_zero(left, 2.0 * right)


def state_flux(prim, gamma, inv_gam1):
    rho, un, u1, u2, p = prim
    mn, m1, m2 = rho * un, rho * u1, rho * u2
    nn = mn * un
    energy = p * inv_gam1 + 0.5 * (nn + m1 * u1 + m2 * u2)
    flux = [mn, nn + p, mn * u1, mn * u2, un * (energy + p)]
    gp = gamma * p
    speed = jnp.abs(un) + gp * lax.rsqrt(jnp.maximum(gp * rho, 1e-30))
    return [rho, mn, m1, m2, energy], flux, speed


def double_flux(left, right):
    if left is right:
        return [f + f for f in left[1]]
    speed = jnp.maximum(left[2], right[2])
    return [
        (left[1][k] + right[1][k]) - speed * (right[0][k] - left[0][k]) for k in range(5)
    ]


def place(normal):
    others = [c for c in range(3) if c != normal]
    return [0, 1 + normal, 1 + others[0], 1 + others[1], 4]


def updated(cons, flux_right, flux_left, normal):
    out = list(cons)
    for k, field in enumerate(place(normal)):
        out[field] = cons[field] - (0.5 * STEP) * (flux_right[k] - flux_left[k])
    return out


class Sweep:
    def __init__(self, n, normal, load, load_gamma, halo=None):
        self.n, self.normal = n, normal
        self.load, self.load_gamma, self.halo = load, load_gamma, halo
        self.cons, self.gam, self.prim, self.diff, self.rise, self.state = {}, {}, {}, {}, {}, {}

    def zone(self, i):
        return i if self.halo else min(max(i, 0), self.n - 1)

    def get_gam(self, i):
        i = self.zone(i)
        if i not in self.gam:
            gamma = self.load_gamma(i)
            gam1 = gamma - 1.0
            self.gam[i] = (gamma, recip(gam1), gam1)
        return self.gam[i]

    def get_cons(self, i):
        if i not in self.cons:
            self.cons[i] = self.load(i)
        return self.cons[i]

    def get(self, i):
        i = self.zone(i)
        if i not in self.prim:
            if 0 <= i < self.n:
                self.prim[i] = primitives(self.get_cons(i), self.get_gam(i)[2], self.normal)
            else:
                self.prim[i] = self.halo(i)
        return self.prim[i]

    def get_diff(self, i):
        if i not in self.diff:
            a, b = self.get(i), self.get(i + 1)
            self.diff[i] = [None] * 5 if a is b else [y - x for x, y in zip(a, b)]
        return self.diff[i]

    def get_rise(self, i):
        if i not in self.rise:
            here = self.get_diff(i)
            right = [face_rise(*t) for t in zip(self.get_diff(i - 1), here, self.get_diff(i + 1))]
            self.rise[i] = (right, [None if r is None else h - r for h, r in zip(here, right)])
        return self.rise[i]

    def get_state(self, i, upper):
        i = self.zone(i)
        if (i, upper) not in self.state:
            q, right, left = self.get(i), self.get_rise(i)[0], self.get_rise(i - 1)[1]
            pairs = [edges(*t) for t in zip(q, right, left)]
            side = [p[0] if upper else p[1] for p in pairs]
            self.state[i, upper] = state_flux(side, *self.get_gam(i)[:2])
            if all(p[0] is p[1] for p in pairs):
                self.state[i, not upper] = self.state[i, upper]
        return self.state[i, upper]

    def face(self, i):
        if not self.halo and i < 0:
            return double_flux(self.get_state(0, True), self.get_state(0, True))
        if not self.halo and i == self.n - 1:
            return double_flux(self.get_state(i, True), self.get_state(i, True))
        return double_flux(self.get_state(i, True), self.get_state(i + 1, False))

    def run(self, zones, store, flux=None):
        flux = self.face(zones[0] - 1) if flux is None else flux
        for i in zones:
            before, flux = flux, self.face(i)
            store(i, updated(self.get_cons(i), flux, before, self.normal))
        return flux


def own_row(y):
    odd = lax.rem(lax.axis_index("row"), 2) == 1
    return jnp.where(odd, SUB - 1 - y, y)


def own_sign():
    return jnp.where(lax.rem(lax.axis_index("row"), 2) == 1, -1.0, 1.0)


def rows_at(y, base, nx):
    return pl.ds(pl.multiple_of(own_row(y) * nx + base, SUB), SUB)


def shifted(tiles, by, edge):
    sub = lax.broadcasted_iota(jnp.int32, (SUB, LANES), 0)
    turned_tiles = [pltpu.roll(tile, SUB - 1 if by == 1 else 1, 0) for tile in tiles]
    if by == 1:
        beyond_tiles = turned_tiles[1:] + [edge]
        return [jnp.where(sub == SUB - 1, b, a) for a, b in zip(turned_tiles, beyond_tiles)]
    beyond_tiles = [edge] + turned_tiles[:-1]
    return [jnp.where(sub == 0, b, a) for a, b in zip(turned_tiles, beyond_tiles)]


def sweep_sublanes(cons, gamma):
    gam1 = [g - 1.0 for g in gamma]
    inv_gam1 = [recip(g) for g in gam1]
    prim = [primitives(c, g, 0) for c, g in zip(cons, gam1)]
    upper, lower_next = [], []
    for q in zip(*prim):
        here = [b - a for a, b in zip(q, shifted(q, 1, q[-1]))]
        right = [face_rise(*d) for d in zip(shifted(here, -1, 0.0), here, shifted(here, 1, 0.0))]
        left = shifted([h - r for h, r in zip(here, right)], -1, 0.0)
        pairs = [edges(*t) for t in zip(q, right, left)]
        upper.append([p[0] for p in pairs])
        lower_next.append(shifted([p[1] for p in pairs], 1, q[-1]))
    gamma_next, inv_next = shifted(gamma, 1, gamma[-1]), shifted(inv_gam1, 1, inv_gam1[-1])
    flux = [
        double_flux(state_flux(u, g, i), state_flux(l, gn, i_n))
        for u, l, g, i, gn, i_n in zip(
            zip(*upper), zip(*lower_next), gamma, inv_gam1, gamma_next, inv_next
        )
    ]
    start = state_flux(prim[0], gamma[0], inv_gam1[0])
    start = double_flux(start, start)
    before = [shifted(list(f), -1, e) for f, e in zip(zip(*flux), start)]
    return [updated(c, f, b, 0) for c, f, b in zip(cons, flux, zip(*before))]


def raw_kernel(state_hbm, gamma_hbm, two_ref, sems):
    copies = []
    for j in range(HALO):
        row = own_row(j)
        copies.append(
            pltpu.make_async_copy(
                state_hbm.at[:, :, row, :], two_ref.at[pl.ds(0, 5), j], sems.at[j, 0]
            )
        )
        copies.append(pltpu.make_async_copy(gamma_hbm.at[:, row, :], two_ref.at[5, j], sems.at[j, 1]))
    for k, copy in enumerate(copies):
        copy.start(priority=k % 2)
    for copy in copies:
        copy.wait()


def edge_rows_kernel(state_ref, gamma_ref, one_ref):
    nx, ny = one_ref.shape[1], SUB
    tiles = [pl.ds(base, SUB) for base in range(0, nx, SUB)]
    for j in range(HALO):
        row = own_row(ny - 1 - j)
        at = [pl.ds(base * ny + row, SUB, stride=ny) for base in range(0, nx, SUB)]
        gamma = [gamma_ref[rows, :] for rows in at]
        swept = sweep_sublanes([[state_ref[f, rows, :] for f in range(5)] for rows in at], gamma)
        for tile, cons, g in zip(tiles, swept, gamma):
            for k, value in enumerate(primitives(cons, g - 1.0, 1)):
                one_ref[HALO * k + j, tile, :] = value
            if j == 0:
                one_ref[5 * HALO, tile, :] = g


def first_kernel(state_ref, gamma_ref, swept_ref):
    ny = SUB
    nx = gamma_ref.shape[0] // ny

    def load_gamma(x):
        return gamma_ref[pl.ds(x * ny, ny), :]

    def store(x, cons):
        for f in range(5):
            swept_ref[f, pl.ds(x, ny, stride=nx), :] = cons[f]

    sweep = Sweep(
        nx, 0, lambda x: [state_ref[f, pl.ds(x * ny, ny), :] for f in range(5)], load_gamma
    )
    sweep.run(range(nx), store)
    for x in range(nx):
        swept_ref[5, pl.ds(x, ny, stride=nx), :] = load_gamma(x)


def row_loads(swept_ref, base, nx, sign):
    def load(y):
        row = rows_at(y, base, nx)
        cons = [swept_ref[f, row, :] for f in range(5)]
        cons[2] = cons[2] * sign
        return cons

    return load, lambda y: swept_ref[5, rows_at(y, base, nx), :]


def lanes():
    return lax.broadcasted_iota(jnp.int32, (SUB, LANES), 1)


def groups(by=0):
    return ((lanes() - by) & (LANES - 1)) >> GROUP_BITS


def slots(by=0):
    return (lanes() - by) & (GROUP - 1)


def into_window(window, y, value):
    turn = (GROUP * y + 6) % LANES
    rolled = pltpu.roll(value, turn, 1) if turn else value
    if window is None:
        return rolled
    return jnp.where(groups() == y, rolled, window)


class EdgePack:
    def __init__(self, lower=None, upper=None):
        self.pack = [lower, upper]

    def add(self, y, cons, gamma):
        prim = primitives(cons, gamma - 1.0, 2)
        rolls = [turned(p, -(GROUP * y + 3 * k + 3)) for k, p in enumerate(prim)]
        for side in range(2):
            slot, group = slots(3 * (1 - side)), groups(3 * (1 - side))
            value = turned(gamma, -(GROUP * y + (16 if side else 18)))
            for k in reversed(range(5)):
                value = jnp.where(slot < 3 * (k + 1), rolls[k], value)
            old = self.pack[side]
            self.pack[side] = value if old is None else jnp.where(group == y, value, old)


SPLIT = 5


def kept_arrays(sweep, flux):
    cons, fluxes, speed = sweep.get_state(SPLIT, True)
    kept = [sweep.get(SPLIT + 1), sweep.get(SPLIT + 2), sweep.get_diff(SPLIT)]
    return sum(kept + [sweep.get_rise(SPLIT)[1], cons, fluxes, [speed], flux], [])


KEPT = 36


def second_near(rows, swept_ref, two_ref, next_ref, lower_ref, upper_ref, kept_ref):
    nx = swept_ref.shape[1] // SUB
    row = lax.axis_index("row")
    end = (row == 0) | (row == rows - 1)
    sign = own_sign()
    tiles = [pl.ds(base, SUB) for base in range(0, nx, SUB)]
    halos = []
    for j in range(HALO):
        gamma = [two_ref[5 * HALO + j, tile, :] for tile in tiles]
        cons = [[two_ref[HALO * f + j, tile, :] for f in range(5)] for tile in tiles]
        swept = sweep_sublanes(cons, gamma)
        halos.append([primitives(c, g - 1.0, 1) for c, g in zip(swept, gamma)])
    for base in range(0, nx, SUB):
        at = pl.ds(base, SUB)
        load, load_own_gamma = row_loads(swept_ref, base, nx, sign)
        pack = EdgePack()

        def load_gamma(y):
            if y >= 0:
                return load_own_gamma(y)
            return jnp.where(end, load_own_gamma(0), two_ref[5 * HALO, at, :])

        def halo(y):
            got = list(halos[-1 - y][base // SUB])
            got[1] = got[1] * sign
            return [jnp.where(end, p, q) for p, q in zip(sweep.get(0), got)]

        def store(y, cons):
            cons[2] = cons[2] * sign
            for f in range(5):
                next_ref[f, pl.ds(y * nx + base, SUB), :] = cons[f]
            pack.add(y, cons, load_own_gamma(y))

        sweep = Sweep(SUB, 1, load, load_gamma, halo)
        flux = sweep.run(range(SPLIT), store)
        lower_ref[at, :], upper_ref[at, :] = pack.pack
        kept = kept_arrays(sweep, flux)
        assert len(kept) == KEPT
        for k in range(KEPT):
            kept_ref[k, at, :] = kept[k]


def second_far(
    swept_ref, one_ref, lower_ref, upper_ref, kept_ref, next_ref, to_one_ref, to_two_ref
):
    nx = swept_ref.shape[1] // SUB
    sign = own_sign()
    for base in range(0, nx, SUB):
        at = pl.ds(base, SUB)
        load, load_own_gamma = row_loads(swept_ref, base, nx, sign)
        pack = EdgePack(lower_ref[at, :], upper_ref[at, :])

        def load_gamma(y):
            return load_own_gamma(y) if y < SUB else one_ref[5 * HALO, at, :]

        def halo(y):
            got = [one_ref[HALO * k + y - SUB, at, :] for k in range(5)]
            got[1] = got[1] * sign
            return got

        def store(y, cons):
            cons[2] = cons[2] * sign
            for f in range(5):
                next_ref[f, pl.ds((y - SPLIT) * nx + base, SUB), :] = cons[f]
            pack.add(y, cons, load_own_gamma(y))

        kept = [kept_ref[k, at, :] for k in range(KEPT)]
        sweep = Sweep(SUB, 1, load, load_gamma, halo)
        sweep.prim[SPLIT + 1], sweep.prim[SPLIT + 2] = kept[0:5], kept[5:10]
        sweep.diff[SPLIT] = kept[10:15]
        sweep.rise[SPLIT] = (None, kept[15:20])
        sweep.state[SPLIT, True] = (kept[20:25], kept[25:30], kept[30])
        sweep.run(range(SPLIT, SUB), store, kept[31:36])
        lower, upper = pack.pack
        odd = lax.rem(lax.axis_index("col"), 2) == 1
        to_one_ref[at, :] = jnp.where(odd, lower, upper)
        to_two_ref[at, :] = jnp.where(odd, upper, lower)
        to_two_ref[pl.ds(nx + base, SUB), :] = lower


def sweep_lanes(cons, prim, gamma, normal):
    def ahead(x):
        return pltpu.roll(x, LANES - 1, 1)

    def behind(x):
        return pltpu.roll(x, 1, 1)

    inv_gam1 = recip(gamma - 1.0)
    upper, lower_next = [], []
    for q in prim:
        here = ahead(q) - q
        right = face_rise(behind(here), here, ahead(here))
        left = behind(here - right)
        up, low = edges(q, right, left)
        upper.append(up)
        lower_next.append(ahead(low))
    flux = double_flux(
        state_flux(upper, gamma, inv_gam1),
        state_flux(lower_next, ahead(gamma), ahead(inv_gam1)),
    )
    return updated(cons, flux, [behind(x) for x in flux], normal)


def sweep_lines(cons, lines, gammas, normal):
    gam = {k: (g, recip(g - 1.0)) for k, g in gammas.items()}
    states = {key: [] for key in ((-1, 0), (0, 1), (0, 0), (1, 1))}
    for line in lines:
        diff = {k: line[k + 1] - line[k] for k in range(-3, 3)}
        rise = {k: face_rise(diff[k - 1], diff[k], diff[k + 1]) for k in range(-2, 2)}
        for k, which in states:
            right, left = rise[k], diff[k - 1] - rise[k - 1]
            if which == k + 1:
                states[k, which].append(line[k] + clamp_zero(right, 2.0 * left))
            else:
                states[k, which].append(line[k] - clamp_zero(left, 2.0 * right))
    side = {key: state_flux(prim, *gam[key[0]]) for key, prim in states.items()}
    before = double_flux(side[-1, 0], side[0, 0])
    after = double_flux(side[0, 1], side[1, 1])
    return updated(cons, after, before, normal)


def turned(x, by):
    by %= LANES
    return pltpu.roll(x, LANES - by, 1) if by else x


REACH = range(-HALO, HALO + 1)
LINES = 5 * len(REACH)
EDGE_ARRAYS = LINES + 3 + 5


def beyond(slot, k, cols):
    col = lax.axis_index("col")
    if k < 0:
        return (slot >= 6) & (slot < 6 - k), col == 0
    return (slot >= 6 - k) & (slot < 6), col == cols - 1


def zone_loads(near_ref, far_ref, gamma_ref, base, nx):
    def load(y):
        rows_ref, start = (near_ref, y) if y < SPLIT else (far_ref, y - SPLIT)
        cons = [rows_ref[f, pl.ds(start * nx + base, SUB), :] for f in range(5)]
        gamma = gamma_ref[5, rows_at(y, base, nx), :]
        return cons, primitives(cons, gamma - 1.0, 2), gamma

    return load


def third_kernel(near_ref, far_ref, gamma_ref, out_ref):
    ny = SUB
    nx = out_ref.shape[1] // ny
    for base in range(0, nx, SUB):
        load = zone_loads(near_ref, far_ref, gamma_ref, base, nx)
        for y in range(ny):
            inner = sweep_lanes(*load(y), 2)
            for f in range(5):
                out_ref[f, pl.ds(base * ny + own_row(y), SUB, stride=ny), :] = inner[f]


def window_kernel(cols, near_ref, far_ref, gamma_ref, edge_ref):
    nx = edge_ref.shape[1]
    slot = slots()
    for base in range(0, nx, SUB):
        load = zone_loads(near_ref, far_ref, gamma_ref, base, nx)
        windows = [None] * 11
        for y in range(SUB):
            cons, prim, gamma = load(y)
            for k, value in enumerate(prim + [gamma] + cons):
                windows[k] = into_window(windows[k], y, value)
        at = pl.ds(base, SUB)
        for q, own in enumerate(windows[:6]):
            line = {k: turned(own, k) for k in (REACH if q < 5 else (-1, 0, 1))}
            for n, k in enumerate(line):
                value = line[k]
                if k:
                    where, end = beyond(slot, k, cols)
                    if abs(k) == 1:
                        last = own
                    elif k < 0:
                        last = jnp.where(slot == 6, own, jnp.where(slot == 7, line[-1], line[-2]))
                    else:
                        last = jnp.where(slot == 5, own, jnp.where(slot == 4, line[1], line[2]))
                    value = jnp.where(where & end, last, value)
                edge_ref[len(REACH) * q + n, at, :] = value
        for f in range(5):
            edge_ref[LINES + 3 + f, at, :] = windows[6 + f]


def mend_edges(cols, inner_ref, edge_ref, one_ref, two_ref, out_ref, held, sems):
    nx = edge_ref.shape[1]
    ny = SUB
    odd = lax.rem(lax.axis_index("col"), 2) == 1
    lane = lanes()
    slot = slots()
    at_edge = (lane < HALO) | (lane >= LANES - HALO)
    edge_new = []
    for base in range(0, nx, SUB):
        at = pl.ds(base, SUB)
        one, two = one_ref[at, :], two_ref[at, :]
        lower, upper = jnp.where(odd, one, two), jnp.where(odd, two, one)

        def joined(index, k, lane_by):
            own = edge_ref[index, at, :]
            if not k:
                return own
            where, end = beyond(slot, k, cols)
            got = turned(lower if k < 0 else upper, lane_by)
            return jnp.where(where & jnp.logical_not(end), got, own)

        lines = [
            {k: joined(len(REACH) * q + n, k, 3 * q + k - 3) for n, k in enumerate(REACH)}
            for q in range(5)
        ]
        gammas = {-1: joined(LINES, -1, 9), 0: joined(LINES + 1, 0, 0), 1: joined(LINES + 2, 1, 13)}
        cons = [edge_ref[LINES + 3 + f, at, :] for f in range(5)]
        edge_new.append(sweep_lines(cons, lines, gammas, 2))
    copies = []
    for f in range(5):
        for tile, new in enumerate(edge_new):
            for y in range(ny):
                edge = turned(new[f], GROUP * y + 6)
                at = pl.ds(tile * SUB * ny + own_row(y), SUB, stride=ny)
                held[f, at, :] = jnp.where(at_edge, edge, inner_ref[f, at, :])
        copy = pltpu.make_async_copy(held.at[f], out_ref.at[f], sems.at[f])
        copy.start(priority=f % 2)
        copies.append(copy)
    for copy in copies:
        copy.wait()


def at_end(cols):
    col = lax.axis_index("col")
    return (col == 0) | (col == cols - 1)


def end_kernel(cols, inner_ref, edge_ref, one_ref, out_ref, held, sems):
    @pl.when(at_end(cols))
    def _():
        mend_edges(cols, inner_ref, edge_ref, one_ref, one_ref, out_ref, held, sems)


def middle_kernel(cols, ends_ref, inner_ref, edge_ref, one_ref, two_ref, out_ref, held, sems):
    @pl.when(jnp.logical_not(at_end(cols)))
    def _():
        mend_edges(cols, inner_ref, edge_ref, one_ref, two_ref, out_ref, held, sems)


def swap_pairs(mesh, axis, inner):
    rows, cols = mesh.shape["row"], mesh.shape["col"]
    pairs = []
    for r in range(rows):
        for c in range(cols):
            k, n = (r, rows) if axis == "row" else (c, cols)
            if not inner:
                k ^= 1
            elif 0 < k < n - 1:
                k = ((k - 1) ^ 1) + 1
            else:
                k = None
            if axis == "row":
                to = (r, c ^ 1) if k is None else (k, c)
            else:
                to = (r, cols - 1 - c) if k is None else (r, k)
            pairs.append((r * cols + c, to[0] * cols + to[1]))
    return pairs


def body(mesh, state, gamma):
    rows, cols = mesh.shape["row"], mesh.shape["col"]
    _, nx, ny, nz = state.shape
    assert ny == SUB and nz == LANES and nx % SUB == 0 and rows % 2 == 0 and cols % 2 == 0
    here = lambda *dims: pltpu.VMEM(dims, jnp.float32)
    keep = lambda x: pltpu.with_memory_space_constraint(x, pltpu.VMEM)
    near = pl.BlockSpec(memory_space=pltpu.VMEM)
    swap = lambda x, axis, inner: lax.ppermute(x, ("row", "col"), swap_pairs(mesh, axis, inner))

    two = pl.pallas_call(
        raw_kernel,
        out_shape=here(6, HALO, nx, nz),
        in_specs=[pl.BlockSpec(memory_space=pltpu.HBM)] * 2,
        out_specs=near,
        scratch_shapes=[pltpu.SemaphoreType.DMA((HALO, 2))],
        name="raw_edges",
    )(state, gamma)
    two = swap(two, "row", True).reshape(6 * HALO, nx, nz)
    held = (keep(state.reshape(5, nx * ny, nz)), keep(gamma.reshape(nx * ny, nz)))
    one = pl.pallas_call(
        edge_rows_kernel,
        out_shape=here(5 * HALO + 1, nx, nz),
        in_specs=[near] * 2,
        out_specs=near,
        name="edge_rows",
    )(*held)
    swept = pl.pallas_call(
        first_kernel,
        out_shape=here(6, ny * nx, nz),
        in_specs=[near] * 2,
        out_specs=near,
        name="sweep_first",
    )(*held)
    one = swap(one, "row", False)
    near_rows, lower, upper, kept = pl.pallas_call(
        functools.partial(second_near, rows),
        out_shape=(here(5, SPLIT * nx, nz), here(nx, nz), here(nx, nz), here(KEPT, nx, nz)),
        in_specs=[near] * 2,
        out_specs=(near,) * 4,
        name="second_near",
    )(keep(swept), keep(two))
    far_rows, one, two = pl.pallas_call(
        second_far,
        out_shape=(here(5, (ny - SPLIT) * nx, nz), here(nx, nz), here(2 * nx, nz)),
        in_specs=[near] * 5,
        out_specs=(near,) * 3,
        name="second_far",
    )(keep(swept), keep(one), keep(lower), keep(upper), keep(kept))
    two = swap(two, "col", True)
    one = swap(one, "col", False)
    rows_in = (keep(near_rows), keep(far_rows), keep(swept))
    inner = pl.pallas_call(
        third_kernel,
        out_shape=here(5, nx * ny, nz),
        in_specs=[near] * 3,
        out_specs=near,
        name="sweep_third",
    )(*rows_in)
    edge = pl.pallas_call(
        functools.partial(window_kernel, cols),
        out_shape=here(EDGE_ARRAYS, nx, nz),
        in_specs=[near] * 3,
        out_specs=near,
        name="third_windows",
    )(*rows_in)
    far = pl.BlockSpec(memory_space=pltpu.HBM)
    whole = jax.ShapeDtypeStruct((5, nx * ny, nz), jnp.float32)
    scratch = [pltpu.VMEM(whole.shape, jnp.float32), pltpu.SemaphoreType.DMA((5,))]
    ends = pl.pallas_call(
        functools.partial(end_kernel, cols),
        out_shape=whole,
        in_specs=[near] * 3,
        out_specs=far,
        scratch_shapes=scratch,
        name="third_ends",
    )(keep(inner), keep(edge), keep(one))
    out = pl.pallas_call(
        functools.partial(middle_kernel, cols),
        out_shape=whole,
        in_specs=[far] + [near] * 4,
        out_specs=far,
        input_output_aliases={0: 0},
        scratch_shapes=scratch,
        name="third_middle",
    )(ends, keep(inner), keep(edge), keep(one), keep(two))
    return out.reshape(5, nx, ny, nz)


def solution(mesh):
    in_specs = (P(None, None, "row", "col"), P(None, "row", "col"))
    out_specs = P(None, None, "row", "col")
    return jax.shard_map(
        functools.partial(body, mesh),
        mesh=mesh,
        in_specs=in_specs,
        out_specs=out_specs,
        check_vma=False,
    )
```

```python
import functools

import jax
import jax.numpy as jnp
from jax import lax
from jax.experimental import pallas as pl
from jax.experimental.pallas import tpu as pltpu
from jax.sharding import PartitionSpec as P

STEP = 0.08
HALO = 3
SUB, LANES = 8, 128
GROUP_BITS = 4
GROUP = 1 << GROUP_BITS


def recip(x):
    r = pl.reciprocal(x, approx=True)
    return r * (2.0 - x * r)


def clamp_zero(u, v):
    return jnp.maximum(jnp.minimum(u, jnp.maximum(v, 0.0)), jnp.minimum(v, 0.0))


def primitives(cons, gam1, normal):
    rho, m0, m1, m2, energy = cons
    inv = recip(rho)
    vel = [m0 * inv, m1 * inv, m2 * inv]
    kinetic = 0.5 * (m0 * vel[0] + m1 * vel[1] + m2 * vel[2])
    pressure = gam1 * (energy - kinetic)
    others = [c for c in range(3) if c != normal]
    return [rho, vel[normal], vel[others[0]], vel[others[1]], pressure]


def face_rise(before, here, after):
    if here is None:
        return None
    rise = 0.5 * here
    if before is not None and after is not None:
        rise = rise + (before - after) * (1.0 / 12.0)
    elif before is not None:
        rise = rise + before * (1.0 / 12.0)
    elif after is not None:
        rise = rise - after * (1.0 / 12.0)
    return clamp_zero(rise, here)


def edges(q, right, left):
    if right is None or left is None:
        return q, q
    return q + clamp_zero(right, 2.0 * left), q - clamp_zero(left, 2.0 * right)


def state_flux(prim, gamma, inv_gam1):
    rho, un, u1, u2, p = prim
    mn, m1, m2 = rho * un, rho * u1, rho * u2
    nn = mn * un
    energy = p * inv_gam1 + 0.5 * (nn + m1 * u1 + m2 * u2)
    flux = [mn, nn + p, mn * u1, mn * u2, un * (energy + p)]
    gp = gamma * p
    speed = jnp.abs(un) + gp * lax.rsqrt(jnp.maximum(gp * rho, 1e-30))
    return [rho, mn, m1, m2, energy], flux, speed


def double_flux(left, right):
    if left is right:
        return [f + f for f in left[1]]
    speed = jnp.maximum(left[2], right[2])
    return [
        (left[1][k] + right[1][k]) - speed * (right[0][k] - left[0][k]) for k in range(5)
    ]


def place(normal):
    others = [c for c in range(3) if c != normal]
    return [0, 1 + normal, 1 + others[0], 1 + others[1], 4]


def updated(cons, flux_right, flux_left, normal):
    out = list(cons)
    for k, field in enumerate(place(normal)):
        out[field] = cons[field] - (0.5 * STEP) * (flux_right[k] - flux_left[k])
    return out


class Sweep:
    def __init__(self, n, normal, load, load_gamma, halo=None):
        self.n, self.normal = n, normal
        self.load, self.load_gamma, self.halo = load, load_gamma, halo
        self.cons, self.gam, self.prim, self.diff, self.rise, self.state = {}, {}, {}, {}, {}, {}

    def zone(self, i):
        return i if self.halo else min(max(i, 0), self.n - 1)

    def get_gam(self, i):
        i = self.zone(i)
        if i not in self.gam:
            gamma = self.load_gamma(i)
            gam1 = gamma - 1.0
            self.gam[i] = (gamma, recip(gam1), gam1)
        return self.gam[i]

    def get_cons(self, i):
        if i not in self.cons:
            self.cons[i] = self.load(i)
        return self.cons[i]

    def get(self, i):
        i = self.zone(i)
        if i not in self.prim:
            if 0 <= i < self.n:
                self.prim[i] = primitives(self.get_cons(i), self.get_gam(i)[2], self.normal)
            else:
                self.prim[i] = self.halo(i)
        return self.prim[i]

    def get_diff(self, i):
        if i not in self.diff:
            a, b = self.get(i), self.get(i + 1)
            self.diff[i] = [None] * 5 if a is b else [y - x for x, y in zip(a, b)]
        return self.diff[i]

    def get_rise(self, i):
        if i not in self.rise:
            here = self.get_diff(i)
            right = [face_rise(*t) for t in zip(self.get_diff(i - 1), here, self.get_diff(i + 1))]
            self.rise[i] = (right, [None if r is None else h - r for h, r in zip(here, right)])
        return self.rise[i]

    def get_state(self, i, upper):
        i = self.zone(i)
        if (i, upper) not in self.state:
            q, right, left = self.get(i), self.get_rise(i)[0], self.get_rise(i - 1)[1]
            pairs = [edges(*t) for t in zip(q, right, left)]
            side = [p[0] if upper else p[1] for p in pairs]
            self.state[i, upper] = state_flux(side, *self.get_gam(i)[:2])
            if all(p[0] is p[1] for p in pairs):
                self.state[i, not upper] = self.state[i, upper]
        return self.state[i, upper]

    def face(self, i):
        if not self.halo and i < 0:
            return double_flux(self.get_state(0, True), self.get_state(0, True))
        if not self.halo and i == self.n - 1:
            return double_flux(self.get_state(i, True), self.get_state(i, True))
        return double_flux(self.get_state(i, True), self.get_state(i + 1, False))

    def run(self, zones, store, flux=None):
        flux = self.face(zones[0] - 1) if flux is None else flux
        for i in zones:
            before, flux = flux, self.face(i)
            store(i, updated(self.get_cons(i), flux, before, self.normal))
        return flux


def own_row(y):
    odd = lax.rem(lax.axis_index("row"), 2) == 1
    return jnp.where(odd, SUB - 1 - y, y)


def own_sign():
    return jnp.where(lax.rem(lax.axis_index("row"), 2) == 1, -1.0, 1.0)


def rows_at(y, base, nx):
    return pl.ds(pl.multiple_of(own_row(y) * nx + base, SUB), SUB)


def shifted(tiles, by, edge):
    sub = lax.broadcasted_iota(jnp.int32, (SUB, LANES), 0)
    turned_tiles = [pltpu.roll(tile, SUB - 1 if by == 1 else 1, 0) for tile in tiles]
    if by == 1:
        beyond_tiles = turned_tiles[1:] + [edge]
        return [jnp.where(sub == SUB - 1, b, a) for a, b in zip(turned_tiles, beyond_tiles)]
    beyond_tiles = [edge] + turned_tiles[:-1]
    return [jnp.where(sub == 0, b, a) for a, b in zip(turned_tiles, beyond_tiles)]


def sweep_sublanes(cons, gamma):
    gam1 = [g - 1.0 for g in gamma]
    inv_gam1 = [recip(g) for g in gam1]
    prim = [primitives(c, g, 0) for c, g in zip(cons, gam1)]
    upper, lower_next = [], []
    for q in zip(*prim):
        here = [b - a for a, b in zip(q, shifted(q, 1, q[-1]))]
        right = [face_rise(*d) for d in zip(shifted(here, -1, 0.0), here, shifted(here, 1, 0.0))]
        left = shifted([h - r for h, r in zip(here, right)], -1, 0.0)
        pairs = [edges(*t) for t in zip(q, right, left)]
        upper.append([p[0] for p in pairs])
        lower_next.append(shifted([p[1] for p in pairs], 1, q[-1]))
    gamma_next, inv_next = shifted(gamma, 1, gamma[-1]), shifted(inv_gam1, 1, inv_gam1[-1])
    flux = [
        double_flux(state_flux(u, g, i), state_flux(l, gn, i_n))
        for u, l, g, i, gn, i_n in zip(
            zip(*upper), zip(*lower_next), gamma, inv_gam1, gamma_next, inv_next
        )
    ]
    start = state_flux(prim[0], gamma[0], inv_gam1[0])
    start = double_flux(start, start)
    before = [shifted(list(f), -1, e) for f, e in zip(zip(*flux), start)]
    return [updated(c, f, b, 0) for c, f, b in zip(cons, flux, zip(*before))]


def raw_kernel(state_hbm, gamma_hbm, two_ref, sems):
    copies = []
    for j in range(HALO):
        row = own_row(j)
        copies.append(
            pltpu.make_async_copy(
                state_hbm.at[:, :, row, :], two_ref.at[pl.ds(0, 5), j], sems.at[j, 0]
            )
        )
        copies.append(pltpu.make_async_copy(gamma_hbm.at[:, row, :], two_ref.at[5, j], sems.at[j, 1]))
    for k, copy in enumerate(copies):
        copy.start(priority=k % 2)
    for copy in copies:
        copy.wait()


def edge_rows_kernel(state_ref, gamma_ref, one_ref, rim_ref):
    nx, ny = one_ref.shape[1], SUB
    tiles = range(0, nx, SUB)
    ends = [[None, None] for _ in tiles]

    def put(n, tile, value):
        one_ref[n, pl.ds(tile * SUB, SUB), :] = value
        ends[tile][n // SUB] = into_window(ends[tile][n // SUB], n % SUB, value)

    for j in range(HALO):
        row = own_row(ny - 1 - j)
        at = [pl.ds(base * ny + row, SUB, stride=ny) for base in tiles]
        gamma = [gamma_ref[rows, :] for rows in at]
        swept = sweep_sublanes([[state_ref[f, rows, :] for f in range(5)] for rows in at], gamma)
        for tile, (cons, g) in enumerate(zip(swept, gamma)):
            for k, value in enumerate(primitives(cons, g - 1.0, 1)):
                put(HALO * k + j, tile, value)
            if j == 0:
                put(5 * HALO, tile, g)
    for tile, base in enumerate(tiles):
        for n in range(2):
            rim_ref[pl.ds(n * nx + base, SUB), :] = ends[tile][n]


def first_kernel(state_ref, gamma_ref, swept_ref):
    ny = SUB
    nx = gamma_ref.shape[0] // ny

    def load_gamma(x):
        return gamma_ref[pl.ds(x * ny, ny), :]

    def store(x, cons):
        for f in range(5):
            swept_ref[f, pl.ds(x, ny, stride=nx), :] = cons[f]

    sweep = Sweep(
        nx, 0, lambda x: [state_ref[f, pl.ds(x * ny, ny), :] for f in range(5)], load_gamma
    )
    sweep.run(range(nx), store)
    for x in range(nx):
        swept_ref[5, pl.ds(x, ny, stride=nx), :] = load_gamma(x)


def row_loads(swept_ref, base, nx, sign):
    def load(y):
        row = rows_at(y, base, nx)
        cons = [swept_ref[f, row, :] for f in range(5)]
        cons[2] = cons[2] * sign
        return cons

    return load, lambda y: swept_ref[5, rows_at(y, base, nx), :]


def lanes():
    return lax.broadcasted_iota(jnp.int32, (SUB, LANES), 1)


def groups(by=0):
    return ((lanes() - by) & (LANES - 1)) >> GROUP_BITS


def slots(by=0):
    return (lanes() - by) & (GROUP - 1)


def into_window(window, y, value):
    turn = (GROUP * y + 6) % LANES
    rolled = pltpu.roll(value, turn, 1) if turn else value
    if window is None:
        return rolled
    return jnp.where(groups() == y, rolled, window)


class EdgePack:
    def __init__(self, lower=None, upper=None):
        self.pack = [lower, upper]

    def add(self, y, cons, gamma):
        prim = primitives(cons, gamma - 1.0, 2)
        rolls = [turned(p, -(GROUP * y + 3 * k + 3)) for k, p in enumerate(prim)]
        for side in range(2):
            slot, group = slots(3 * (1 - side)), groups(3 * (1 - side))
            value = turned(gamma, -(GROUP * y + (16 if side else 18)))
            for k in reversed(range(5)):
                value = jnp.where(slot < 3 * (k + 1), rolls[k], value)
            old = self.pack[side]
            self.pack[side] = value if old is None else jnp.where(group == y, value, old)


SPLIT = 5


def kept_arrays(sweep, flux):
    cons, fluxes, speed = sweep.get_state(SPLIT, True)
    kept = [sweep.get(SPLIT + 1), sweep.get(SPLIT + 2), sweep.get_diff(SPLIT)]
    return sum(kept + [sweep.get_rise(SPLIT)[1], cons, fluxes, [speed], flux], [])


KEPT = 36


def second_near(rows, swept_ref, two_ref, next_ref, lower_ref, upper_ref, kept_ref):
    nx = swept_ref.shape[1] // SUB
    row = lax.axis_index("row")
    end = (row == 0) | (row == rows - 1)
    sign = own_sign()
    tiles = [pl.ds(base, SUB) for base in range(0, nx, SUB)]
    halos = []
    for j in range(HALO):
        gamma = [two_ref[5 * HALO + j, tile, :] for tile in tiles]
        cons = [[two_ref[HALO * f + j, tile, :] for f in range(5)] for tile in tiles]
        swept = sweep_sublanes(cons, gamma)
        halos.append([primitives(c, g - 1.0, 1) for c, g in zip(swept, gamma)])
    for base in range(0, nx, SUB):
        at = pl.ds(base, SUB)
        load, load_own_gamma = row_loads(swept_ref, base, nx, sign)
        pack = EdgePack()

        def load_gamma(y):
            if y >= 0:
                return load_own_gamma(y)
            return jnp.where(end, load_own_gamma(0), two_ref[5 * HALO, at, :])

        def halo(y):
            got = list(halos[-1 - y][base // SUB])
            got[1] = got[1] * sign
            return [jnp.where(end, p, q) for p, q in zip(sweep.get(0), got)]

        def store(y, cons):
            cons[2] = cons[2] * sign
            for f in range(5):
                next_ref[f, pl.ds(y * nx + base, SUB), :] = cons[f]
            pack.add(y, cons, load_own_gamma(y))

        sweep = Sweep(SUB, 1, load, load_gamma, halo)
        flux = sweep.run(range(SPLIT), store)
        lower_ref[at, :], upper_ref[at, :] = pack.pack
        kept = kept_arrays(sweep, flux)
        assert len(kept) == KEPT
        for k in range(KEPT):
            kept_ref[k, at, :] = kept[k]


def sweep_far(swept_ref, kept_ref, base, received, store):
    nx = swept_ref.shape[1] // SUB
    at = pl.ds(base, SUB)
    sign = own_sign()
    load, load_own_gamma = row_loads(swept_ref, base, nx, sign)

    def load_gamma(y):
        return load_own_gamma(y) if y < SUB else received(5 * HALO)

    def halo(y):
        got = [received(HALO * k + y - SUB) for k in range(5)]
        got[1] = got[1] * sign
        return got

    def signed_store(y, cons):
        cons[2] = cons[2] * sign
        store(y, cons, load_own_gamma(y))

    kept = [kept_ref[k, at, :] for k in range(KEPT)]
    sweep = Sweep(SUB, 1, load, load_gamma, halo)
    sweep.prim[SPLIT + 1], sweep.prim[SPLIT + 2] = kept[0:5], kept[5:10]
    sweep.diff[SPLIT] = kept[10:15]
    sweep.rise[SPLIT] = (None, kept[15:20])
    sweep.state[SPLIT, True] = (kept[20:25], kept[25:30], kept[30])
    sweep.run(range(SPLIT, SUB), signed_store, kept[31:36])


def rim_kernel(
    swept_ref, rim_ref, lower_ref, upper_ref, kept_ref, next_ref, to_one_ref, to_two_ref
):
    nx = swept_ref.shape[1] // SUB
    for base in range(0, nx, SUB):
        at = pl.ds(base, SUB)
        pack = EdgePack(lower_ref[at, :], upper_ref[at, :])

        def received(n):
            return turned(rim_ref[pl.ds(n // SUB * nx + base, SUB), :], GROUP * (n % SUB) + 6)

        def store(y, cons, gamma):
            for f in range(5):
                next_ref[f, pl.ds((y - SPLIT) * nx + base, SUB), :] = cons[f]
            pack.add(y, cons, gamma)

        sweep_far(swept_ref, kept_ref, base, received, store)
        lower, upper = pack.pack
        odd = lax.rem(lax.axis_index("col"), 2) == 1
        to_one_ref[at, :] = jnp.where(odd, lower, upper)
        to_two_ref[at, :] = jnp.where(odd, upper, lower)
        to_two_ref[pl.ds(nx + base, SUB), :] = lower


def second_far(swept_ref, one_ref, kept_ref, *others):
    next_ref = others[-1]
    nx = swept_ref.shape[1] // SUB
    for base in range(0, nx, SUB):

        def store(y, cons, gamma):
            for f in range(5):
                next_ref[f, pl.ds((y - SPLIT) * nx + base, SUB), :] = cons[f]

        sweep_far(swept_ref, kept_ref, base, lambda n: one_ref[n, pl.ds(base, SUB), :], store)


def sweep_lanes(cons, prim, gamma, normal):
    def ahead(x):
        return pltpu.roll(x, LANES - 1, 1)

    def behind(x):
        return pltpu.roll(x, 1, 1)

    inv_gam1 = recip(gamma - 1.0)
    upper, lower_next = [], []
    for q in prim:
        here = ahead(q) - q
        right = face_rise(behind(here), here, ahead(here))
        left = behind(here - right)
        up, low = edges(q, right, left)
        upper.append(up)
        lower_next.append(ahead(low))
    flux = double_flux(
        state_flux(upper, gamma, inv_gam1),
        state_flux(lower_next, ahead(gamma), ahead(inv_gam1)),
    )
    return updated(cons, flux, [behind(x) for x in flux], normal)


def sweep_lines(cons, lines, gammas, normal):
    gam = {k: (g, recip(g - 1.0)) for k, g in gammas.items()}
    states = {key: [] for key in ((-1, 0), (0, 1), (0, 0), (1, 1))}
    for line in lines:
        diff = {k: line[k + 1] - line[k] for k in range(-3, 3)}
        rise = {k: face_rise(diff[k - 1], diff[k], diff[k + 1]) for k in range(-2, 2)}
        for k, which in states:
            right, left = rise[k], diff[k - 1] - rise[k - 1]
            if which == k + 1:
                states[k, which].append(line[k] + clamp_zero(right, 2.0 * left))
            else:
                states[k, which].append(line[k] - clamp_zero(left, 2.0 * right))
    side = {key: state_flux(prim, *gam[key[0]]) for key, prim in states.items()}
    before = double_flux(side[-1, 0], side[0, 0])
    after = double_flux(side[0, 1], side[1, 1])
    return updated(cons, after, before, normal)


def turned(x, by):
    by %= LANES
    return pltpu.roll(x, LANES - by, 1) if by else x


REACH = range(-HALO, HALO + 1)
LINES = 5 * len(REACH)
EDGE_ARRAYS = LINES + 3 + 5


def beyond(slot, k, cols):
    col = lax.axis_index("col")
    if k < 0:
        return (slot >= 6) & (slot < 6 - k), col == 0
    return (slot >= 6 - k) & (slot < 6), col == cols - 1


def zone_loads(near_ref, far_ref, gamma_ref, base, nx):
    def load(y):
        rows_ref, start = (near_ref, y) if y < SPLIT else (far_ref, y - SPLIT)
        cons = [rows_ref[f, pl.ds(start * nx + base, SUB), :] for f in range(5)]
        gamma = gamma_ref[5, rows_at(y, base, nx), :]
        return cons, primitives(cons, gamma - 1.0, 2), gamma

    return load


def third_kernel(first, rows_ref, gamma_ref, out_ref):
    nx = gamma_ref.shape[1] // SUB
    for base in range(0, nx, SUB):
        for y in range(rows_ref.shape[1] // nx):
            at = pl.ds(y * nx + base, SUB)
            cons = [rows_ref[f, at, :] for f in range(5)]
            gamma = gamma_ref[5, rows_at(first + y, base, nx), :]
            inner = sweep_lanes(cons, primitives(cons, gamma - 1.0, 2), gamma, 2)
            for f in range(5):
                out_ref[f, at, :] = inner[f]


def window_kernel(cols, near_ref, far_ref, gamma_ref, edge_ref):
    nx = edge_ref.shape[1]
    slot = slots()
    for base in range(0, nx, SUB):
        load = zone_loads(near_ref, far_ref, gamma_ref, base, nx)
        windows = [None] * 11
        for y in range(SUB):
            cons, prim, gamma = load(y)
            for k, value in enumerate(prim + [gamma] + cons):
                windows[k] = into_window(windows[k], y, value)
        at = pl.ds(base, SUB)
        for q, own in enumerate(windows[:6]):
            line = {k: turned(own, k) for k in (REACH if q < 5 else (-1, 0, 1))}
            for n, k in enumerate(line):
                value = line[k]
                if k:
                    where, end = beyond(slot, k, cols)
                    if abs(k) == 1:
                        last = own
                    elif k < 0:
                        last = jnp.where(slot == 6, own, jnp.where(slot == 7, line[-1], line[-2]))
                    else:
                        last = jnp.where(slot == 5, own, jnp.where(slot == 4, line[1], line[2]))
                    value = jnp.where(where & end, last, value)
                edge_ref[len(REACH) * q + n, at, :] = value
        for f in range(5):
            edge_ref[LINES + 3 + f, at, :] = windows[6 + f]


def mend_edges(cols, near_ref, far_ref, edge_ref, one_ref, two_ref, out_ref, held, sems):
    nx = edge_ref.shape[1]
    ny = SUB
    odd = lax.rem(lax.axis_index("col"), 2) == 1
    lane = lanes()
    slot = slots()
    at_edge = (lane < HALO) | (lane >= LANES - HALO)
    edge_new = []
    for base in range(0, nx, SUB):
        at = pl.ds(base, SUB)
        one, two = one_ref[at, :], two_ref[at, :]
        lower, upper = jnp.where(odd, one, two), jnp.where(odd, two, one)

        def joined(index, k, lane_by):
            own = edge_ref[index, at, :]
            if not k:
                return own
            where, end = beyond(slot, k, cols)
            got = turned(lower if k < 0 else upper, lane_by)
            return jnp.where(where & jnp.logical_not(end), got, own)

        lines = [
            {k: joined(len(REACH) * q + n, k, 3 * q + k - 3) for n, k in enumerate(REACH)}
            for q in range(5)
        ]
        gammas = {-1: joined(LINES, -1, 9), 0: joined(LINES + 1, 0, 0), 1: joined(LINES + 2, 1, 13)}
        cons = [edge_ref[LINES + 3 + f, at, :] for f in range(5)]
        edge_new.append(sweep_lines(cons, lines, gammas, 2))
    copies = []
    for f in range(5):
        for tile, new in enumerate(edge_new):
            for y in range(ny):
                edge = turned(new[f], GROUP * y + 6)
                at = pl.ds(tile * SUB * ny + own_row(y), SUB, stride=ny)
                rows_ref, start = (near_ref, y) if y < SPLIT else (far_ref, y - SPLIT)
                inner = rows_ref[f, pl.ds(start * nx + tile * SUB, SUB), :]
                held[f, at, :] = jnp.where(at_edge, edge, inner)
        copy = pltpu.make_async_copy(held.at[f], out_ref.at[f], sems.at[f])
        copy.start(priority=f % 2)
        copies.append(copy)
    for copy in copies:
        copy.wait()


def at_end(cols):
    col = lax.axis_index("col")
    return (col == 0) | (col == cols - 1)


def end_kernel(cols, near_ref, far_ref, edge_ref, one_ref, out_ref, held, sems):
    @pl.when(at_end(cols))
    def _():
        mend_edges(cols, near_ref, far_ref, edge_ref, one_ref, one_ref, out_ref, held, sems)


def middle_kernel(
    cols, ends_ref, near_ref, far_ref, edge_ref, one_ref, two_ref, out_ref, held, sems
):
    @pl.when(jnp.logical_not(at_end(cols)))
    def _():
        mend_edges(cols, near_ref, far_ref, edge_ref, one_ref, two_ref, out_ref, held, sems)


def swap_pairs(mesh, axis, inner):
    rows, cols = mesh.shape["row"], mesh.shape["col"]
    pairs = []
    for r in range(rows):
        for c in range(cols):
            k, n = (r, rows) if axis == "row" else (c, cols)
            if not inner:
                k ^= 1
            elif 0 < k < n - 1:
                k = ((k - 1) ^ 1) + 1
            else:
                k = None
            if axis == "row":
                to = (r, c ^ 1) if k is None else (k, c)
            else:
                to = (r, cols - 1 - c) if k is None else (r, k)
            pairs.append((r * cols + c, to[0] * cols + to[1]))
    return pairs


def body(mesh, state, gamma):
    rows, cols = mesh.shape["row"], mesh.shape["col"]
    _, nx, ny, nz = state.shape
    assert ny == SUB and nz == LANES and nx % SUB == 0 and rows % 2 == 0 and cols % 2 == 0
    here = lambda *dims: pltpu.VMEM(dims, jnp.float32)
    keep = lambda x: pltpu.with_memory_space_constraint(x, pltpu.VMEM)
    near = pl.BlockSpec(memory_space=pltpu.VMEM)
    swap = lambda x, axis, inner: lax.ppermute(x, ("row", "col"), swap_pairs(mesh, axis, inner))

    two = pl.pallas_call(
        raw_kernel,
        out_shape=here(6, HALO, nx, nz),
        in_specs=[pl.BlockSpec(memory_space=pltpu.HBM)] * 2,
        out_specs=near,
        scratch_shapes=[pltpu.SemaphoreType.DMA((HALO, 2))],
        name="raw_edges",
    )(state, gamma)
    two = swap(two, "row", True).reshape(6 * HALO, nx, nz)
    held = (keep(state.reshape(5, nx * ny, nz)), keep(gamma.reshape(nx * ny, nz)))
    one, rim = pl.pallas_call(
        edge_rows_kernel,
        out_shape=(here(5 * HALO + 1, nx, nz), here(2 * nx, nz)),
        in_specs=[near] * 2,
        out_specs=(near,) * 2,
        name="edge_rows",
    )(*held)
    swept = pl.pallas_call(
        first_kernel,
        out_shape=here(6, ny * nx, nz),
        in_specs=[near] * 2,
        out_specs=near,
        name="sweep_first",
    )(*held)
    rim = swap(rim, "row", False)
    one = swap(one, "row", False)
    near_rows, lower, upper, kept = pl.pallas_call(
        functools.partial(second_near, rows),
        out_shape=(here(5, SPLIT * nx, nz), here(nx, nz), here(nx, nz), here(KEPT, nx, nz)),
        in_specs=[near] * 2,
        out_specs=(near,) * 4,
        name="second_near",
    )(keep(swept), keep(two))
    far_shape = here(5, (ny - SPLIT) * nx, nz)
    rim_rows, to_one, to_two = pl.pallas_call(
        rim_kernel,
        out_shape=(far_shape, here(nx, nz), here(2 * nx, nz)),
        in_specs=[near] * 5,
        out_specs=(near,) * 3,
        cost_estimate=pl.CostEstimate(flops=10**9, bytes_accessed=0, transcendentals=0),
        name="second_rim",
    )(keep(swept), keep(rim), keep(lower), keep(upper), keep(kept))
    two = swap(to_two, "col", True)
    col_one = swap(to_one, "col", False)
    def third(first, rows_in):
        return pl.pallas_call(
            functools.partial(third_kernel, first),
            out_shape=here(*rows_in.shape),
            in_specs=[near] * 2,
            out_specs=near,
            name="third_far" if first else "third_near",
        )(keep(rows_in), keep(swept))

    inner_near = third(0, near_rows)
    edge = pl.pallas_call(
        functools.partial(window_kernel, cols),
        out_shape=here(EDGE_ARRAYS, nx, nz),
        in_specs=[near] * 3,
        out_specs=near,
        name="third_windows",
    )(keep(near_rows), keep(rim_rows), keep(swept))
    far_rows = pl.pallas_call(
        second_far,
        out_shape=far_shape,
        in_specs=[near] * 5,
        out_specs=near,
        name="second_far",
    )(keep(swept), keep(one), keep(kept), keep(inner_near), keep(edge))
    inner = (keep(inner_near), keep(third(SPLIT, far_rows)))
    far = pl.BlockSpec(memory_space=pltpu.HBM)
    whole = jax.ShapeDtypeStruct((5, nx * ny, nz), jnp.float32)
    scratch = [pltpu.VMEM(whole.shape, jnp.float32), pltpu.SemaphoreType.DMA((5,))]
    ends = pl.pallas_call(
        functools.partial(end_kernel, cols),
        out_shape=whole,
        in_specs=[near] * 4,
        out_specs=far,
        scratch_shapes=scratch,
        name="third_ends",
    )(*inner, keep(edge), keep(col_one))
    out = pl.pallas_call(
        functools.partial(middle_kernel, cols),
        out_shape=whole,
        in_specs=[far] + [near] * 5,
        out_specs=far,
        input_output_aliases={0: 0},
        scratch_shapes=scratch,
        name="third_middle",
    )(ends, *inner, keep(edge), keep(col_one), keep(two))
    return out.reshape(5, nx, ny, nz)


def solution(mesh):
    in_specs = (P(None, None, "row", "col"), P(None, "row", "col"))
    out_specs = P(None, None, "row", "col")
    return jax.shard_map(
        functools.partial(body, mesh),
        mesh=mesh,
        in_specs=in_specs,
        out_specs=out_specs,
        check_vma=False,
    )
```

```python
import functools

import jax
import jax.numpy as jnp
from jax import lax
from jax.experimental import pallas as pl
from jax.experimental.pallas import tpu as pltpu
from jax.sharding import PartitionSpec as P

STEP = 0.08
HALO = 3
SUB, LANES = 8, 128
GROUP_BITS = 4
GROUP = 1 << GROUP_BITS


def recip(x):
    r = pl.reciprocal(x, approx=True)
    return r * (2.0 - x * r)


def clamp_zero(u, v):
    return jnp.maximum(jnp.minimum(u, jnp.maximum(v, 0.0)), jnp.minimum(v, 0.0))


def primitives(cons, gam1, normal):
    rho, m0, m1, m2, energy = cons
    inv = recip(rho)
    vel = [m0 * inv, m1 * inv, m2 * inv]
    kinetic = 0.5 * (m0 * vel[0] + m1 * vel[1] + m2 * vel[2])
    pressure = gam1 * (energy - kinetic)
    others = [c for c in range(3) if c != normal]
    return [rho, vel[normal], vel[others[0]], vel[others[1]], pressure]


def face_rise(before, here, after):
    if here is None:
        return None
    rise = 0.5 * here
    if before is not None and after is not None:
        rise = rise + (before - after) * (1.0 / 12.0)
    elif before is not None:
        rise = rise + before * (1.0 / 12.0)
    elif after is not None:
        rise = rise - after * (1.0 / 12.0)
    return clamp_zero(rise, here)


def edges(q, right, left):
    if right is None or left is None:
        return q, q
    return q + clamp_zero(right, 2.0 * left), q - clamp_zero(left, 2.0 * right)


def state_flux(prim, gamma, inv_gam1):
    rho, un, u1, u2, p = prim
    mn, m1, m2 = rho * un, rho * u1, rho * u2
    nn = mn * un
    energy = p * inv_gam1 + 0.5 * (nn + m1 * u1 + m2 * u2)
    flux = [mn, nn + p, mn * u1, mn * u2, un * (energy + p)]
    gp = gamma * p
    speed = jnp.abs(un) + gp * lax.rsqrt(jnp.maximum(gp * rho, 1e-30))
    return [rho, mn, m1, m2, energy], flux, speed


def double_flux(left, right):
    if left is right:
        return [f + f for f in left[1]]
    speed = jnp.maximum(left[2], right[2])
    return [
        (left[1][k] + right[1][k]) - speed * (right[0][k] - left[0][k]) for k in range(5)
    ]


def place(normal):
    others = [c for c in range(3) if c != normal]
    return [0, 1 + normal, 1 + others[0], 1 + others[1], 4]


def updated(cons, flux_right, flux_left, normal):
    out = list(cons)
    for k, field in enumerate(place(normal)):
        out[field] = cons[field] - (0.5 * STEP) * (flux_right[k] - flux_left[k])
    return out


class Sweep:
    def __init__(self, n, normal, load, load_gamma, halo=None):
        self.n, self.normal = n, normal
        self.load, self.load_gamma, self.halo = load, load_gamma, halo
        self.cons, self.gam, self.prim, self.diff, self.rise, self.state = {}, {}, {}, {}, {}, {}

    def zone(self, i):
        return i if self.halo else min(max(i, 0), self.n - 1)

    def get_gam(self, i):
        i = self.zone(i)
        if i not in self.gam:
            gamma = self.load_gamma(i)
            gam1 = gamma - 1.0
            self.gam[i] = (gamma, recip(gam1), gam1)
        return self.gam[i]

    def get_cons(self, i):
        if i not in self.cons:
            self.cons[i] = self.load(i)
        return self.cons[i]

    def get(self, i):
        i = self.zone(i)
        if i not in self.prim:
            if 0 <= i < self.n:
                self.prim[i] = primitives(self.get_cons(i), self.get_gam(i)[2], self.normal)
            else:
                self.prim[i] = self.halo(i)
        return self.prim[i]

    def get_diff(self, i):
        if i not in self.diff:
            a, b = self.get(i), self.get(i + 1)
            self.diff[i] = [None] * 5 if a is b else [y - x for x, y in zip(a, b)]
        return self.diff[i]

    def get_rise(self, i):
        if i not in self.rise:
            here = self.get_diff(i)
            right = [face_rise(*t) for t in zip(self.get_diff(i - 1), here, self.get_diff(i + 1))]
            self.rise[i] = (right, [None if r is None else h - r for h, r in zip(here, right)])
        return self.rise[i]

    def get_state(self, i, upper):
        i = self.zone(i)
        if (i, upper) not in self.state:
            q, right, left = self.get(i), self.get_rise(i)[0], self.get_rise(i - 1)[1]
            pairs = [edges(*t) for t in zip(q, right, left)]
            side = [p[0] if upper else p[1] for p in pairs]
            self.state[i, upper] = state_flux(side, *self.get_gam(i)[:2])
            if all(p[0] is p[1] for p in pairs):
                self.state[i, not upper] = self.state[i, upper]
        return self.state[i, upper]

    def face(self, i):
        if not self.halo and i < 0:
            return double_flux(self.get_state(0, True), self.get_state(0, True))
        if not self.halo and i == self.n - 1:
            return double_flux(self.get_state(i, True), self.get_state(i, True))
        return double_flux(self.get_state(i, True), self.get_state(i + 1, False))

    def run(self, zones, store, flux=None):
        flux = self.face(zones[0] - 1) if flux is None else flux
        for i in zones:
            before, flux = flux, self.face(i)
            store(i, updated(self.get_cons(i), flux, before, self.normal))
        return flux


def own_row(y):
    odd = lax.rem(lax.axis_index("row"), 2) == 1
    return jnp.where(odd, SUB - 1 - y, y)


def own_sign():
    return jnp.where(lax.rem(lax.axis_index("row"), 2) == 1, -1.0, 1.0)


def rows_at(y, base, nx):
    return pl.ds(pl.multiple_of(own_row(y) * nx + base, SUB), SUB)


def shifted(tiles, by, edge):
    sub = lax.broadcasted_iota(jnp.int32, (SUB, LANES), 0)
    turned_tiles = [pltpu.roll(tile, SUB - 1 if by == 1 else 1, 0) for tile in tiles]
    if by == 1:
        beyond_tiles = turned_tiles[1:] + [edge]
        return [jnp.where(sub == SUB - 1, b, a) for a, b in zip(turned_tiles, beyond_tiles)]
    beyond_tiles = [edge] + turned_tiles[:-1]
    return [jnp.where(sub == 0, b, a) for a, b in zip(turned_tiles, beyond_tiles)]


def sweep_sublanes(cons, gamma):
    gam1 = [g - 1.0 for g in gamma]
    inv_gam1 = [recip(g) for g in gam1]
    prim = [primitives(c, g, 0) for c, g in zip(cons, gam1)]
    upper, lower_next = [], []
    for q in zip(*prim):
        here = [b - a for a, b in zip(q, shifted(q, 1, q[-1]))]
        right = [face_rise(*d) for d in zip(shifted(here, -1, 0.0), here, shifted(here, 1, 0.0))]
        left = shifted([h - r for h, r in zip(here, right)], -1, 0.0)
        pairs = [edges(*t) for t in zip(q, right, left)]
        upper.append([p[0] for p in pairs])
        lower_next.append(shifted([p[1] for p in pairs], 1, q[-1]))
    gamma_next, inv_next = shifted(gamma, 1, gamma[-1]), shifted(inv_gam1, 1, inv_gam1[-1])
    flux = [
        double_flux(state_flux(u, g, i), state_flux(l, gn, i_n))
        for u, l, g, i, gn, i_n in zip(
            zip(*upper), zip(*lower_next), gamma, inv_gam1, gamma_next, inv_next
        )
    ]
    start = state_flux(prim[0], gamma[0], inv_gam1[0])
    start = double_flux(start, start)
    before = [shifted(list(f), -1, e) for f, e in zip(zip(*flux), start)]
    return [updated(c, f, b, 0) for c, f, b in zip(cons, flux, zip(*before))]


def raw_kernel(state_hbm, gamma_hbm, two_ref, sems):
    copies = []
    for j in range(HALO):
        row = own_row(j)
        copies.append(
            pltpu.make_async_copy(
                state_hbm.at[:, :, row, :], two_ref.at[pl.ds(0, 5), j], sems.at[j, 0]
            )
        )
        copies.append(pltpu.make_async_copy(gamma_hbm.at[:, row, :], two_ref.at[5, j], sems.at[j, 1]))
    for k, copy in enumerate(copies):
        copy.start(priority=k % 2)
    for copy in copies:
        copy.wait()


def edge_rows_kernel(state_ref, gamma_ref, one_ref, rim_ref):
    nx, ny = one_ref.shape[1], SUB
    tiles = range(0, nx, SUB)
    ends = [[None, None] for _ in tiles]

    def put(n, tile, value):
        one_ref[n, pl.ds(tile * SUB, SUB), :] = value
        ends[tile][n // SUB] = into_window(ends[tile][n // SUB], n % SUB, value)

    for j in range(HALO):
        row = own_row(ny - 1 - j)
        at = [pl.ds(base * ny + row, SUB, stride=ny) for base in tiles]
        gamma = [gamma_ref[rows, :] for rows in at]
        swept = sweep_sublanes([[state_ref[f, rows, :] for f in range(5)] for rows in at], gamma)
        for tile, (cons, g) in enumerate(zip(swept, gamma)):
            for k, value in enumerate(primitives(cons, g - 1.0, 1)):
                put(HALO * k + j, tile, value)
            if j == 0:
                put(5 * HALO, tile, g)
    for tile, base in enumerate(tiles):
        for n in range(2):
            rim_ref[pl.ds(n * nx + base, SUB), :] = ends[tile][n]


def first_kernel(state_ref, gamma_ref, swept_ref):
    ny = SUB
    nx = gamma_ref.shape[0] // ny

    def load_gamma(x):
        return gamma_ref[pl.ds(x * ny, ny), :]

    def store(x, cons):
        for f in range(5):
            swept_ref[f, pl.ds(x, ny, stride=nx), :] = cons[f]

    sweep = Sweep(
        nx, 0, lambda x: [state_ref[f, pl.ds(x * ny, ny), :] for f in range(5)], load_gamma
    )
    sweep.run(range(nx), store)
    for x in range(nx):
        swept_ref[5, pl.ds(x, ny, stride=nx), :] = load_gamma(x)


def row_loads(swept_ref, base, nx, sign):
    def load(y):
        row = rows_at(y, base, nx)
        cons = [swept_ref[f, row, :] for f in range(5)]
        cons[2] = cons[2] * sign
        return cons

    return load, lambda y: swept_ref[5, rows_at(y, base, nx), :]


def lanes():
    return lax.broadcasted_iota(jnp.int32, (SUB, LANES), 1)


def groups(by=0):
    return ((lanes() - by) & (LANES - 1)) >> GROUP_BITS


def slots(by=0):
    return (lanes() - by) & (GROUP - 1)


def into_window(window, y, value):
    turn = (GROUP * y + 6) % LANES
    rolled = pltpu.roll(value, turn, 1) if turn else value
    if window is None:
        return rolled
    return jnp.where(groups() == y, rolled, window)


class EdgePack:
    def __init__(self, lower=None, upper=None):
        self.pack = [lower, upper]

    def add(self, y, cons, gamma):
        prim = primitives(cons, gamma - 1.0, 2)
        rolls = [turned(p, -(GROUP * y + 3 * k + 3)) for k, p in enumerate(prim)]
        for side in range(2):
            slot, group = slots(3 * (1 - side)), groups(3 * (1 - side))
            value = turned(gamma, -(GROUP * y + (16 if side else 18)))
            for k in reversed(range(5)):
                value = jnp.where(slot < 3 * (k + 1), rolls[k], value)
            old = self.pack[side]
            self.pack[side] = value if old is None else jnp.where(group == y, value, old)


SPLIT = 5


def kept_arrays(sweep, flux):
    cons, fluxes, speed = sweep.get_state(SPLIT, True)
    kept = [sweep.get(SPLIT + 1), sweep.get(SPLIT + 2), sweep.get_diff(SPLIT)]
    return sum(kept + [sweep.get_rise(SPLIT)[1], cons, fluxes, [speed], flux], [])


KEPT = 36


def second_near(rows, swept_ref, two_ref, next_ref, lower_ref, upper_ref, kept_ref):
    nx = swept_ref.shape[1] // SUB
    row = lax.axis_index("row")
    end = (row == 0) | (row == rows - 1)
    sign = own_sign()
    tiles = [pl.ds(base, SUB) for base in range(0, nx, SUB)]
    halos = []
    for j in range(HALO):
        gamma = [two_ref[5 * HALO + j, tile, :] for tile in tiles]
        cons = [[two_ref[HALO * f + j, tile, :] for f in range(5)] for tile in tiles]
        swept = sweep_sublanes(cons, gamma)
        halos.append([primitives(c, g - 1.0, 1) for c, g in zip(swept, gamma)])
    for base in range(0, nx, SUB):
        at = pl.ds(base, SUB)
        load, load_own_gamma = row_loads(swept_ref, base, nx, sign)
        pack = EdgePack()

        def load_gamma(y):
            if y >= 0:
                return load_own_gamma(y)
            return jnp.where(end, load_own_gamma(0), two_ref[5 * HALO, at, :])

        def halo(y):
            got = list(halos[-1 - y][base // SUB])
            got[1] = got[1] * sign
            return [jnp.where(end, p, q) for p, q in zip(sweep.get(0), got)]

        def store(y, cons):
            cons[2] = cons[2] * sign
            for f in range(5):
                next_ref[f, pl.ds(y * nx + base, SUB), :] = cons[f]
            pack.add(y, cons, load_own_gamma(y))

        sweep = Sweep(SUB, 1, load, load_gamma, halo)
        flux = sweep.run(range(SPLIT), store)
        lower_ref[at, :], upper_ref[at, :] = pack.pack
        kept = kept_arrays(sweep, flux)
        assert len(kept) == KEPT
        for k in range(KEPT):
            kept_ref[k, at, :] = kept[k]


def sweep_far(swept_ref, kept_ref, base, received, store):
    nx = swept_ref.shape[1] // SUB
    at = pl.ds(base, SUB)
    sign = own_sign()
    load, load_own_gamma = row_loads(swept_ref, base, nx, sign)

    def load_gamma(y):
        return load_own_gamma(y) if y < SUB else received(5 * HALO)

    def halo(y):
        got = [received(HALO * k + y - SUB) for k in range(5)]
        got[1] = got[1] * sign
        return got

    def signed_store(y, cons):
        cons[2] = cons[2] * sign
        store(y, cons, load_own_gamma(y))

    kept = [kept_ref[k, at, :] for k in range(KEPT)]
    sweep = Sweep(SUB, 1, load, load_gamma, halo)
    sweep.prim[SPLIT + 1], sweep.prim[SPLIT + 2] = kept[0:5], kept[5:10]
    sweep.diff[SPLIT] = kept[10:15]
    sweep.rise[SPLIT] = (None, kept[15:20])
    sweep.state[SPLIT, True] = (kept[20:25], kept[25:30], kept[30])
    sweep.run(range(SPLIT, SUB), signed_store, kept[31:36])


def rim_kernel(
    swept_ref, rim_ref, lower_ref, upper_ref, kept_ref, next_ref, to_one_ref, to_two_ref
):
    nx = swept_ref.shape[1] // SUB
    for base in range(0, nx, SUB):
        at = pl.ds(base, SUB)
        pack = EdgePack(lower_ref[at, :], upper_ref[at, :])

        def received(n):
            return turned(rim_ref[pl.ds(n // SUB * nx + base, SUB), :], GROUP * (n % SUB) + 6)

        def store(y, cons, gamma):
            for f in range(5):
                next_ref[f, pl.ds((y - SPLIT) * nx + base, SUB), :] = cons[f]
            pack.add(y, cons, gamma)

        sweep_far(swept_ref, kept_ref, base, received, store)
        lower, upper = pack.pack
        odd = lax.rem(lax.axis_index("col"), 2) == 1
        to_one_ref[at, :] = jnp.where(odd, lower, upper)
        to_two_ref[at, :] = jnp.where(odd, upper, lower)
        to_two_ref[pl.ds(nx + base, SUB), :] = lower


def second_far(swept_ref, one_ref, kept_ref, *others):
    next_ref = others[-1]
    nx = swept_ref.shape[1] // SUB
    for base in range(0, nx, SUB):

        def store(y, cons, gamma):
            for f in range(5):
                next_ref[f, pl.ds((y - SPLIT) * nx + base, SUB), :] = cons[f]

        sweep_far(swept_ref, kept_ref, base, lambda n: one_ref[n, pl.ds(base, SUB), :], store)


def turned(x, by):
    by %= LANES
    return pltpu.roll(x, LANES - by, 1) if by else x


def sweep_lanes(cons, prim, gamma, normal):
    inv_gam1 = recip(gamma - 1.0)
    upper, lower_next = [], []
    for q in prim:
        line = [turned(q, k) for k in range(-2, 4)]
        diff = [b - a for a, b in zip(line, line[1:])]
        rise = [face_rise(*diff[k : k + 3]) for k in range(3)]
        upper.append(q + clamp_zero(rise[1], 2.0 * (diff[1] - rise[0])))
        lower_next.append(line[3] - clamp_zero(diff[2] - rise[1], 2.0 * rise[2]))
    flux = double_flux(
        state_flux(upper, gamma, inv_gam1),
        state_flux(lower_next, turned(gamma, 1), turned(inv_gam1, 1)),
    )
    return updated(cons, flux, [turned(x, -1) for x in flux], normal)


def sweep_lines(cons, lines, gammas, normal):
    gam = {k: (g, recip(g - 1.0)) for k, g in gammas.items()}
    states = {key: [] for key in ((-1, 0), (0, 1), (0, 0), (1, 1))}
    for line in lines:
        diff = {k: line[k + 1] - line[k] for k in range(-3, 3)}
        rise = {k: face_rise(diff[k - 1], diff[k], diff[k + 1]) for k in range(-2, 2)}
        for k, which in states:
            right, left = rise[k], diff[k - 1] - rise[k - 1]
            if which == k + 1:
                states[k, which].append(line[k] + clamp_zero(right, 2.0 * left))
            else:
                states[k, which].append(line[k] - clamp_zero(left, 2.0 * right))
    side = {key: state_flux(prim, *gam[key[0]]) for key, prim in states.items()}
    before = double_flux(side[-1, 0], side[0, 0])
    after = double_flux(side[0, 1], side[1, 1])
    return updated(cons, after, before, normal)


REACH = range(-HALO, HALO + 1)
LINES = 5 * len(REACH)
EDGE_ARRAYS = LINES + 3 + 5


def beyond(slot, k, cols):
    col = lax.axis_index("col")
    if k < 0:
        return (slot >= 6) & (slot < 6 - k), col == 0
    return (slot >= 6 - k) & (slot < 6), col == cols - 1


def zone_loads(near_ref, far_ref, gamma_ref, base, nx):
    def load(y):
        rows_ref, start = (near_ref, y) if y < SPLIT else (far_ref, y - SPLIT)
        cons = [rows_ref[f, pl.ds(start * nx + base, SUB), :] for f in range(5)]
        gamma = gamma_ref[5, rows_at(y, base, nx), :]
        return cons, primitives(cons, gamma - 1.0, 2), gamma

    return load


def third_kernel(first, rows_ref, gamma_ref, out_ref):
    nx = gamma_ref.shape[1] // SUB
    for base in range(0, nx, SUB):
        for y in range(rows_ref.shape[1] // nx):
            at = pl.ds(y * nx + base, SUB)
            cons = [rows_ref[f, at, :] for f in range(5)]
            gamma = gamma_ref[5, rows_at(first + y, base, nx), :]
            inner = sweep_lanes(cons, primitives(cons, gamma - 1.0, 2), gamma, 2)
            for f in range(5):
                out_ref[f, at, :] = inner[f]


def window_kernel(cols, near_ref, far_ref, gamma_ref, edge_ref):
    nx = edge_ref.shape[1]
    slot = slots()
    for base in range(0, nx, SUB):
        load = zone_loads(near_ref, far_ref, gamma_ref, base, nx)
        windows = [None] * 11
        for y in range(SUB):
            cons, prim, gamma = load(y)
            for k, value in enumerate(prim + [gamma] + cons):
                windows[k] = into_window(windows[k], y, value)
        at = pl.ds(base, SUB)
        for q, own in enumerate(windows[:6]):
            line = {k: turned(own, k) for k in (REACH if q < 5 else (-1, 0, 1))}
            for n, k in enumerate(line):
                value = line[k]
                if k:
                    where, end = beyond(slot, k, cols)
                    if abs(k) == 1:
                        last = own
                    elif k < 0:
                        last = jnp.where(slot == 6, own, jnp.where(slot == 7, line[-1], line[-2]))
                    else:
                        last = jnp.where(slot == 5, own, jnp.where(slot == 4, line[1], line[2]))
                    value = jnp.where(where & end, last, value)
                edge_ref[len(REACH) * q + n, at, :] = value
        for f in range(5):
            edge_ref[LINES + 3 + f, at, :] = windows[6 + f]


def mend_edges(cols, near_ref, far_ref, edge_ref, one_ref, two_ref, out_ref, held, sems):
    nx = edge_ref.shape[1]
    ny = SUB
    odd = lax.rem(lax.axis_index("col"), 2) == 1
    lane = lanes()
    slot = slots()
    at_edge = (lane < HALO) | (lane >= LANES - HALO)
    edge_new = []
    for base in range(0, nx, SUB):
        at = pl.ds(base, SUB)
        one, two = one_ref[at, :], two_ref[at, :]
        lower, upper = jnp.where(odd, one, two), jnp.where(odd, two, one)

        def joined(index, k, lane_by):
            own = edge_ref[index, at, :]
            if not k:
                return own
            where, end = beyond(slot, k, cols)
            got = turned(lower if k < 0 else upper, lane_by)
            return jnp.where(where & jnp.logical_not(end), got, own)

        lines = [
            {k: joined(len(REACH) * q + n, k, 3 * q + k - 3) for n, k in enumerate(REACH)}
            for q in range(5)
        ]
        gammas = {-1: joined(LINES, -1, 9), 0: joined(LINES + 1, 0, 0), 1: joined(LINES + 2, 1, 13)}
        cons = [edge_ref[LINES + 3 + f, at, :] for f in range(5)]
        edge_new.append(sweep_lines(cons, lines, gammas, 2))
    copies = []
    for f in range(5):
        for tile, new in enumerate(edge_new):
            for y in range(ny):
                edge = turned(new[f], GROUP * y + 6)
                at = pl.ds(tile * SUB * ny + own_row(y), SUB, stride=ny)
                rows_ref, start = (near_ref, y) if y < SPLIT else (far_ref, y - SPLIT)
                inner = rows_ref[f, pl.ds(start * nx + tile * SUB, SUB), :]
                held[f, at, :] = jnp.where(at_edge, edge, inner)
        copy = pltpu.make_async_copy(held.at[f], out_ref.at[f], sems.at[f])
        copy.start(priority=f % 2)
        copies.append(copy)
    for copy in copies:
        copy.wait()


def at_end(cols):
    col = lax.axis_index("col")
    return (col == 0) | (col == cols - 1)


def end_kernel(cols, near_ref, far_ref, edge_ref, one_ref, out_ref, held, sems):
    @pl.when(at_end(cols))
    def _():
        mend_edges(cols, near_ref, far_ref, edge_ref, one_ref, one_ref, out_ref, held, sems)


def middle_kernel(
    cols, ends_ref, near_ref, far_ref, edge_ref, one_ref, two_ref, out_ref, held, sems
):
    @pl.when(jnp.logical_not(at_end(cols)))
    def _():
        mend_edges(cols, near_ref, far_ref, edge_ref, one_ref, two_ref, out_ref, held, sems)


def swap_pairs(mesh, axis, inner):
    rows, cols = mesh.shape["row"], mesh.shape["col"]
    pairs = []
    for r in range(rows):
        for c in range(cols):
            k, n = (r, rows) if axis == "row" else (c, cols)
            if not inner:
                k ^= 1
            elif 0 < k < n - 1:
                k = ((k - 1) ^ 1) + 1
            else:
                k = None
            if axis == "row":
                to = (r, c ^ 1) if k is None else (k, c)
            else:
                to = (r, cols - 1 - c) if k is None else (r, k)
            pairs.append((r * cols + c, to[0] * cols + to[1]))
    return pairs


def body(mesh, state, gamma):
    rows, cols = mesh.shape["row"], mesh.shape["col"]
    _, nx, ny, nz = state.shape
    assert ny == SUB and nz == LANES and nx % SUB == 0 and rows % 2 == 0 and cols % 2 == 0
    here = lambda *dims: pltpu.VMEM(dims, jnp.float32)
    keep = lambda x: pltpu.with_memory_space_constraint(x, pltpu.VMEM)
    near = pl.BlockSpec(memory_space=pltpu.VMEM)
    swap = lambda x, axis, inner: lax.ppermute(x, ("row", "col"), swap_pairs(mesh, axis, inner))

    two = pl.pallas_call(
        raw_kernel,
        out_shape=here(6, HALO, nx, nz),
        in_specs=[pl.BlockSpec(memory_space=pltpu.HBM)] * 2,
        out_specs=near,
        scratch_shapes=[pltpu.SemaphoreType.DMA((HALO, 2))],
        name="raw_edges",
    )(state, gamma)
    two = swap(two, "row", True).reshape(6 * HALO, nx, nz)
    held = (keep(state.reshape(5, nx * ny, nz)), keep(gamma.reshape(nx * ny, nz)))
    one, rim = pl.pallas_call(
        edge_rows_kernel,
        out_shape=(here(5 * HALO + 1, nx, nz), here(2 * nx, nz)),
        in_specs=[near] * 2,
        out_specs=(near,) * 2,
        name="edge_rows",
    )(*held)
    swept = pl.pallas_call(
        first_kernel,
        out_shape=here(6, ny * nx, nz),
        in_specs=[near] * 2,
        out_specs=near,
        name="sweep_first",
    )(*held)
    rim = swap(rim, "row", False)
    one = swap(one, "row", False)
    near_rows, lower, upper, kept = pl.pallas_call(
        functools.partial(second_near, rows),
        out_shape=(here(5, SPLIT * nx, nz), here(nx, nz), here(nx, nz), here(KEPT, nx, nz)),
        in_specs=[near] * 2,
        out_specs=(near,) * 4,
        name="second_near",
    )(keep(swept), keep(two))
    far_shape = here(5, (ny - SPLIT) * nx, nz)
    rim_rows, to_one, to_two = pl.pallas_call(
        rim_kernel,
        out_shape=(far_shape, here(nx, nz), here(2 * nx, nz)),
        in_specs=[near] * 5,
        out_specs=(near,) * 3,
        cost_estimate=pl.CostEstimate(flops=10**9, bytes_accessed=0, transcendentals=0),
        name="second_rim",
    )(keep(swept), keep(rim), keep(lower), keep(upper), keep(kept))
    two = swap(to_two, "col", True)
    col_one = swap(to_one, "col", False)
    def third(first, rows_in):
        return pl.pallas_call(
            functools.partial(third_kernel, first),
            out_shape=here(*rows_in.shape),
            in_specs=[near] * 2,
            out_specs=near,
            name="third_far" if first else "third_near",
        )(keep(rows_in), keep(swept))

    inner_near = third(0, near_rows)
    edge = pl.pallas_call(
        functools.partial(window_kernel, cols),
        out_shape=here(EDGE_ARRAYS, nx, nz),
        in_specs=[near] * 3,
        out_specs=near,
        name="third_windows",
    )(keep(near_rows), keep(rim_rows), keep(swept))
    far_rows = pl.pallas_call(
        second_far,
        out_shape=far_shape,
        in_specs=[near] * 5,
        out_specs=near,
        name="second_far",
    )(keep(swept), keep(one), keep(kept), keep(inner_near), keep(edge))
    inner = (keep(inner_near), keep(third(SPLIT, far_rows)))
    far = pl.BlockSpec(memory_space=pltpu.HBM)
    whole = jax.ShapeDtypeStruct((5, nx * ny, nz), jnp.float32)
    scratch = [pltpu.VMEM(whole.shape, jnp.float32), pltpu.SemaphoreType.DMA((5,))]
    ends = pl.pallas_call(
        functools.partial(end_kernel, cols),
        out_shape=whole,
        in_specs=[near] * 4,
        out_specs=far,
        scratch_shapes=scratch,
        name="third_ends",
    )(*inner, keep(edge), keep(col_one))
    out = pl.pallas_call(
        functools.partial(middle_kernel, cols),
        out_shape=whole,
        in_specs=[far] + [near] * 5,
        out_specs=far,
        input_output_aliases={0: 0},
        scratch_shapes=scratch,
        name="third_middle",
    )(ends, *inner, keep(edge), keep(col_one), keep(two))
    return out.reshape(5, nx, ny, nz)


def solution(mesh):
    in_specs = (P(None, None, "row", "col"), P(None, "row", "col"))
    out_specs = P(None, None, "row", "col")
    return jax.shard_map(
        functools.partial(body, mesh),
        mesh=mesh,
        in_specs=in_specs,
        out_specs=out_specs,
        check_vma=False,
    )
```

```python
import functools

import jax
import jax.numpy as jnp
from jax import lax
from jax.experimental import pallas as pl
from jax.experimental.pallas import tpu as pltpu
from jax.sharding import PartitionSpec as P

STEP = 0.08
HALO = 3
SUB, LANES = 8, 128
GROUP_BITS = 4
GROUP = 1 << GROUP_BITS


def recip(x):
    r = pl.reciprocal(x, approx=True)
    return r * (2.0 - x * r)


def clamp_zero(u, v):
    return jnp.maximum(jnp.minimum(u, jnp.maximum(v, 0.0)), jnp.minimum(v, 0.0))


def primitives(cons, gam1, normal):
    rho, m0, m1, m2, energy = cons
    inv = recip(rho)
    vel = [m0 * inv, m1 * inv, m2 * inv]
    kinetic = 0.5 * (m0 * vel[0] + m1 * vel[1] + m2 * vel[2])
    pressure = gam1 * (energy - kinetic)
    others = [c for c in range(3) if c != normal]
    return [rho, vel[normal], vel[others[0]], vel[others[1]], pressure]


def face_rise(before, here, after):
    if here is None:
        return None
    rise = 0.5 * here
    if before is not None and after is not None:
        rise = rise + (before - after) * (1.0 / 12.0)
    elif before is not None:
        rise = rise + before * (1.0 / 12.0)
    elif after is not None:
        rise = rise - after * (1.0 / 12.0)
    return clamp_zero(rise, here)


def edges(q, right, left):
    if right is None or left is None:
        return q, q
    return q + clamp_zero(right, 2.0 * left), q - clamp_zero(left, 2.0 * right)


def state_flux(prim, gamma, inv_gam1):
    rho, un, u1, u2, p = prim
    mn, m1, m2 = rho * un, rho * u1, rho * u2
    nn = mn * un
    energy = p * inv_gam1 + 0.5 * (nn + m1 * u1 + m2 * u2)
    flux = [mn, nn + p, mn * u1, mn * u2, un * (energy + p)]
    gp = gamma * p
    speed = jnp.abs(un) + gp * lax.rsqrt(jnp.maximum(gp * rho, 1e-30))
    return [rho, mn, m1, m2, energy], flux, speed


def double_flux(left, right):
    if left is right:
        return [f + f for f in left[1]]
    speed = jnp.maximum(left[2], right[2])
    return [
        (left[1][k] + right[1][k]) - speed * (right[0][k] - left[0][k]) for k in range(5)
    ]


def place(normal):
    others = [c for c in range(3) if c != normal]
    return [0, 1 + normal, 1 + others[0], 1 + others[1], 4]


def updated(cons, flux_right, flux_left, normal):
    out = list(cons)
    for k, field in enumerate(place(normal)):
        out[field] = cons[field] - (0.5 * STEP) * (flux_right[k] - flux_left[k])
    return out


class Sweep:
    def __init__(self, n, normal, load, load_gamma, halo=None):
        self.n, self.normal = n, normal
        self.load, self.load_gamma, self.halo = load, load_gamma, halo
        self.cons, self.gam, self.prim, self.diff, self.rise, self.state = {}, {}, {}, {}, {}, {}
        self.flux = {}

    def zone(self, i):
        return i if self.halo else min(max(i, 0), self.n - 1)

    def get_gam(self, i):
        i = self.zone(i)
        if i not in self.gam:
            gamma = self.load_gamma(i)
            gam1 = gamma - 1.0
            self.gam[i] = (gamma, recip(gam1), gam1)
        return self.gam[i]

    def get_cons(self, i):
        if i not in self.cons:
            self.cons[i] = self.load(i)
        return self.cons[i]

    def get(self, i):
        i = self.zone(i)
        if i not in self.prim:
            if 0 <= i < self.n:
                self.prim[i] = primitives(self.get_cons(i), self.get_gam(i)[2], self.normal)
            else:
                self.prim[i] = self.halo(i)
        return self.prim[i]

    def get_diff(self, i):
        if i not in self.diff:
            a, b = self.get(i), self.get(i + 1)
            self.diff[i] = [None] * 5 if a is b else [y - x for x, y in zip(a, b)]
        return self.diff[i]

    def get_rise(self, i):
        if i not in self.rise:
            here = self.get_diff(i)
            right = [face_rise(*t) for t in zip(self.get_diff(i - 1), here, self.get_diff(i + 1))]
            self.rise[i] = (right, [None if r is None else h - r for h, r in zip(here, right)])
        return self.rise[i]

    def get_state(self, i, upper):
        i = self.zone(i)
        if (i, upper) not in self.state:
            q, right, left = self.get(i), self.get_rise(i)[0], self.get_rise(i - 1)[1]
            pairs = [edges(*t) for t in zip(q, right, left)]
            side = [p[0] if upper else p[1] for p in pairs]
            self.state[i, upper] = state_flux(side, *self.get_gam(i)[:2])
            if all(p[0] is p[1] for p in pairs):
                self.state[i, not upper] = self.state[i, upper]
        return self.state[i, upper]

    def face(self, i):
        if i in self.flux:
            return self.flux[i]
        if not self.halo and i < 0:
            return double_flux(self.get_state(0, True), self.get_state(0, True))
        if not self.halo and i == self.n - 1:
            return double_flux(self.get_state(i, True), self.get_state(i, True))
        return double_flux(self.get_state(i, True), self.get_state(i + 1, False))

    def run(self, zones, store, flux=None):
        flux = self.face(zones[0] - 1) if flux is None else flux
        for i in zones:
            before, flux = flux, self.face(i)
            store(i, updated(self.get_cons(i), flux, before, self.normal))
        return flux


def own_row(y):
    odd = lax.rem(lax.axis_index("row"), 2) == 1
    return jnp.where(odd, SUB - 1 - y, y)


def own_sign():
    return jnp.where(lax.rem(lax.axis_index("row"), 2) == 1, -1.0, 1.0)


def rows_at(y, base, nx):
    return pl.ds(pl.multiple_of(own_row(y) * nx + base, SUB), SUB)


def shifted(tiles, by, edge):
    sub = lax.broadcasted_iota(jnp.int32, (SUB, LANES), 0)
    turned_tiles = [pltpu.roll(tile, SUB - 1 if by == 1 else 1, 0) for tile in tiles]
    if by == 1:
        beyond_tiles = turned_tiles[1:] + [edge]
        return [jnp.where(sub == SUB - 1, b, a) for a, b in zip(turned_tiles, beyond_tiles)]
    beyond_tiles = [edge] + turned_tiles[:-1]
    return [jnp.where(sub == 0, b, a) for a, b in zip(turned_tiles, beyond_tiles)]


def sweep_sublanes(cons, gamma):
    gam1 = [g - 1.0 for g in gamma]
    inv_gam1 = [recip(g) for g in gam1]
    prim = [primitives(c, g, 0) for c, g in zip(cons, gam1)]
    upper, lower_next = [], []
    for q in zip(*prim):
        here = [b - a for a, b in zip(q, shifted(q, 1, q[-1]))]
        right = [face_rise(*d) for d in zip(shifted(here, -1, 0.0), here, shifted(here, 1, 0.0))]
        left = shifted([h - r for h, r in zip(here, right)], -1, 0.0)
        pairs = [edges(*t) for t in zip(q, right, left)]
        upper.append([p[0] for p in pairs])
        lower_next.append(shifted([p[1] for p in pairs], 1, q[-1]))
    gamma_next, inv_next = shifted(gamma, 1, gamma[-1]), shifted(inv_gam1, 1, inv_gam1[-1])
    flux = [
        double_flux(state_flux(u, g, i), state_flux(l, gn, i_n))
        for u, l, g, i, gn, i_n in zip(
            zip(*upper), zip(*lower_next), gamma, inv_gam1, gamma_next, inv_next
        )
    ]
    start = state_flux(prim[0], gamma[0], inv_gam1[0])
    start = double_flux(start, start)
    before = [shifted(list(f), -1, e) for f, e in zip(zip(*flux), start)]
    return [updated(c, f, b, 0) for c, f, b in zip(cons, flux, zip(*before))]


def raw_kernel(state_hbm, gamma_hbm, two_ref, sems):
    copies = []
    for j in range(HALO):
        row = own_row(j)
        copies.append(
            pltpu.make_async_copy(
                state_hbm.at[:, :, row, :], two_ref.at[pl.ds(0, 5), j], sems.at[j, 0]
            )
        )
        copies.append(pltpu.make_async_copy(gamma_hbm.at[:, row, :], two_ref.at[5, j], sems.at[j, 1]))
    for k, copy in enumerate(copies):
        copy.start(priority=k % 2)
    for copy in copies:
        copy.wait()


def edge_rows_kernel(state_ref, gamma_ref, one_ref, rim_ref):
    nx, ny = one_ref.shape[1], SUB
    tiles = range(0, nx, SUB)
    ends = [[None, None] for _ in tiles]

    def put(n, tile, value):
        one_ref[n, pl.ds(tile * SUB, SUB), :] = value
        ends[tile][n // SUB] = into_window(ends[tile][n // SUB], n % SUB, value)

    for j in range(HALO):
        row = own_row(ny - 1 - j)
        at = [pl.ds(base * ny + row, SUB, stride=ny) for base in tiles]
        gamma = [gamma_ref[rows, :] for rows in at]
        swept = sweep_sublanes([[state_ref[f, rows, :] for f in range(5)] for rows in at], gamma)
        for tile, (cons, g) in enumerate(zip(swept, gamma)):
            for k, value in enumerate(primitives(cons, g - 1.0, 1)):
                put(HALO * k + j, tile, value)
            if j == 0:
                put(5 * HALO, tile, g)
    for tile, base in enumerate(tiles):
        for n in range(2):
            rim_ref[pl.ds(n * nx + base, SUB), :] = ends[tile][n]


def first_kernel(state_ref, gamma_ref, swept_ref):
    ny = SUB
    nx = gamma_ref.shape[0] // ny

    def load_gamma(x):
        return gamma_ref[pl.ds(x * ny, ny), :]

    def store(x, cons):
        for f in range(5):
            swept_ref[f, pl.ds(x, ny, stride=nx), :] = cons[f]

    sweep = Sweep(
        nx, 0, lambda x: [state_ref[f, pl.ds(x * ny, ny), :] for f in range(5)], load_gamma
    )
    sweep.run(range(nx), store)
    for x in range(nx):
        swept_ref[5, pl.ds(x, ny, stride=nx), :] = load_gamma(x)


def row_loads(swept_ref, base, nx, sign):
    def load(y):
        row = rows_at(y, base, nx)
        cons = [swept_ref[f, row, :] for f in range(5)]
        cons[2] = cons[2] * sign
        return cons

    return load, lambda y: swept_ref[5, rows_at(y, base, nx), :]


def lanes():
    return lax.broadcasted_iota(jnp.int32, (SUB, LANES), 1)


def groups(by=0):
    return ((lanes() - by) & (LANES - 1)) >> GROUP_BITS


def slots(by=0):
    return (lanes() - by) & (GROUP - 1)


def into_window(window, y, value):
    turn = (GROUP * y + 6) % LANES
    rolled = pltpu.roll(value, turn, 1) if turn else value
    if window is None:
        return rolled
    return jnp.where(groups() == y, rolled, window)


class EdgePack:
    def __init__(self, lower=None, upper=None):
        self.pack = [lower, upper]

    def add(self, y, cons, gamma):
        prim = primitives(cons, gamma - 1.0, 2)
        rolls = [turned(p, -(GROUP * y + 3 * k + 3)) for k, p in enumerate(prim)]
        for side in range(2):
            slot, group = slots(3 * (1 - side)), groups(3 * (1 - side))
            value = turned(gamma, -(GROUP * y + (16 if side else 18)))
            for k in reversed(range(5)):
                value = jnp.where(slot < 3 * (k + 1), rolls[k], value)
            old = self.pack[side]
            self.pack[side] = value if old is None else jnp.where(group == y, value, old)


SPLIT = 5
INNER = 3


def far_arrays(sweep):
    cons, fluxes, speed = sweep.get_state(SPLIT, True)
    kept = [sweep.get(SPLIT + 1), sweep.get(SPLIT + 2), sweep.get_diff(SPLIT)]
    return sum(kept + [sweep.get_rise(SPLIT)[1], cons, fluxes, [speed], sweep.face(SPLIT - 1)], [])


def near_arrays(sweep):
    last = INNER - 1
    cons, fluxes, speed = sweep.get_state(last, False)
    kept = [sweep.get(last - 2), sweep.get(last - 1), sweep.get_diff(last - 2)]
    kept += [sweep.get_diff(last - 1), sweep.get_rise(last - 1)[0]]
    return sum(kept + [cons, fluxes, [speed], sweep.face(last)], [])


KEPT_FAR, KEPT_NEAR = 36, 41


def inner_kernel(swept_ref, next_ref, lower_ref, upper_ref, near_ref, far_ref):
    nx = swept_ref.shape[1] // SUB
    sign = own_sign()
    for base in range(0, nx, SUB):
        at = pl.ds(base, SUB)
        load, load_gamma = row_loads(swept_ref, base, nx, sign)
        pack = EdgePack()

        def store(y, cons):
            cons[2] = cons[2] * sign
            for f in range(5):
                next_ref[f, pl.ds((y - INNER) * nx + base, SUB), :] = cons[f]
            pack.add(y, cons, load_gamma(y))

        sweep = Sweep(SUB, 1, load, load_gamma, lambda y: None)
        for i in range(INNER - 1, SPLIT):
            sweep.flux[i] = sweep.face(i)
        sweep.run(range(INNER, SPLIT), store)
        lower_ref[at, :], upper_ref[at, :] = pack.pack
        for ref, kept in ((near_ref, near_arrays(sweep)), (far_ref, far_arrays(sweep))):
            assert len(kept) == ref.shape[0]
            for k, value in enumerate(kept):
                ref[k, at, :] = value


def second_near(
    rows,
    swept_ref,
    two_ref,
    inner_ref,
    lower_in,
    upper_in,
    kept_ref,
    ahead_ref,
    next_ref,
    lower_ref,
    upper_ref,
):
    nx = swept_ref.shape[1] // SUB
    row = lax.axis_index("row")
    end = (row == 0) | (row == rows - 1)
    sign = own_sign()
    tiles = [pl.ds(base, SUB) for base in range(0, nx, SUB)]
    halos = []
    for j in range(HALO):
        gamma = [two_ref[5 * HALO + j, tile, :] for tile in tiles]
        cons = [[two_ref[HALO * f + j, tile, :] for f in range(5)] for tile in tiles]
        swept = sweep_sublanes(cons, gamma)
        halos.append([primitives(c, g - 1.0, 1) for c, g in zip(swept, gamma)])
    for base in range(0, nx, SUB):
        at = pl.ds(base, SUB)
        load, load_own_gamma = row_loads(swept_ref, base, nx, sign)
        pack = EdgePack(lower_in[at, :], upper_in[at, :])
        kept = [kept_ref[k, at, :] for k in range(KEPT_NEAR)]

        def load_gamma(y):
            if y >= 0:
                return load_own_gamma(y)
            return jnp.where(end, load_own_gamma(0), two_ref[5 * HALO, at, :])

        def halo(y):
            got = list(halos[-1 - y][base // SUB])
            got[1] = got[1] * sign
            return [jnp.where(end, p, q) for p, q in zip(kept[0:5], got)]

        def store(y, cons):
            cons[2] = cons[2] * sign
            for f in range(5):
                next_ref[f, pl.ds(y * nx + base, SUB), :] = cons[f]
            pack.add(y, cons, load_own_gamma(y))

        last = INNER - 1
        sweep = Sweep(SUB, 1, load, load_gamma, halo)
        sweep.prim[last - 2], sweep.prim[last - 1] = kept[0:5], kept[5:10]
        sweep.diff[last - 2], sweep.diff[last - 1] = kept[10:15], kept[15:20]
        sweep.rise[last - 1] = (kept[20:25], None)
        sweep.state[last, False] = (kept[25:30], kept[30:35], kept[35])
        sweep.flux[last] = kept[36:41]
        sweep.run(range(INNER), store)
        lower_ref[at, :], upper_ref[at, :] = pack.pack
        for f in range(5):
            for y in range(SPLIT - INNER):
                at_row = pl.ds(y * nx + base, SUB)
                next_ref[f, pl.ds((y + INNER) * nx + base, SUB), :] = inner_ref[f, at_row, :]


def sweep_far(swept_ref, kept_ref, base, received, store):
    nx = swept_ref.shape[1] // SUB
    at = pl.ds(base, SUB)
    sign = own_sign()
    load, load_own_gamma = row_loads(swept_ref, base, nx, sign)

    def load_gamma(y):
        return load_own_gamma(y) if y < SUB else received(5 * HALO)

    def halo(y):
        got = [received(HALO * k + y - SUB) for k in range(5)]
        got[1] = got[1] * sign
        return got

    def signed_store(y, cons):
        cons[2] = cons[2] * sign
        store(y, cons, load_own_gamma(y))

    kept = [kept_ref[k, at, :] for k in range(KEPT_FAR)]
    sweep = Sweep(SUB, 1, load, load_gamma, halo)
    sweep.prim[SPLIT + 1], sweep.prim[SPLIT + 2] = kept[0:5], kept[5:10]
    sweep.diff[SPLIT] = kept[10:15]
    sweep.rise[SPLIT] = (None, kept[15:20])
    sweep.state[SPLIT, True] = (kept[20:25], kept[25:30], kept[30])
    sweep.run(range(SPLIT, SUB), signed_store, kept[31:36])


def rim_kernel(
    swept_ref, rim_ref, lower_ref, upper_ref, kept_ref, next_ref, to_one_ref, to_two_ref
):
    nx = swept_ref.shape[1] // SUB
    for base in range(0, nx, SUB):
        at = pl.ds(base, SUB)
        pack = EdgePack(lower_ref[at, :], upper_ref[at, :])

        def received(n):
            return turned(rim_ref[pl.ds(n // SUB * nx + base, SUB), :], GROUP * (n % SUB) + 6)

        def store(y, cons, gamma):
            for f in range(5):
                next_ref[f, pl.ds((y - SPLIT) * nx + base, SUB), :] = cons[f]
            pack.add(y, cons, gamma)

        sweep_far(swept_ref, kept_ref, base, received, store)
        lower, upper = pack.pack
        odd = lax.rem(lax.axis_index("col"), 2) == 1
        to_one_ref[at, :] = jnp.where(odd, lower, upper)
        to_two_ref[at, :] = jnp.where(odd, upper, lower)
        to_two_ref[pl.ds(nx + base, SUB), :] = lower


def second_far(swept_ref, one_ref, kept_ref, *others):
    next_ref = others[-1]
    nx = swept_ref.shape[1] // SUB
    for base in range(0, nx, SUB):

        def store(y, cons, gamma):
            for f in range(5):
                next_ref[f, pl.ds((y - SPLIT) * nx + base, SUB), :] = cons[f]

        sweep_far(swept_ref, kept_ref, base, lambda n: one_ref[n, pl.ds(base, SUB), :], store)


def turned(x, by):
    by %= LANES
    return pltpu.roll(x, LANES - by, 1) if by else x


def sweep_lanes(cons, prim, gamma, normal):
    inv_gam1 = recip(gamma - 1.0)
    upper, lower_next = [], []
    for q in prim:
        line = [turned(q, k) for k in range(-2, 4)]
        diff = [b - a for a, b in zip(line, line[1:])]
        rise = [face_rise(*diff[k : k + 3]) for k in range(3)]
        upper.append(q + clamp_zero(rise[1], 2.0 * (diff[1] - rise[0])))
        lower_next.append(line[3] - clamp_zero(diff[2] - rise[1], 2.0 * rise[2]))
    flux = double_flux(
        state_flux(upper, gamma, inv_gam1),
        state_flux(lower_next, turned(gamma, 1), turned(inv_gam1, 1)),
    )
    return updated(cons, flux, [turned(x, -1) for x in flux], normal)


def sweep_lines(cons, lines, gammas, normal):
    gam = {k: (g, recip(g - 1.0)) for k, g in gammas.items()}
    states = {key: [] for key in ((-1, 0), (0, 1), (0, 0), (1, 1))}
    for line in lines:
        diff = {k: line[k + 1] - line[k] for k in range(-3, 3)}
        rise = {k: face_rise(diff[k - 1], diff[k], diff[k + 1]) for k in range(-2, 2)}
        for k, which in states:
            right, left = rise[k], diff[k - 1] - rise[k - 1]
            if which == k + 1:
                states[k, which].append(line[k] + clamp_zero(right, 2.0 * left))
            else:
                states[k, which].append(line[k] - clamp_zero(left, 2.0 * right))
    side = {key: state_flux(prim, *gam[key[0]]) for key, prim in states.items()}
    before = double_flux(side[-1, 0], side[0, 0])
    after = double_flux(side[0, 1], side[1, 1])
    return updated(cons, after, before, normal)


REACH = range(-HALO, HALO + 1)
LINES = 5 * len(REACH)
EDGE_ARRAYS = LINES + 3 + 5


def beyond(slot, k, cols):
    col = lax.axis_index("col")
    if k < 0:
        return (slot >= 6) & (slot < 6 - k), col == 0
    return (slot >= 6 - k) & (slot < 6), col == cols - 1


def zone_loads(near_ref, far_ref, gamma_ref, base, nx):
    def load(y):
        rows_ref, start = (near_ref, y) if y < SPLIT else (far_ref, y - SPLIT)
        cons = [rows_ref[f, pl.ds(start * nx + base, SUB), :] for f in range(5)]
        gamma = gamma_ref[5, rows_at(y, base, nx), :]
        return cons, primitives(cons, gamma - 1.0, 2), gamma

    return load


def third_kernel(first, count, rows_ref, gamma_ref, out_ref):
    nx = gamma_ref.shape[1] // SUB
    for base in range(0, nx, SUB):
        for y in range(count):
            at = pl.ds(y * nx + base, SUB)
            cons = [rows_ref[f, at, :] for f in range(5)]
            gamma = gamma_ref[5, rows_at(first + y, base, nx), :]
            inner = sweep_lanes(cons, primitives(cons, gamma - 1.0, 2), gamma, 2)
            for f in range(5):
                out_ref[f, at, :] = inner[f]


def window_kernel(cols, near_ref, far_ref, gamma_ref, edge_ref):
    nx = edge_ref.shape[1]
    slot = slots()
    for base in range(0, nx, SUB):
        load = zone_loads(near_ref, far_ref, gamma_ref, base, nx)
        windows = [None] * 11
        for y in range(SUB):
            cons, prim, gamma = load(y)
            for k, value in enumerate(prim + [gamma] + cons):
                windows[k] = into_window(windows[k], y, value)
        at = pl.ds(base, SUB)
        for q, own in enumerate(windows[:6]):
            line = {k: turned(own, k) for k in (REACH if q < 5 else (-1, 0, 1))}
            for n, k in enumerate(line):
                value = line[k]
                if k:
                    where, end = beyond(slot, k, cols)
                    if abs(k) == 1:
                        last = own
                    elif k < 0:
                        last = jnp.where(slot == 6, own, jnp.where(slot == 7, line[-1], line[-2]))
                    else:
                        last = jnp.where(slot == 5, own, jnp.where(slot == 4, line[1], line[2]))
                    value = jnp.where(where & end, last, value)
                edge_ref[len(REACH) * q + n, at, :] = value
        for f in range(5):
            edge_ref[LINES + 3 + f, at, :] = windows[6 + f]


def mend_edges(cols, near_ref, inner_ref, far_ref, edge_ref, one_ref, two_ref, out_ref, held, sems):
    nx = edge_ref.shape[1]
    ny = SUB
    odd = lax.rem(lax.axis_index("col"), 2) == 1
    lane = lanes()
    slot = slots()
    at_edge = (lane < HALO) | (lane >= LANES - HALO)
    edge_new = []
    for base in range(0, nx, SUB):
        at = pl.ds(base, SUB)
        one, two = one_ref[at, :], two_ref[at, :]
        lower, upper = jnp.where(odd, one, two), jnp.where(odd, two, one)

        def joined(index, k, lane_by):
            own = edge_ref[index, at, :]
            if not k:
                return own
            where, end = beyond(slot, k, cols)
            got = turned(lower if k < 0 else upper, lane_by)
            return jnp.where(where & jnp.logical_not(end), got, own)

        lines = [
            {k: joined(len(REACH) * q + n, k, 3 * q + k - 3) for n, k in enumerate(REACH)}
            for q in range(5)
        ]
        gammas = {-1: joined(LINES, -1, 9), 0: joined(LINES + 1, 0, 0), 1: joined(LINES + 2, 1, 13)}
        cons = [edge_ref[LINES + 3 + f, at, :] for f in range(5)]
        edge_new.append(sweep_lines(cons, lines, gammas, 2))
    copies = []
    for f in range(5):
        for tile, new in enumerate(edge_new):
            for y in range(ny):
                edge = turned(new[f], GROUP * y + 6)
                at = pl.ds(tile * SUB * ny + own_row(y), SUB, stride=ny)
                if y < INNER:
                    rows_ref, start = near_ref, y
                elif y < SPLIT:
                    rows_ref, start = inner_ref, y - INNER
                else:
                    rows_ref, start = far_ref, y - SPLIT
                inner = rows_ref[f, pl.ds(start * nx + tile * SUB, SUB), :]
                held[f, at, :] = jnp.where(at_edge, edge, inner)
        copy = pltpu.make_async_copy(held.at[f], out_ref.at[f], sems.at[f])
        copy.start(priority=f % 2)
        copies.append(copy)
    for copy in copies:
        copy.wait()


def at_end(cols):
    col = lax.axis_index("col")
    return (col == 0) | (col == cols - 1)


def end_kernel(cols, near_ref, inner_ref, far_ref, edge_ref, one_ref, out_ref, held, sems):
    @pl.when(at_end(cols))
    def _():
        mend_edges(
            cols, near_ref, inner_ref, far_ref, edge_ref, one_ref, one_ref, out_ref, held, sems
        )


def middle_kernel(
    cols, ends_ref, near_ref, inner_ref, far_ref, edge_ref, one_ref, two_ref, out_ref, held, sems
):
    @pl.when(jnp.logical_not(at_end(cols)))
    def _():
        mend_edges(
            cols, near_ref, inner_ref, far_ref, edge_ref, one_ref, two_ref, out_ref, held, sems
        )


def swap_pairs(mesh, axis, inner):
    rows, cols = mesh.shape["row"], mesh.shape["col"]
    pairs = []
    for r in range(rows):
        for c in range(cols):
            k, n = (r, rows) if axis == "row" else (c, cols)
            if not inner:
                k ^= 1
            elif 0 < k < n - 1:
                k = ((k - 1) ^ 1) + 1
            else:
                k = None
            if axis == "row":
                to = (r, c ^ 1) if k is None else (k, c)
            else:
                to = (r, cols - 1 - c) if k is None else (r, k)
            pairs.append((r * cols + c, to[0] * cols + to[1]))
    return pairs


def body(mesh, state, gamma):
    rows, cols = mesh.shape["row"], mesh.shape["col"]
    _, nx, ny, nz = state.shape
    assert ny == SUB and nz == LANES and nx % SUB == 0 and rows % 2 == 0 and cols % 2 == 0
    here = lambda *dims: pltpu.VMEM(dims, jnp.float32)
    keep = lambda x: pltpu.with_memory_space_constraint(x, pltpu.VMEM)
    near = pl.BlockSpec(memory_space=pltpu.VMEM)
    swap = lambda x, axis, inner: lax.ppermute(x, ("row", "col"), swap_pairs(mesh, axis, inner))

    two = pl.pallas_call(
        raw_kernel,
        out_shape=here(6, HALO, nx, nz),
        in_specs=[pl.BlockSpec(memory_space=pltpu.HBM)] * 2,
        out_specs=near,
        scratch_shapes=[pltpu.SemaphoreType.DMA((HALO, 2))],
        name="raw_edges",
    )(state, gamma)
    two = swap(two, "row", True).reshape(6 * HALO, nx, nz)
    held = (keep(state.reshape(5, nx * ny, nz)), keep(gamma.reshape(nx * ny, nz)))
    one, rim = pl.pallas_call(
        edge_rows_kernel,
        out_shape=(here(5 * HALO + 1, nx, nz), here(2 * nx, nz)),
        in_specs=[near] * 2,
        out_specs=(near,) * 2,
        name="edge_rows",
    )(*held)
    swept = pl.pallas_call(
        first_kernel,
        out_shape=here(6, ny * nx, nz),
        in_specs=[near] * 2,
        out_specs=near,
        name="sweep_first",
    )(*held)
    rim = swap(rim, "row", False)
    one = swap(one, "row", False)
    inner_rows, lower, upper, kept_near, kept = pl.pallas_call(
        inner_kernel,
        out_shape=(
            here(5, (SPLIT - INNER) * nx, nz),
            here(nx, nz),
            here(nx, nz),
            here(KEPT_NEAR, nx, nz),
            here(KEPT_FAR, nx, nz),
        ),
        in_specs=[near],
        out_specs=(near,) * 5,
        name="second_inner",
    )(keep(swept))

    def third(first, count, rows_in, name):
        return pl.pallas_call(
            functools.partial(third_kernel, first, count),
            out_shape=here(5, count * nx, nz),
            in_specs=[near] * 2,
            out_specs=near,
            name=name,
        )(keep(rows_in), keep(swept))

    inner_z = third(INNER, SPLIT - INNER, inner_rows, "third_inner")
    near_rows, lower, upper = pl.pallas_call(
        functools.partial(second_near, rows),
        out_shape=(here(5, SPLIT * nx, nz), here(nx, nz), here(nx, nz)),
        in_specs=[near] * 7,
        out_specs=(near,) * 3,
        name="second_near",
    )(
        keep(swept),
        keep(two),
        keep(inner_rows),
        keep(lower),
        keep(upper),
        keep(kept_near),
        keep(inner_z),
    )
    far_shape = here(5, (ny - SPLIT) * nx, nz)
    rim_rows, to_one, to_two = pl.pallas_call(
        rim_kernel,
        out_shape=(far_shape, here(nx, nz), here(2 * nx, nz)),
        in_specs=[near] * 5,
        out_specs=(near,) * 3,
        cost_estimate=pl.CostEstimate(flops=10**9, bytes_accessed=0, transcendentals=0),
        name="second_rim",
    )(keep(swept), keep(rim), keep(lower), keep(upper), keep(kept))
    two = swap(to_two, "col", True)
    col_one = swap(to_one, "col", False)
    inner_near = third(0, INNER, near_rows, "third_near")
    edge = pl.pallas_call(
        functools.partial(window_kernel, cols),
        out_shape=here(EDGE_ARRAYS, nx, nz),
        in_specs=[near] * 3,
        out_specs=near,
        name="third_windows",
    )(keep(near_rows), keep(rim_rows), keep(swept))
    far_rows = pl.pallas_call(
        second_far,
        out_shape=far_shape,
        in_specs=[near] * 5,
        out_specs=near,
        name="second_far",
    )(keep(swept), keep(one), keep(kept), keep(inner_near), keep(edge))
    inner = (keep(inner_near), keep(inner_z), keep(third(SPLIT, ny - SPLIT, far_rows, "third_far")))
    far = pl.BlockSpec(memory_space=pltpu.HBM)
    whole = jax.ShapeDtypeStruct((5, nx * ny, nz), jnp.float32)
    scratch = [pltpu.VMEM(whole.shape, jnp.float32), pltpu.SemaphoreType.DMA((5,))]
    ends = pl.pallas_call(
        functools.partial(end_kernel, cols),
        out_shape=whole,
        in_specs=[near] * 5,
        out_specs=far,
        scratch_shapes=scratch,
        name="third_ends",
    )(*inner, keep(edge), keep(col_one))
    out = pl.pallas_call(
        functools.partial(middle_kernel, cols),
        out_shape=whole,
        in_specs=[far] + [near] * 6,
        out_specs=far,
        input_output_aliases={0: 0},
        scratch_shapes=scratch,
        name="third_middle",
    )(ends, *inner, keep(edge), keep(col_one), keep(two))
    return out.reshape(5, nx, ny, nz)


def solution(mesh):
    in_specs = (P(None, None, "row", "col"), P(None, "row", "col"))
    out_specs = P(None, None, "row", "col")
    return jax.shard_map(
        functools.partial(body, mesh),
        mesh=mesh,
        in_specs=in_specs,
        out_specs=out_specs,
        check_vma=False,
    )
```

```python
import functools

import jax
import jax.numpy as jnp
from jax import lax
from jax.experimental import pallas as pl
from jax.experimental.pallas import tpu as pltpu
from jax.sharding import PartitionSpec as P

STEP = 0.08
HALO = 3
SUB, LANES = 8, 128
GROUP_BITS = 4
GROUP = 1 << GROUP_BITS


def recip(x):
    r = pl.reciprocal(x, approx=True)
    return r * (2.0 - x * r)


def clamp_zero(u, v):
    return jnp.maximum(jnp.minimum(u, jnp.maximum(v, 0.0)), jnp.minimum(v, 0.0))


def primitives(cons, gam1, normal):
    rho, m0, m1, m2, energy = cons
    inv = recip(rho)
    vel = [m0 * inv, m1 * inv, m2 * inv]
    kinetic = 0.5 * (m0 * vel[0] + m1 * vel[1] + m2 * vel[2])
    pressure = gam1 * (energy - kinetic)
    others = [c for c in range(3) if c != normal]
    return [rho, vel[normal], vel[others[0]], vel[others[1]], pressure]


def face_rise(before, here, after):
    if here is None:
        return None
    rise = 0.5 * here
    if before is not None and after is not None:
        rise = rise + (before - after) * (1.0 / 12.0)
    elif before is not None:
        rise = rise + before * (1.0 / 12.0)
    elif after is not None:
        rise = rise - after * (1.0 / 12.0)
    return clamp_zero(rise, here)


def edges(q, right, left):
    if right is None or left is None:
        return q, q
    return q + clamp_zero(right, 2.0 * left), q - clamp_zero(left, 2.0 * right)


def state_flux(prim, gamma, inv_gam1):
    rho, un, u1, u2, p = prim
    mn, m1, m2 = rho * un, rho * u1, rho * u2
    nn = mn * un
    energy = p * inv_gam1 + 0.5 * (nn + m1 * u1 + m2 * u2)
    flux = [mn, nn + p, mn * u1, mn * u2, un * (energy + p)]
    gp = gamma * p
    speed = jnp.abs(un) + gp * lax.rsqrt(jnp.maximum(gp * rho, 1e-30))
    return [rho, mn, m1, m2, energy], flux, speed


def double_flux(left, right):
    if left is right:
        return [f + f for f in left[1]]
    speed = jnp.maximum(left[2], right[2])
    return [
        (left[1][k] + right[1][k]) - speed * (right[0][k] - left[0][k]) for k in range(5)
    ]


def place(normal):
    others = [c for c in range(3) if c != normal]
    return [0, 1 + normal, 1 + others[0], 1 + others[1], 4]


def updated(cons, flux_right, flux_left, normal):
    out = list(cons)
    for k, field in enumerate(place(normal)):
        out[field] = cons[field] - (0.5 * STEP) * (flux_right[k] - flux_left[k])
    return out


class Sweep:
    def __init__(self, n, normal, load, load_gamma, halo=None):
        self.n, self.normal = n, normal
        self.load, self.load_gamma, self.halo = load, load_gamma, halo
        self.cons, self.gam, self.prim, self.diff, self.rise, self.state = {}, {}, {}, {}, {}, {}
        self.flux = {}

    def zone(self, i):
        return i if self.halo else min(max(i, 0), self.n - 1)

    def get_gam(self, i):
        i = self.zone(i)
        if i not in self.gam:
            gamma = self.load_gamma(i)
            gam1 = gamma - 1.0
            self.gam[i] = (gamma, recip(gam1), gam1)
        return self.gam[i]

    def get_cons(self, i):
        if i not in self.cons:
            self.cons[i] = self.load(i)
        return self.cons[i]

    def get(self, i):
        i = self.zone(i)
        if i not in self.prim:
            if 0 <= i < self.n:
                self.prim[i] = primitives(self.get_cons(i), self.get_gam(i)[2], self.normal)
            else:
                self.prim[i] = self.halo(i)
        return self.prim[i]

    def get_diff(self, i):
        if i not in self.diff:
            a, b = self.get(i), self.get(i + 1)
            self.diff[i] = [None] * 5 if a is b else [y - x for x, y in zip(a, b)]
        return self.diff[i]

    def get_rise(self, i):
        if i not in self.rise:
            here = self.get_diff(i)
            right = [face_rise(*t) for t in zip(self.get_diff(i - 1), here, self.get_diff(i + 1))]
            self.rise[i] = (right, [None if r is None else h - r for h, r in zip(here, right)])
        return self.rise[i]

    def get_state(self, i, upper):
        i = self.zone(i)
        if (i, upper) not in self.state:
            q, right, left = self.get(i), self.get_rise(i)[0], self.get_rise(i - 1)[1]
            pairs = [edges(*t) for t in zip(q, right, left)]
            side = [p[0] if upper else p[1] for p in pairs]
            self.state[i, upper] = state_flux(side, *self.get_gam(i)[:2])
            if all(p[0] is p[1] for p in pairs):
                self.state[i, not upper] = self.state[i, upper]
        return self.state[i, upper]

    def face(self, i):
        if i in self.flux:
            return self.flux[i]
        if not self.halo and i < 0:
            return double_flux(self.get_state(0, True), self.get_state(0, True))
        if not self.halo and i == self.n - 1:
            return double_flux(self.get_state(i, True), self.get_state(i, True))
        return double_flux(self.get_state(i, True), self.get_state(i + 1, False))

    def run(self, zones, store, flux=None):
        flux = self.face(zones[0] - 1) if flux is None else flux
        for i in zones:
            before, flux = flux, self.face(i)
            store(i, updated(self.get_cons(i), flux, before, self.normal))
        return flux


def own_row(y):
    odd = lax.rem(lax.axis_index("row"), 2) == 1
    return jnp.where(odd, SUB - 1 - y, y)


def own_sign():
    return jnp.where(lax.rem(lax.axis_index("row"), 2) == 1, -1.0, 1.0)


def rows_at(y, base, nx):
    return pl.ds(pl.multiple_of(own_row(y) * nx + base, SUB), SUB)


def shifted(tiles, by, edge):
    sub = lax.broadcasted_iota(jnp.int32, (SUB, LANES), 0)
    turned_tiles = [pltpu.roll(tile, SUB - 1 if by == 1 else 1, 0) for tile in tiles]
    if by == 1:
        beyond_tiles = turned_tiles[1:] + [edge]
        return [jnp.where(sub == SUB - 1, b, a) for a, b in zip(turned_tiles, beyond_tiles)]
    beyond_tiles = [edge] + turned_tiles[:-1]
    return [jnp.where(sub == 0, b, a) for a, b in zip(turned_tiles, beyond_tiles)]


def sweep_sublanes(cons, gamma):
    gam1 = [g - 1.0 for g in gamma]
    inv_gam1 = [recip(g) for g in gam1]
    prim = [primitives(c, g, 0) for c, g in zip(cons, gam1)]
    upper, lower_next = [], []
    for q in zip(*prim):
        here = [b - a for a, b in zip(q, shifted(q, 1, q[-1]))]
        right = [face_rise(*d) for d in zip(shifted(here, -1, 0.0), here, shifted(here, 1, 0.0))]
        left = shifted([h - r for h, r in zip(here, right)], -1, 0.0)
        pairs = [edges(*t) for t in zip(q, right, left)]
        upper.append([p[0] for p in pairs])
        lower_next.append(shifted([p[1] for p in pairs], 1, q[-1]))
    gamma_next, inv_next = shifted(gamma, 1, gamma[-1]), shifted(inv_gam1, 1, inv_gam1[-1])
    flux = [
        double_flux(state_flux(u, g, i), state_flux(l, gn, i_n))
        for u, l, g, i, gn, i_n in zip(
            zip(*upper), zip(*lower_next), gamma, inv_gam1, gamma_next, inv_next
        )
    ]
    start = state_flux(prim[0], gamma[0], inv_gam1[0])
    start = double_flux(start, start)
    before = [shifted(list(f), -1, e) for f, e in zip(zip(*flux), start)]
    return [updated(c, f, b, 0) for c, f, b in zip(cons, flux, zip(*before))]


def raw_kernel(state_hbm, gamma_hbm, two_ref, sems):
    copies = []
    for j in range(HALO):
        row = own_row(j)
        copies.append(
            pltpu.make_async_copy(
                state_hbm.at[:, :, row, :], two_ref.at[pl.ds(0, 5), j], sems.at[j, 0]
            )
        )
        copies.append(pltpu.make_async_copy(gamma_hbm.at[:, row, :], two_ref.at[5, j], sems.at[j, 1]))
    for k, copy in enumerate(copies):
        copy.start(priority=k % 2)
    for copy in copies:
        copy.wait()


def edge_rows_kernel(state_ref, gamma_ref, one_ref, rim_ref):
    nx, ny = one_ref.shape[1], SUB
    tiles = range(0, nx, SUB)
    ends = [[None, None] for _ in tiles]

    def put(n, tile, value):
        one_ref[n, pl.ds(tile * SUB, SUB), :] = value
        ends[tile][n // SUB] = into_window(ends[tile][n // SUB], n % SUB, value)

    for j in range(HALO):
        row = own_row(ny - 1 - j)
        at = [pl.ds(base * ny + row, SUB, stride=ny) for base in tiles]
        gamma = [gamma_ref[rows, :] for rows in at]
        swept = sweep_sublanes([[state_ref[f, rows, :] for f in range(5)] for rows in at], gamma)
        for tile, (cons, g) in enumerate(zip(swept, gamma)):
            for k, value in enumerate(primitives(cons, g - 1.0, 1)):
                put(HALO * k + j, tile, value)
            if j == 0:
                put(5 * HALO, tile, g)
    for tile, base in enumerate(tiles):
        for n in range(2):
            rim_ref[pl.ds(n * nx + base, SUB), :] = ends[tile][n]


def first_kernel(state_ref, gamma_ref, swept_ref):
    ny = SUB
    nx = gamma_ref.shape[0] // ny

    def load_gamma(x):
        return gamma_ref[pl.ds(x * ny, ny), :]

    def store(x, cons):
        for f in range(5):
            swept_ref[f, pl.ds(x, ny, stride=nx), :] = cons[f]

    sweep = Sweep(
        nx, 0, lambda x: [state_ref[f, pl.ds(x * ny, ny), :] for f in range(5)], load_gamma
    )
    sweep.run(range(nx), store)
    for x in range(nx):
        swept_ref[5, pl.ds(x, ny, stride=nx), :] = load_gamma(x)


def row_loads(swept_ref, base, nx, sign):
    def load(y):
        row = rows_at(y, base, nx)
        cons = [swept_ref[f, row, :] for f in range(5)]
        cons[2] = cons[2] * sign
        return cons

    return load, lambda y: swept_ref[5, rows_at(y, base, nx), :]


def lanes():
    return lax.broadcasted_iota(jnp.int32, (SUB, LANES), 1)


def groups(by=0):
    return ((lanes() - by) & (LANES - 1)) >> GROUP_BITS


def slots(by=0):
    return (lanes() - by) & (GROUP - 1)


def into_window(window, y, value):
    turn = (GROUP * y + 6) % LANES
    rolled = pltpu.roll(value, turn, 1) if turn else value
    if window is None:
        return rolled
    return jnp.where(groups() == y, rolled, window)


class EdgePack:
    def __init__(self, lower=None, upper=None):
        self.pack = [lower, upper]

    def add(self, y, cons, gamma):
        prim = primitives(cons, gamma - 1.0, 2)
        rolls = [turned(p, -(GROUP * y + 3 * k + 3)) for k, p in enumerate(prim)]
        for side in range(2):
            slot, group = slots(3 * (1 - side)), groups(3 * (1 - side))
            value = turned(gamma, -(GROUP * y + (16 if side else 18)))
            for k in reversed(range(5)):
                value = jnp.where(slot < 3 * (k + 1), rolls[k], value)
            old = self.pack[side]
            self.pack[side] = value if old is None else jnp.where(group == y, value, old)


SPLIT = 5
INNER = 3


def far_arrays(sweep):
    cons, fluxes, speed = sweep.get_state(SPLIT, True)
    kept = [sweep.get(SPLIT + 1), sweep.get(SPLIT + 2), sweep.get_diff(SPLIT)]
    return sum(kept + [sweep.get_rise(SPLIT)[1], cons, fluxes, [speed], sweep.face(SPLIT - 1)], [])


def near_arrays(sweep):
    last = INNER - 1
    cons, fluxes, speed = sweep.get_state(last, False)
    kept = [sweep.get(last - 2), sweep.get(last - 1), sweep.get_diff(last - 2)]
    kept += [sweep.get_diff(last - 1), sweep.get_rise(last - 1)[0]]
    return sum(kept + [cons, fluxes, [speed], sweep.face(last)], [])


KEPT_FAR, KEPT_NEAR = 36, 41


def inner_kernel(swept_ref, next_ref, lower_ref, upper_ref, near_ref, far_ref):
    nx = swept_ref.shape[1] // SUB
    sign = own_sign()
    for base in range(0, nx, SUB):
        at = pl.ds(base, SUB)
        load, load_gamma = row_loads(swept_ref, base, nx, sign)
        pack = EdgePack()

        def store(y, cons):
            cons[2] = cons[2] * sign
            for f in range(5):
                next_ref[f, pl.ds((y - INNER) * nx + base, SUB), :] = cons[f]
            pack.add(y, cons, load_gamma(y))

        sweep = Sweep(SUB, 1, load, load_gamma, lambda y: None)
        for i in range(INNER - 1, SPLIT):
            sweep.flux[i] = sweep.face(i)
        sweep.run(range(INNER, SPLIT), store)
        lower_ref[at, :], upper_ref[at, :] = pack.pack
        for ref, kept in ((near_ref, near_arrays(sweep)), (far_ref, far_arrays(sweep))):
            assert len(kept) == ref.shape[0]
            for k, value in enumerate(kept):
                ref[k, at, :] = value


def second_near(
    rows,
    swept_ref,
    two_ref,
    inner_ref,
    lower_in,
    upper_in,
    kept_ref,
    ahead_ref,
    next_ref,
    lower_ref,
    upper_ref,
):
    nx = swept_ref.shape[1] // SUB
    row = lax.axis_index("row")
    end = (row == 0) | (row == rows - 1)
    sign = own_sign()
    tiles = [pl.ds(base, SUB) for base in range(0, nx, SUB)]
    halos = []
    for j in range(HALO):
        gamma = [two_ref[5 * HALO + j, tile, :] for tile in tiles]
        cons = [[two_ref[HALO * f + j, tile, :] for f in range(5)] for tile in tiles]
        swept = sweep_sublanes(cons, gamma)
        halos.append([primitives(c, g - 1.0, 1) for c, g in zip(swept, gamma)])
    for base in range(0, nx, SUB):
        at = pl.ds(base, SUB)
        load, load_own_gamma = row_loads(swept_ref, base, nx, sign)
        pack = EdgePack(lower_in[at, :], upper_in[at, :])
        kept = [kept_ref[k, at, :] for k in range(KEPT_NEAR)]

        def load_gamma(y):
            if y >= 0:
                return load_own_gamma(y)
            return jnp.where(end, load_own_gamma(0), two_ref[5 * HALO, at, :])

        def halo(y):
            got = list(halos[-1 - y][base // SUB])
            got[1] = got[1] * sign
            return [jnp.where(end, p, q) for p, q in zip(kept[0:5], got)]

        def store(y, cons):
            cons[2] = cons[2] * sign
            for f in range(5):
                next_ref[f, pl.ds(y * nx + base, SUB), :] = cons[f]
            pack.add(y, cons, load_own_gamma(y))

        last = INNER - 1
        sweep = Sweep(SUB, 1, load, load_gamma, halo)
        sweep.prim[last - 2], sweep.prim[last - 1] = kept[0:5], kept[5:10]
        sweep.diff[last - 2], sweep.diff[last - 1] = kept[10:15], kept[15:20]
        sweep.rise[last - 1] = (kept[20:25], None)
        sweep.state[last, False] = (kept[25:30], kept[30:35], kept[35])
        sweep.flux[last] = kept[36:41]
        sweep.run(range(INNER), store)
        lower_ref[at, :], upper_ref[at, :] = pack.pack
        for f in range(5):
            for y in range(SPLIT - INNER):
                at_row = pl.ds(y * nx + base, SUB)
                next_ref[f, pl.ds((y + INNER) * nx + base, SUB), :] = inner_ref[f, at_row, :]


def sweep_far(swept_ref, kept_ref, base, received, store):
    nx = swept_ref.shape[1] // SUB
    at = pl.ds(base, SUB)
    sign = own_sign()
    load, load_own_gamma = row_loads(swept_ref, base, nx, sign)

    def load_gamma(y):
        return load_own_gamma(y) if y < SUB else received(5 * HALO)

    def halo(y):
        got = [received(HALO * k + y - SUB) for k in range(5)]
        got[1] = got[1] * sign
        return got

    def signed_store(y, cons):
        cons[2] = cons[2] * sign
        store(y, cons, load_own_gamma(y))

    kept = [kept_ref[k, at, :] for k in range(KEPT_FAR)]
    sweep = Sweep(SUB, 1, load, load_gamma, halo)
    sweep.prim[SPLIT + 1], sweep.prim[SPLIT + 2] = kept[0:5], kept[5:10]
    sweep.diff[SPLIT] = kept[10:15]
    sweep.rise[SPLIT] = (None, kept[15:20])
    sweep.state[SPLIT, True] = (kept[20:25], kept[25:30], kept[30])
    sweep.run(range(SPLIT, SUB), signed_store, kept[31:36])


def rim_kernel(
    swept_ref, rim_ref, lower_ref, upper_ref, kept_ref, next_ref, to_one_ref, to_two_ref
):
    nx = swept_ref.shape[1] // SUB
    for base in range(0, nx, SUB):
        at = pl.ds(base, SUB)
        pack = EdgePack(lower_ref[at, :], upper_ref[at, :])

        def received(n):
            return turned(rim_ref[pl.ds(n // SUB * nx + base, SUB), :], GROUP * (n % SUB) + 6)

        def store(y, cons, gamma):
            for f in range(5):
                next_ref[f, pl.ds((y - SPLIT) * nx + base, SUB), :] = cons[f]
            pack.add(y, cons, gamma)

        sweep_far(swept_ref, kept_ref, base, received, store)
        lower, upper = pack.pack
        odd = lax.rem(lax.axis_index("col"), 2) == 1
        to_one_ref[at, :] = jnp.where(odd, lower, upper)
        to_two_ref[at, :] = jnp.where(odd, upper, lower)
        to_two_ref[pl.ds(nx + base, SUB), :] = lower


def second_far(swept_ref, one_ref, kept_ref, *others):
    next_ref = others[-1]
    nx = swept_ref.shape[1] // SUB
    for base in range(0, nx, SUB):

        def store(y, cons, gamma):
            inner = sweep_lanes(cons, primitives(cons, gamma - 1.0, 2), gamma, 2)
            for f in range(5):
                next_ref[f, pl.ds((y - SPLIT) * nx + base, SUB), :] = inner[f]

        sweep_far(swept_ref, kept_ref, base, lambda n: one_ref[n, pl.ds(base, SUB), :], store)


def turned(x, by):
    by %= LANES
    return pltpu.roll(x, LANES - by, 1) if by else x


def sweep_lanes(cons, prim, gamma, normal):
    inv_gam1 = recip(gamma - 1.0)
    upper, lower_next = [], []
    for q in prim:
        line = [turned(q, k) for k in range(-2, 4)]
        diff = [b - a for a, b in zip(line, line[1:])]
        rise = [face_rise(*diff[k : k + 3]) for k in range(3)]
        upper.append(q + clamp_zero(rise[1], 2.0 * (diff[1] - rise[0])))
        lower_next.append(line[3] - clamp_zero(diff[2] - rise[1], 2.0 * rise[2]))
    flux = double_flux(
        state_flux(upper, gamma, inv_gam1),
        state_flux(lower_next, turned(gamma, 1), turned(inv_gam1, 1)),
    )
    return updated(cons, flux, [turned(x, -1) for x in flux], normal)


def sweep_lines(cons, lines, gammas, normal):
    gam = {k: (g, recip(g - 1.0)) for k, g in gammas.items()}
    states = {key: [] for key in ((-1, 0), (0, 1), (0, 0), (1, 1))}
    for line in lines:
        diff = {k: line[k + 1] - line[k] for k in range(-3, 3)}
        rise = {k: face_rise(diff[k - 1], diff[k], diff[k + 1]) for k in range(-2, 2)}
        for k, which in states:
            right, left = rise[k], diff[k - 1] - rise[k - 1]
            if which == k + 1:
                states[k, which].append(line[k] + clamp_zero(right, 2.0 * left))
            else:
                states[k, which].append(line[k] - clamp_zero(left, 2.0 * right))
    side = {key: state_flux(prim, *gam[key[0]]) for key, prim in states.items()}
    before = double_flux(side[-1, 0], side[0, 0])
    after = double_flux(side[0, 1], side[1, 1])
    return updated(cons, after, before, normal)


REACH = range(-HALO, HALO + 1)
LINES = 5 * len(REACH)
EDGE_ARRAYS = LINES + 3 + 5


def beyond(slot, k, cols):
    col = lax.axis_index("col")
    if k < 0:
        return (slot >= 6) & (slot < 6 - k), col == 0
    return (slot >= 6 - k) & (slot < 6), col == cols - 1


def zone_loads(near_ref, far_ref, gamma_ref, base, nx):
    def load(y):
        rows_ref, start = (near_ref, y) if y < SPLIT else (far_ref, y - SPLIT)
        cons = [rows_ref[f, pl.ds(start * nx + base, SUB), :] for f in range(5)]
        gamma = gamma_ref[5, rows_at(y, base, nx), :]
        return cons, primitives(cons, gamma - 1.0, 2), gamma

    return load


def third_kernel(first, count, rows_ref, gamma_ref, out_ref):
    nx = gamma_ref.shape[1] // SUB
    for base in range(0, nx, SUB):
        for y in range(count):
            at = pl.ds(y * nx + base, SUB)
            cons = [rows_ref[f, at, :] for f in range(5)]
            gamma = gamma_ref[5, rows_at(first + y, base, nx), :]
            inner = sweep_lanes(cons, primitives(cons, gamma - 1.0, 2), gamma, 2)
            for f in range(5):
                out_ref[f, at, :] = inner[f]


def window_kernel(cols, near_ref, far_ref, gamma_ref, edge_ref):
    nx = edge_ref.shape[1]
    slot = slots()
    for base in range(0, nx, SUB):
        load = zone_loads(near_ref, far_ref, gamma_ref, base, nx)
        windows = [None] * 11
        for y in range(SUB):
            cons, prim, gamma = load(y)
            for k, value in enumerate(prim + [gamma] + cons):
                windows[k] = into_window(windows[k], y, value)
        at = pl.ds(base, SUB)
        for q, own in enumerate(windows[:6]):
            line = {k: turned(own, k) for k in (REACH if q < 5 else (-1, 0, 1))}
            for n, k in enumerate(line):
                value = line[k]
                if k:
                    where, end = beyond(slot, k, cols)
                    if abs(k) == 1:
                        last = own
                    elif k < 0:
                        last = jnp.where(slot == 6, own, jnp.where(slot == 7, line[-1], line[-2]))
                    else:
                        last = jnp.where(slot == 5, own, jnp.where(slot == 4, line[1], line[2]))
                    value = jnp.where(where & end, last, value)
                edge_ref[len(REACH) * q + n, at, :] = value
        for f in range(5):
            edge_ref[LINES + 3 + f, at, :] = windows[6 + f]


def mend_edges(cols, near_ref, inner_ref, far_ref, edge_ref, one_ref, two_ref, out_ref, held, sems):
    nx = edge_ref.shape[1]
    ny = SUB
    odd = lax.rem(lax.axis_index("col"), 2) == 1
    lane = lanes()
    slot = slots()
    at_edge = (lane < HALO) | (lane >= LANES - HALO)
    edge_new = []
    for base in range(0, nx, SUB):
        at = pl.ds(base, SUB)
        one, two = one_ref[at, :], two_ref[at, :]
        lower, upper = jnp.where(odd, one, two), jnp.where(odd, two, one)

        def joined(index, k, lane_by):
            own = edge_ref[index, at, :]
            if not k:
                return own
            where, end = beyond(slot, k, cols)
            got = turned(lower if k < 0 else upper, lane_by)
            return jnp.where(where & jnp.logical_not(end), got, own)

        lines = [
            {k: joined(len(REACH) * q + n, k, 3 * q + k - 3) for n, k in enumerate(REACH)}
            for q in range(5)
        ]
        gammas = {-1: joined(LINES, -1, 9), 0: joined(LINES + 1, 0, 0), 1: joined(LINES + 2, 1, 13)}
        cons = [edge_ref[LINES + 3 + f, at, :] for f in range(5)]
        edge_new.append(sweep_lines(cons, lines, gammas, 2))
    copies = []
    for f in range(5):
        for tile, new in enumerate(edge_new):
            for y in range(ny):
                edge = turned(new[f], GROUP * y + 6)
                at = pl.ds(tile * SUB * ny + own_row(y), SUB, stride=ny)
                if y < INNER:
                    rows_ref, start = near_ref, y
                elif y < SPLIT:
                    rows_ref, start = inner_ref, y - INNER
                else:
                    rows_ref, start = far_ref, y - SPLIT
                inner = rows_ref[f, pl.ds(start * nx + tile * SUB, SUB), :]
                held[f, at, :] = jnp.where(at_edge, edge, inner)
        copy = pltpu.make_async_copy(held.at[f], out_ref.at[f], sems.at[f])
        copy.start(priority=f % 2)
        copies.append(copy)
    for copy in copies:
        copy.wait()


def at_end(cols):
    col = lax.axis_index("col")
    return (col == 0) | (col == cols - 1)


def end_kernel(cols, near_ref, inner_ref, far_ref, edge_ref, one_ref, out_ref, held, sems):
    @pl.when(at_end(cols))
    def _():
        mend_edges(
            cols, near_ref, inner_ref, far_ref, edge_ref, one_ref, one_ref, out_ref, held, sems
        )


def middle_kernel(
    cols, ends_ref, near_ref, inner_ref, far_ref, edge_ref, one_ref, two_ref, out_ref, held, sems
):
    @pl.when(jnp.logical_not(at_end(cols)))
    def _():
        mend_edges(
            cols, near_ref, inner_ref, far_ref, edge_ref, one_ref, two_ref, out_ref, held, sems
        )


def swap_pairs(mesh, axis, inner):
    rows, cols = mesh.shape["row"], mesh.shape["col"]
    pairs = []
    for r in range(rows):
        for c in range(cols):
            k, n = (r, rows) if axis == "row" else (c, cols)
            if not inner:
                k ^= 1
            elif 0 < k < n - 1:
                k = ((k - 1) ^ 1) + 1
            else:
                k = None
            if axis == "row":
                to = (r, c ^ 1) if k is None else (k, c)
            else:
                to = (r, cols - 1 - c) if k is None else (r, k)
            pairs.append((r * cols + c, to[0] * cols + to[1]))
    return pairs


def body(mesh, state, gamma):
    rows, cols = mesh.shape["row"], mesh.shape["col"]
    _, nx, ny, nz = state.shape
    assert ny == SUB and nz == LANES and nx % SUB == 0 and rows % 2 == 0 and cols % 2 == 0
    here = lambda *dims: pltpu.VMEM(dims, jnp.float32)
    keep = lambda x: pltpu.with_memory_space_constraint(x, pltpu.VMEM)
    near = pl.BlockSpec(memory_space=pltpu.VMEM)
    swap = lambda x, axis, inner: lax.ppermute(x, ("row", "col"), swap_pairs(mesh, axis, inner))

    two = pl.pallas_call(
        raw_kernel,
        out_shape=here(6, HALO, nx, nz),
        in_specs=[pl.BlockSpec(memory_space=pltpu.HBM)] * 2,
        out_specs=near,
        scratch_shapes=[pltpu.SemaphoreType.DMA((HALO, 2))],
        name="raw_edges",
    )(state, gamma)
    two = swap(two, "row", True).reshape(6 * HALO, nx, nz)
    held = (keep(state.reshape(5, nx * ny, nz)), keep(gamma.reshape(nx * ny, nz)))
    one, rim = pl.pallas_call(
        edge_rows_kernel,
        out_shape=(here(5 * HALO + 1, nx, nz), here(2 * nx, nz)),
        in_specs=[near] * 2,
        out_specs=(near,) * 2,
        name="edge_rows",
    )(*held)
    swept = pl.pallas_call(
        first_kernel,
        out_shape=here(6, ny * nx, nz),
        in_specs=[near] * 2,
        out_specs=near,
        name="sweep_first",
    )(*held)
    rim = swap(rim, "row", False)
    one = swap(one, "row", False)
    inner_rows, lower, upper, kept_near, kept = pl.pallas_call(
        inner_kernel,
        out_shape=(
            here(5, (SPLIT - INNER) * nx, nz),
            here(nx, nz),
            here(nx, nz),
            here(KEPT_NEAR, nx, nz),
            here(KEPT_FAR, nx, nz),
        ),
        in_specs=[near],
        out_specs=(near,) * 5,
        name="second_inner",
    )(keep(swept))

    def third(first, count, rows_in, name):
        return pl.pallas_call(
            functools.partial(third_kernel, first, count),
            out_shape=here(5, count * nx, nz),
            in_specs=[near] * 2,
            out_specs=near,
            name=name,
        )(keep(rows_in), keep(swept))

    inner_z = third(INNER, SPLIT - INNER, inner_rows, "third_inner")
    near_rows, lower, upper = pl.pallas_call(
        functools.partial(second_near, rows),
        out_shape=(here(5, SPLIT * nx, nz), here(nx, nz), here(nx, nz)),
        in_specs=[near] * 7,
        out_specs=(near,) * 3,
        name="second_near",
    )(
        keep(swept),
        keep(two),
        keep(inner_rows),
        keep(lower),
        keep(upper),
        keep(kept_near),
        keep(inner_z),
    )
    far_shape = here(5, (ny - SPLIT) * nx, nz)
    rim_rows, to_one, to_two = pl.pallas_call(
        rim_kernel,
        out_shape=(far_shape, here(nx, nz), here(2 * nx, nz)),
        in_specs=[near] * 5,
        out_specs=(near,) * 3,
        cost_estimate=pl.CostEstimate(flops=10**9, bytes_accessed=0, transcendentals=0),
        name="second_rim",
    )(keep(swept), keep(rim), keep(lower), keep(upper), keep(kept))
    two = swap(to_two, "col", True)
    col_one = swap(to_one, "col", False)
    inner_near = third(0, INNER, near_rows, "third_near")
    edge = pl.pallas_call(
        functools.partial(window_kernel, cols),
        out_shape=here(EDGE_ARRAYS, nx, nz),
        in_specs=[near] * 3,
        out_specs=near,
        name="third_windows",
    )(keep(near_rows), keep(rim_rows), keep(swept))
    far_rows = pl.pallas_call(
        second_far,
        out_shape=far_shape,
        in_specs=[near] * 5,
        out_specs=near,
        name="second_far",
    )(keep(swept), keep(one), keep(kept), keep(inner_near), keep(edge))
    inner = (keep(inner_near), keep(inner_z), keep(far_rows))
    far = pl.BlockSpec(memory_space=pltpu.HBM)
    whole = jax.ShapeDtypeStruct((5, nx * ny, nz), jnp.float32)
    scratch = [pltpu.VMEM(whole.shape, jnp.float32), pltpu.SemaphoreType.DMA((5,))]
    ends = pl.pallas_call(
        functools.partial(end_kernel, cols),
        out_shape=whole,
        in_specs=[near] * 5,
        out_specs=far,
        scratch_shapes=scratch,
        name="third_ends",
    )(*inner, keep(edge), keep(col_one))
    out = pl.pallas_call(
        functools.partial(middle_kernel, cols),
        out_shape=whole,
        in_specs=[far] + [near] * 6,
        out_specs=far,
        input_output_aliases={0: 0},
        scratch_shapes=scratch,
        name="third_middle",
    )(ends, *inner, keep(edge), keep(col_one), keep(two))
    return out.reshape(5, nx, ny, nz)


def solution(mesh):
    in_specs = (P(None, None, "row", "col"), P(None, "row", "col"))
    out_specs = P(None, None, "row", "col")
    return jax.shard_map(
        functools.partial(body, mesh),
        mesh=mesh,
        in_specs=in_specs,
        out_specs=out_specs,
        check_vma=False,
    )
```
